256 devices in a mesh: gx: 32 (over y, x, core), gy: 8 (over z).
Axes of the slice: x: 4, y: 4, z: 8, core: 2. Of those that a mesh axis runs over, the one named last changes fastest.
Arguments:
- velocity: float32 [3, 256, 256, 256], P(None, 'gx', 'gy'), may hold values from -6 to 6
- forcing: float32 [3, 256, 256, 256], P(None, 'gx', 'gy'), may hold values from -6 to 6
- viscosity: float32 [256, 256, 256], P('gx', 'gy'), may hold values from 0.1 to 10
Outputs:
- updated: float32 [3, 256, 256, 256], P(None, 'gx', 'gy')
The draws below stay inside these ranges and needn't reach their ends.
All inputs are finite; a program needn't handle non-finite values.
Results may differ from the reference program's by a relative error of at most 0.000064.
Values sent between devices are 32-bit elements; how exact they have to be, the bound alone decides.
No kernel may reach another device: no remote copies, remote signals or barrier semaphores. Data moves between devices by JAX's collectives and lax.ppermute only.
A program may use at most 64 MiB of HBM per device.

```python
import math
import jax
import jax.numpy as jnp

CX = 8
NZ = 256
KC = 4
NX = 256
NY = 256
N_GX = 32


def block_levels(own_key, shape, pieces, smallest, top_value):
    def one(axis_at, shards_of):
        draws = jax.random.uniform(jax.random.fold_in(jax.random.fold_in(own_key, 6), axis_at), (shards_of,), jnp.float32, smallest / len(pieces), top_value / len(pieces))
        return jnp.repeat(jnp.exp(draws), shape[axis_at] // shards_of).reshape((-1,) + (1,) * (len(shape) - axis_at - 1))

    factor_of = one(*pieces[0])
    for cut in pieces[1:]:
        factor_of = factor_of * one(*cut)
    return factor_of


def scatter_about(rng, dims, deviation, limit, split=(), held_as=jnp.bfloat16):
    level = block_levels(rng, dims, split, -0.22, 0.18) if split else 1.0
    values = jax.random.normal(rng, dims, jnp.float32) * deviation * level
    return jnp.minimum(jnp.maximum(values, -limit), limit).astype(held_as)


def setup_inputs(seed: int = 0) -> dict:
    key_list = jax.random.split(jax.random.key(seed), 4)
    velocity = scatter_about(key_list[0], (3, NX, NY, NZ), 1.0, 6.0, ((1, 32), (2, 8)), jnp.float32)
    forcing = scatter_about(key_list[1], (3, NX, NY, NZ), 1.0, 6.0, ((1, 32), (2, 8)), jnp.float32)
    viscosity = jnp.clip(jnp.exp(math.log(10.0) - 4.6051702 * jax.random.uniform(key_list[2], (NX, NY, NZ), jnp.float32) ** block_levels(key_list[2], (NX, NY, NZ), ((0, 32), (1, 8)), -0.2, 0.2)), 0.1, 10.0)
    return {"velocity": velocity, "forcing": forcing, "viscosity": viscosity}


def neighbours(padded):
    size_x = padded.shape[-3] - 2
    size_y = padded.shape[-2] - 2
    size_z = padded.shape[-1] - 2
    summed = None
    for step_x in (-1, 0, 1):
        for step_y in (-1, 0, 1):
            for step_z in (-1, 0, 1):
                distance = abs(step_x) + abs(step_y) + abs(step_z)
                if distance == 0:
                    continue
                factor = 0.5 ** (distance - 1)
                shifted = padded[..., 1 + step_x:1 + step_x + size_x, 1 + step_y:1 + step_y + size_y, 1 + step_z:1 + step_z + size_z]
                summed = factor * shifted if summed is None else summed + factor * shifted
    return summed


def apply_operator(field, padded, visc_field):
    return visc_field * (14.5 * field - neighbours(padded))


def smooth_once(field, padded, rhs_field, visc_field):
    return field + 0.8 * (rhs_field - apply_operator(field, padded, visc_field)) / (14.5 * visc_field)


def pad_all(field):
    return jnp.pad(field, [(0, 0)] * (field.ndim - 3) + [(1, 1)] * 3)


def restrict_sum(fine):
    lead, size_x, size_y, size_z = fine.shape
    return fine.reshape(lead, size_x // 2, 2, size_y // 2, 2, size_z // 2, 2).sum(axis=(2, 4, 6))


def reference(velocity, forcing, viscosity):
    field = velocity
    for sweep_count in range(2):
        field = smooth_once(field, pad_all(field), forcing, viscosity)
    residual_field = forcing - apply_operator(field, pad_all(field), viscosity)
    coarse_rhs = 0.5 * restrict_sum(residual_field)
    coarse_visc = 0.125 * restrict_sum(viscosity[None])[0]
    groups = N_GX // 2
    rhs_groups = coarse_rhs.reshape(3, groups, CX, NY // 2, NZ // 2)
    visc_groups = coarse_visc.reshape(groups, CX, NY // 2, NZ // 2)
    correction = jnp.zeros_like(rhs_groups)
    for sweep_count in range(KC):
        correction = smooth_once(correction, pad_all(correction), rhs_groups, visc_groups)
    correction = correction.reshape(3, NX // 2, NY // 2, NZ // 2)
    lifted = jnp.repeat(jnp.repeat(jnp.repeat(correction, 2, axis=1), 2, axis=2), 2, axis=3)
    field = field + lifted
    return smooth_once(field, pad_all(field), forcing, viscosity)
```

```python
import jax
import jax.numpy as jnp
from jax import lax
from jax.experimental import pallas as pl
from jax.experimental.pallas import tpu as pltpu
from jax.sharding import PartitionSpec as P

KC = 4
CA = 1.0 - 0.8 * 16.5 / 14.5
CB = 1.6 / 14.5
CG = 0.8 / 14.5

ROWS = 8
COLS = 32
DEPTH = 256
WIDE = 48
LEFT = 8
CROWS = 4
CCOLS = 16
CWIDE = 24
CLEFT = 4
CDEPTH = 128


def places():
    index_x = lax.axis_index("gx")
    index_y = lax.axis_index("gy")
    core = index_x % 2
    has_off = jnp.logical_and(index_x != 0, index_x != lax.axis_size("gx") - 1)
    even_y = index_y % 2 == 0
    return core, has_off, even_y, index_y != 0, index_y != lax.axis_size("gy") - 1


def row_of(core, row, rows=ROWS):
    return row + core * (rows - 1 - 2 * row)


def sums_yz(a):
    rows, depth = a.shape
    a = a + 0.5 * (pltpu.roll(a, 1, 0) + pltpu.roll(a, rows - 1, 0))
    lane = lax.broadcasted_iota(jnp.int32, a.shape, 1)
    low = jnp.where(lane == 0, 0.0, pltpu.roll(a, 1, 1))
    high = jnp.where(lane == depth - 1, 0.0, pltpu.roll(a, depth - 1, 1))
    return a + 0.5 * (low + high)


def sums_x(get, row, first, last):
    near = [get(r) for r in (row - 1, row + 1) if first <= r <= last]
    total = None
    if near:
        total = 0.5 * (near[0] if len(near) == 1 else near[0] + near[1])
    if first <= row <= last:
        total = get(row) if total is None else get(row) + total
    return total


def widened(a):
    side = jnp.zeros((LEFT, a.shape[1]), a.dtype)
    return jnp.concatenate([side, a, side], 0)


def column_mask(shape, left, width, has_low, has_high):
    place = lax.broadcasted_iota(jnp.int32, shape, 0)
    keep = jnp.logical_and(
        jnp.logical_or(place >= left, has_low), jnp.logical_or(place < left + width, has_high)
    )
    return jnp.where(keep, 1.0, 0.0)


def pair_table(size):
    fine = lax.broadcasted_iota(jnp.int32, (size, size // 2), 0) // 2
    coarse = lax.broadcasted_iota(jnp.int32, (size, size // 2), 1)
    return jnp.where(fine == coarse, 1.0, 0.0)


def pair_table_t(size):
    coarse = lax.broadcasted_iota(jnp.int32, (size // 2, size), 0)
    fine = lax.broadcasted_iota(jnp.int32, (size // 2, size), 1) // 2
    return jnp.where(fine == coarse, 1.0, 0.0)


def exact_dot(a, b):
    return jnp.dot(a, b, precision=lax.Precision.HIGHEST, preferred_element_type=jnp.float32)


def halves(ref, value):
    for h in range(2):
        ref[h] = value[:, CDEPTH * h : CDEPTH * (h + 1)]


def paired_columns(ref, value):
    halves(ref, value)
    return jnp.concatenate(
        [
            ref[h, pl.ds(0, CCOLS, stride=2)] + ref[h, pl.ds(1, CCOLS, stride=2)]
            for h in range(2)
        ],
        1,
    )


def doubled_columns(ref, value):
    for h in range(2):
        part = value[:, CDEPTH * h : CDEPTH * (h + 1)]
        ref[h, pl.ds(0, CWIDE, stride=2)] = part
        ref[h, pl.ds(1, CWIDE, stride=2)] = part
    return jnp.concatenate([ref[0], ref[1]], 1)


def sweeps_kernel(v_ref, f_ref, e_ref, out_ref, edge_ref, za_ref, zb_ref, u_ref, w_ref):
    core, has_off, even_y, has_low, has_high = places()
    mask = column_mask((WIDE, DEPTH), LEFT, COLS, has_low, has_high)
    mask_off = mask * jnp.where(has_off, 1.0, 0.0)

    def one(k, carry):
        for r in range(ROWS):
            u_ref[r] = sums_yz(widened(v_ref[k, row_of(core, r)]))
        for r in range(-1, ROWS + 1):
            value = CB * sums_x(lambda i: u_ref[i], r, 0, ROWS - 1)
            if 0 <= r < ROWS:
                own = row_of(core, r)
                value = value + widened(CA * v_ref[k, own] + CG * f_ref[k, own] / e_ref[own])
            w_ref[r + 1] = value * (mask if r >= 0 else mask_off)
        for r in range(ROWS + 2):
            u_ref[r] = sums_yz(w_ref[r])
        for r in range(-2, ROWS + 2):
            value = CB * sums_x(lambda i: u_ref[i + 1], r, -1, ROWS)
            if -1 <= r <= ROWS:
                value = value + CA * w_ref[r + 1]
            if 0 <= r < ROWS:
                own = row_of(core, r)
                value = value + widened(CG * f_ref[k, own] / e_ref[own])
            value = value * (mask if r >= 0 else mask_off)
            out_ref[k, r + 2] = value
            if r < 1:
                edge_ref[k, r + 2] = value
            if r >= ROWS - 1:
                edge_ref[k, r + 2 - ROWS + 2] = value
            at = 3 * (r + 2)
            low = value[LEFT - 2 : LEFT + 1]
            high = value[LEFT + COLS - 1 : LEFT + COLS + 2]
            za_ref[k, at : at + 3] = jnp.where(even_y, high, low)
            zb_ref[k, at : at + 3] = jnp.where(even_y, low, high)
        return carry

    lax.fori_loop(0, 3, one, 0)


def from_sides(even_y, a, b):
    return jnp.where(even_y, b, a), jnp.where(even_y, a, b)


def merge_kernel(edge_ref, za_ref, zb_ref, off_ref, on_ref, row_ref):
    _, _, even_y, _, _ = places()

    def one(k, carry):
        for j, r in enumerate((-2, -1, 0, ROWS - 1, ROWS, ROWS + 1)):
            at = 3 * (r + 2)
            low, high = from_sides(even_y, za_ref[k, at : at + 3], zb_ref[k, at : at + 3])
            row_ref[...] = edge_ref[k, j]
            row_ref[LEFT - 1 : LEFT + 2] = row_ref[LEFT - 1 : LEFT + 2] + low
            row_ref[LEFT + COLS - 2 : LEFT + COLS + 1] = (
                row_ref[LEFT + COLS - 2 : LEFT + COLS + 1] + high
            )
            ref, slot = (off_ref, 2 - j) if j < 3 else (on_ref, j - 3)
            ref[k, COLS * slot : COLS * (slot + 1)] = row_ref[LEFT : LEFT + COLS]
            base = 3 * COLS + 2 * slot
            ref[k, base : base + 1] = row_ref[LEFT - 1 : LEFT]
            ref[k, base + 1 : base + 2] = row_ref[LEFT + COLS : LEFT + COLS + 1]
        return carry

    lax.fori_loop(0, 3, one, 0)


def residual_kernel(
    own_ref, za_ref, zb_ref, off_ref, on_ref, f_ref, e_ref,
    s_ref, gc_ref, ca_ref, cb_ref, u_ref, r_ref, g_ref,
):
    core, _, even_y, _, _ = places()
    table = pair_table(DEPTH)
    for j in range(CROWS):
        g_ref[CCOLS * (3 * CROWS + j) : CCOLS * (3 * CROWS + j + 1)] = paired_columns(
            r_ref, e_ref[row_of(core, 2 * j)] + e_ref[row_of(core, 2 * j + 1)]
        )

    def one(k, carry):
        for r in range(-1, ROWS + 1):
            at = 3 * (r + 2)
            low, high = from_sides(even_y, za_ref[k, at : at + 3], zb_ref[k, at : at + 3])
            s_ref[k, r + 1] = own_ref[k, r + 2]
            s_ref[k, r + 1, LEFT - 1 : LEFT + 2] = s_ref[k, r + 1, LEFT - 1 : LEFT + 2] + low
            s_ref[k, r + 1, LEFT + COLS - 2 : LEFT + COLS + 1] = (
                s_ref[k, r + 1, LEFT + COLS - 2 : LEFT + COLS + 1] + high
            )
            for ref, slot in ((off_ref, r + 1), (on_ref, ROWS - r)):
                if 0 <= slot < 3:
                    base = 3 * COLS + 2 * slot
                    s_ref[k, r + 1, LEFT : LEFT + COLS] = (
                        s_ref[k, r + 1, LEFT : LEFT + COLS]
                        + ref[k, COLS * slot : COLS * (slot + 1)]
                    )
                    s_ref[k, r + 1, LEFT - 1 : LEFT] = (
                        s_ref[k, r + 1, LEFT - 1 : LEFT] + ref[k, base : base + 1]
                    )
                    s_ref[k, r + 1, LEFT + COLS : LEFT + COLS + 1] = (
                        s_ref[k, r + 1, LEFT + COLS : LEFT + COLS + 1] + ref[k, base + 1 : base + 2]
                    )
            u_ref[r + 1] = sums_yz(s_ref[k, r + 1])[LEFT : LEFT + COLS]
        for j in range(CROWS):
            total = None
            for r in (2 * j, 2 * j + 1):
                own = row_of(core, r)
                near = sums_x(lambda i: u_ref[i + 1], r, -1, ROWS)
                value = f_ref[k, own] - e_ref[own] * (
                    16.5 * s_ref[k, r + 1, LEFT : LEFT + COLS] - 2.0 * near
                )
                total = value if total is None else total + value
            at = pl.multiple_of(k * (CROWS * CCOLS) + j * CCOLS, CCOLS)
            g_ref[pl.ds(at, CCOLS)] = paired_columns(r_ref, total)
        return carry

    lax.fori_loop(0, 3, one, 0)
    sums = exact_dot(g_ref[...], table)
    size = CROWS * CCOLS
    inverse = (4.0 * CG) / sums[3 * size :]
    for k in range(3):
        value = sums[k * size : (k + 1) * size] * inverse
        for j in range(CROWS):
            row = value[j * CCOLS : (j + 1) * CCOLS]
            gc_ref[k, j] = row
            low = row[:4]
            high = row[CCOLS - 4 :]
            ca_ref[k, 4 * j : 4 * j + 4] = jnp.where(even_y, high, low)
            cb_ref[k, 4 * j : 4 * j + 4] = jnp.where(even_y, low, high)


def coarse_wide_kernel(gc_ref, ca_ref, cb_ref, out_ref):
    _, _, even_y, _, _ = places()
    for k in range(3):
        for j in range(CROWS):
            low, high = from_sides(even_y, ca_ref[k, 4 * j : 4 * j + 4], cb_ref[k, 4 * j : 4 * j + 4])
            out_ref[k, j] = jnp.concatenate([low, gc_ref[k, j], high], 0)


def coarse_kernel(own_ref, partner_ref, cor_ref, edge_ref, c_ref, u_ref):
    _, _, _, has_low, has_high = places()
    mask = column_mask((CWIDE, CDEPTH), CLEFT, CCOLS, has_low, has_high)
    total = 2 * CROWS

    def rhs(k, r):
        return own_ref[k, r] if r < CROWS else partner_ref[k, total - 1 - r]

    def one(k, carry):
        for r in range(total):
            c_ref[r] = rhs(k, r)
        for _ in range(KC - 1):
            for r in range(total):
                u_ref[r] = sums_yz(c_ref[r])
            for r in range(total):
                c_ref[r] = mask * (
                    CA * c_ref[r] + CB * sums_x(lambda i: u_ref[i], r, 0, total - 1) + rhs(k, r)
                )
        for r in range(CROWS + 1):
            cor_ref[k, r] = c_ref[r]
        edge_ref[k] = c_ref[0]
        return carry

    lax.fori_loop(0, 3, one, 0)


def final_kernel(s_ref, cor_ref, edge_ref, f_ref, e_ref, out_ref, l_ref, u_ref):
    core, _, _, _, _ = places()
    table = pair_table_t(DEPTH)

    def one(k, carry):
        rows = [edge_ref[k]] + [cor_ref[k, j] for j in range(CROWS + 1)]
        lifted = exact_dot(jnp.concatenate(rows, 0), table)
        for j in range(CROWS + 2):
            part = lifted[j * CWIDE : (j + 1) * CWIDE]
            part = doubled_columns(l_ref, part)
            for r in (2 * j - 2, 2 * j - 1):
                if -1 <= r <= ROWS:
                    value = s_ref[k, r + 1] + part
                    u_ref[r + 1] = sums_yz(value)[LEFT : LEFT + COLS]
                    if 0 <= r < ROWS:
                        own = row_of(core, r)
                        out_ref[k, own] = (
                            CA * value[LEFT : LEFT + COLS] + CG * f_ref[k, own] / e_ref[own]
                        )
        for r in range(ROWS):
            own = row_of(core, r)
            out_ref[k, own] = out_ref[k, own] + CB * sums_x(lambda i: u_ref[i + 1], r, -1, ROWS)
        return carry

    lax.fori_loop(0, 3, one, 0)


def call(kernel, outs, scratch, *args):
    return pl.pallas_call(
        kernel,
        out_shape=[jax.ShapeDtypeStruct(o, jnp.float32) for o in outs],
        in_specs=[pl.BlockSpec(memory_space=pltpu.VMEM)] * len(args),
        out_specs=[pl.BlockSpec(memory_space=pltpu.VMEM)] * len(outs),
        scratch_shapes=[pltpu.VMEM(s, jnp.float32) for s in scratch],
        compiler_params=pltpu.CompilerParams(vmem_limit_bytes=24 * 2**20),
    )(*args)


def swap(value, axis, parity):
    pairs = []
    for i in range(parity, lax.axis_size(axis) - 1, 2):
        pairs += [(i, i + 1), (i + 1, i)]
    return lax.ppermute(value, axis, pairs)


def body(velocity, forcing, viscosity):
    wide = (3, ROWS + 4, WIDE, DEPTH)
    zmsg = (3, 40, DEPTH)
    xmsg = (3, 104, DEPTH)
    own, edge, za, zb = call(
        sweeps_kernel,
        [wide, (3, 6, WIDE, DEPTH), zmsg, zmsg],
        [(ROWS + 2, WIDE, DEPTH)] * 2,
        velocity, forcing, viscosity,
    )
    zb = swap(zb, "gy", 1)
    za = swap(za, "gy", 0)
    off, on = call(merge_kernel, [xmsg, xmsg], [(WIDE, DEPTH)], edge, za, zb)
    off = swap(off, "gx", 1)
    on = swap(on, "gx", 0)
    cmsg = (3, 16, CDEPTH)
    smooth, gc, ca, cb = call(
        residual_kernel,
        [(3, ROWS + 2, WIDE, DEPTH), (3, CROWS, CCOLS, CDEPTH), cmsg, cmsg],
        [(ROWS + 2, COLS, DEPTH), (2, COLS, CDEPTH), (4 * CROWS * CCOLS, DEPTH)],
        own, za, zb, off, on, forcing, viscosity,
    )
    cb = swap(cb, "gy", 1)
    ca = swap(ca, "gy", 0)
    (gcw,) = call(coarse_wide_kernel, [(3, CROWS, CWIDE, CDEPTH)], [], gc, ca, cb)
    partner = swap(gcw, "gx", 0)
    cor, cedge = call(
        coarse_kernel,
        [(3, CROWS + 1, CWIDE, CDEPTH), (3, CWIDE, CDEPTH)],
        [(2 * CROWS, CWIDE, CDEPTH)] * 2,
        gcw, partner,
    )
    cedge = swap(cedge, "gx", 1)
    (out,) = call(
        final_kernel,
        [velocity.shape],
        [(2, WIDE, CDEPTH), (ROWS + 2, COLS, DEPTH)],
        smooth, cor, cedge, forcing, viscosity,
    )
    return out


def solution(mesh):
    placed = (P(None, "gx", "gy", None), P(None, "gx", "gy", None), P("gx", "gy", None))
    return jax.shard_map(
        body, mesh=mesh, in_specs=placed, out_specs=P(None, "gx", "gy", None), check_vma=False
    )
```

```python
import jax
import jax.numpy as jnp
from jax import lax
from jax.experimental import pallas as pl
from jax.experimental.pallas import tpu as pltpu
from jax.sharding import PartitionSpec as P

KC = 4
CA = 1.0 - 0.8 * 16.5 / 14.5
CB = 1.6 / 14.5
CG = 0.8 / 14.5

ROWS = 8
COLS = 32
DEPTH = 256
WIDE = 48
LEFT = 8
CROWS = 4
CCOLS = 16
CWIDE = 24
CLEFT = 4
CDEPTH = 128


def places():
    index_x = lax.axis_index("gx")
    index_y = lax.axis_index("gy")
    core = index_x % 2
    has_off = jnp.logical_and(index_x != 0, index_x != lax.axis_size("gx") - 1)
    even_y = index_y % 2 == 0
    return core, has_off, even_y, index_y != 0, index_y != lax.axis_size("gy") - 1


def row_of(core, row, rows=ROWS):
    return row + core * (rows - 1 - 2 * row)


def sums_yz(a):
    rows, depth = a.shape
    a = a + 0.5 * (pltpu.roll(a, 1, 0) + pltpu.roll(a, rows - 1, 0))
    lane = lax.broadcasted_iota(jnp.int32, a.shape, 1)
    low = jnp.where(lane == 0, 0.0, pltpu.roll(a, 1, 1))
    high = jnp.where(lane == depth - 1, 0.0, pltpu.roll(a, depth - 1, 1))
    return a + 0.5 * (low + high)


def sums_x(get, row, first, last):
    near = [get(r) for r in (row - 1, row + 1) if first <= r <= last]
    total = None
    if near:
        total = 0.5 * (near[0] if len(near) == 1 else near[0] + near[1])
    if first <= row <= last:
        total = get(row) if total is None else get(row) + total
    return total


def widened(a):
    side = jnp.zeros((LEFT, a.shape[1]), a.dtype)
    return jnp.concatenate([side, a, side], 0)


def column_mask(shape, left, width, has_low, has_high):
    place = lax.broadcasted_iota(jnp.int32, shape, 0)
    keep = jnp.logical_and(
        jnp.logical_or(place >= left, has_low), jnp.logical_or(place < left + width, has_high)
    )
    return jnp.where(keep, 1.0, 0.0)


def pair_table(size):
    fine = lax.broadcasted_iota(jnp.int32, (size, size // 2), 0) // 2
    coarse = lax.broadcasted_iota(jnp.int32, (size, size // 2), 1)
    return jnp.where(fine == coarse, 1.0, 0.0)


def pair_table_t(size):
    coarse = lax.broadcasted_iota(jnp.int32, (size // 2, size), 0)
    fine = lax.broadcasted_iota(jnp.int32, (size // 2, size), 1) // 2
    return jnp.where(fine == coarse, 1.0, 0.0)


def exact_dot(a, b):
    return jnp.dot(a, b, precision=lax.Precision.HIGHEST, preferred_element_type=jnp.float32)


def halves(ref, value):
    for h in range(2):
        ref[h] = value[:, CDEPTH * h : CDEPTH * (h + 1)]


def paired_columns(ref, value):
    halves(ref, value)
    return jnp.concatenate(
        [
            ref[h, pl.ds(0, CCOLS, stride=2)] + ref[h, pl.ds(1, CCOLS, stride=2)]
            for h in range(2)
        ],
        1,
    )


def doubled_columns(ref, value):
    for h in range(2):
        part = value[:, CDEPTH * h : CDEPTH * (h + 1)]
        ref[h, pl.ds(0, CWIDE, stride=2)] = part
        ref[h, pl.ds(1, CWIDE, stride=2)] = part
    return jnp.concatenate([ref[0], ref[1]], 1)


def from_sides(even_y, a, b):
    return jnp.where(even_y, b, a), jnp.where(even_y, a, b)


XMSG = (3, 112, DEPTH)
ZMSG = (4, 32, DEPTH)
CMSG = (3, 56, CDEPTH)


def sweeps_kernel(
    v_hbm, f_hbm, e_hbm, own_ref, g_ref, off_ref, on_ref, za_ref, zb_ref,
    v_ref, f_ref, e_ref, u_ref, w_ref, sems,
):
    def copy_v(k):
        return pltpu.make_async_copy(v_hbm.at[k], v_ref.at[k], sems.at[k])

    def copy_f(k):
        return pltpu.make_async_copy(f_hbm.at[k], f_ref.at[k], sems.at[3 + k])

    copy_e = pltpu.make_async_copy(e_hbm, e_ref, sems.at[6])
    copy_e.start()
    for k in range(3):
        copy_v(k).start()
        copy_f(k).start()
    core, has_off, even_y, has_low, has_high = places()
    mask = column_mask((WIDE, DEPTH), LEFT, COLS, has_low, has_high)
    mask_off = mask * jnp.where(has_off, 1.0, 0.0)
    copy_e.wait()
    for r in range(ROWS):
        value = e_ref[row_of(core, r)]
        low = value[:4]
        high = value[COLS - 4 :]
        za_ref[3, 4 * r : 4 * r + 4] = jnp.where(even_y, high, low)
        zb_ref[3, 4 * r : 4 * r + 4] = jnp.where(even_y, low, high)

    def one(k, carry):
        copy_v(k).wait()
        for r in range(ROWS):
            u_ref[r] = sums_yz(widened(v_ref[k, row_of(core, r)]))
        copy_f(k).wait()
        for r in range(ROWS):
            own = row_of(core, r)
            g_ref[k, r] = CG * f_ref[k, own] / e_ref[own]
        for r in range(-1, ROWS + 1):
            value = CB * sums_x(lambda i: u_ref[i], r, 0, ROWS - 1)
            if 0 <= r < ROWS:
                own = row_of(core, r)
                value = value + widened(CA * v_ref[k, own] + g_ref[k, r])
            w_ref[r + 1] = value * (mask if r >= 0 else mask_off)
        for r in range(ROWS + 2):
            u_ref[r] = sums_yz(w_ref[r])
        for r in range(-2, ROWS + 2):
            value = CB * sums_x(lambda i: u_ref[i + 1], r, -1, ROWS)
            if -1 <= r <= ROWS:
                value = value + CA * w_ref[r + 1]
            if 0 <= r < ROWS:
                value = value + widened(g_ref[k, r])
            value = value * (mask if r >= 0 else mask_off)
            for ref, slot in ((off_ref, -r), (on_ref, r - ROWS + 1)):
                if 0 <= slot < 3:
                    ref[k, COLS * slot : COLS * (slot + 1)] = value[LEFT : LEFT + COLS]
                    at = 3 * COLS + 4 * slot
                    ref[k, at : at + 2] = value[LEFT - 2 : LEFT]
                    ref[k, at + 2 : at + 4] = value[LEFT + COLS : LEFT + COLS + 2]
            if -1 <= r <= ROWS:
                own_ref[k, r + 1] = value
                at = 3 * (r + 1)
                low = value[LEFT - 2 : LEFT + 1]
                high = value[LEFT + COLS - 1 : LEFT + COLS + 2]
                za_ref[k, at : at + 3] = jnp.where(even_y, high, low)
                zb_ref[k, at : at + 3] = jnp.where(even_y, low, high)
        return carry

    lax.fori_loop(0, 3, one, 0)


def spill(ref, k, slot):
    at = 3 * COLS + 4 * slot
    low = jnp.concatenate([ref[k, at : at + 2], ref[k, COLS * slot : COLS * slot + 1]], 0)
    high = jnp.concatenate(
        [ref[k, COLS * (slot + 1) - 1 : COLS * (slot + 1)], ref[k, at + 2 : at + 4]], 0
    )
    return low, high


def residual_kernel(
    own_ref, on_ref, zb_ref, za_ref, off_ref, g_ref, e_ref,
    s_ref, gc_ref, ca_ref, cb_ref, u_ref, r_ref, q_ref,
):
    core, _, even_y, _, _ = places()
    table = pair_table(DEPTH)
    for j in range(CROWS):
        q_ref[CCOLS * (3 * CROWS + j) : CCOLS * (3 * CROWS + j + 1)] = paired_columns(
            r_ref, e_ref[row_of(core, 2 * j)] + e_ref[row_of(core, 2 * j + 1)]
        )

    def one(k, carry):
        for side, ref in enumerate((off_ref, on_ref)):
            for slot in range(3):
                low, high = spill(ref, k, slot)
                for out, piece in (
                    (ca_ref, jnp.where(even_y, high, low)),
                    (cb_ref, jnp.where(even_y, low, high)),
                ):
                    for h in range(2):
                        at = 16 + 18 * h + 9 * side + 3 * slot
                        out[k, at : at + 3] = piece[:, CDEPTH * h : CDEPTH * (h + 1)]
        for r in range(-1, ROWS + 1):
            at = 3 * (r + 1)
            low, high = from_sides(even_y, za_ref[k, at : at + 3], zb_ref[k, at : at + 3])
            s_ref[k, r + 1] = own_ref[k, r + 1]
            s_ref[k, r + 1, LEFT - 1 : LEFT + 2] = s_ref[k, r + 1, LEFT - 1 : LEFT + 2] + low
            s_ref[k, r + 1, LEFT + COLS - 2 : LEFT + COLS + 1] = (
                s_ref[k, r + 1, LEFT + COLS - 2 : LEFT + COLS + 1] + high
            )
            for ref, slot in ((off_ref, r + 1), (on_ref, ROWS - r)):
                if 0 <= slot < 3:
                    base = 3 * COLS + 4 * slot
                    s_ref[k, r + 1, LEFT : LEFT + COLS] = (
                        s_ref[k, r + 1, LEFT : LEFT + COLS]
                        + ref[k, COLS * slot : COLS * (slot + 1)]
                    )
                    s_ref[k, r + 1, LEFT - 1 : LEFT] = (
                        s_ref[k, r + 1, LEFT - 1 : LEFT] + ref[k, base + 1 : base + 2]
                    )
                    s_ref[k, r + 1, LEFT + COLS : LEFT + COLS + 1] = (
                        s_ref[k, r + 1, LEFT + COLS : LEFT + COLS + 1] + ref[k, base + 2 : base + 3]
                    )
            u_ref[r + 1] = sums_yz(s_ref[k, r + 1])[LEFT : LEFT + COLS]
        for j in range(CROWS):
            total = None
            for r in (2 * j, 2 * j + 1):
                own = row_of(core, r)
                near = sums_x(lambda i: u_ref[i + 1], r, -1, ROWS)
                value = e_ref[own] * (
                    g_ref[k, r]
                    - (16.5 * CG) * s_ref[k, r + 1, LEFT : LEFT + COLS]
                    + (2.0 * CG) * near
                )
                total = value if total is None else total + value
            at = pl.multiple_of(k * (CROWS * CCOLS) + j * CCOLS, CCOLS)
            q_ref[pl.ds(at, CCOLS)] = paired_columns(r_ref, total)
        return carry

    lax.fori_loop(0, 3, one, 0)
    sums = exact_dot(q_ref[...], table)
    size = CROWS * CCOLS
    inverse = 4.0 / sums[3 * size :]
    for k in range(3):
        value = sums[k * size : (k + 1) * size] * inverse
        for j in range(CROWS):
            row = value[j * CCOLS : (j + 1) * CCOLS]
            gc_ref[k, j] = row
            low = row[:4]
            high = row[CCOLS - 4 :]
            ca_ref[k, 4 * j : 4 * j + 4] = jnp.where(even_y, high, low)
            cb_ref[k, 4 * j : 4 * j + 4] = jnp.where(even_y, low, high)


def corner_rows(ref, k, side, slot):
    at = 16 + 9 * side + 3 * slot
    return jnp.concatenate([ref[k, at : at + 3], ref[k, at + 18 : at + 21]], 1)


def corner_kernel(
    gc_ref, cb_ref, ca_ref, off_ref, on_ref, zb_ref, za_ref, e_ref, out_ref, d_ref, u_ref, w_ref, r_ref, q_ref
):
    core, _, even_y, _, _ = places()
    place = lax.broadcasted_iota(jnp.int32, (8, DEPTH), 0)
    d_ref[...] = jnp.zeros_like(d_ref)
    own_part = (place >= 4, place < 4)
    own_at = (4, 0)
    own_from = (0, COLS - 4)
    mine_at = (3, 2)
    theirs_at = (2, 3)

    def at_of(k, side, window, half):
        return 8 * (((k * 2 + side) * 2 + window) * 2 + half)

    def spilled_at(k, side, window, field, slot):
        return 8 * ((((k * 2 + side) * 2 + window) * 2 + field) * 3 + slot)

    for k in range(3):
        for side, ref in enumerate((off_ref, on_ref)):
            for slot in range(3):
                mine = from_sides(
                    even_y, corner_rows(ca_ref, k, side, slot), corner_rows(cb_ref, k, side, slot)
                )
                theirs = spill(ref, k, slot)
                for window in range(2):
                    at = spilled_at(k, side, window, 0, slot) + mine_at[window]
                    d_ref[at : at + 3] = mine[window]
                    at = spilled_at(k, side, window, 1, slot) + theirs_at[window]
                    d_ref[at : at + 3] = theirs[window]
    for side in range(2):
        for q in range(4):
            r = q if side == 0 else ROWS - 1 - q
            own = e_ref[row_of(core, r)]
            halo = from_sides(even_y, za_ref[3, 4 * r : 4 * r + 4], zb_ref[3, 4 * r : 4 * r + 4])
            for window in range(2):
                n = (side * 2 + window) * 4 + q
                w_ref[n, own_at[window] : own_at[window] + 4] = own[
                    own_from[window] : own_from[window] + 4
                ]
                w_ref[n, 4 - own_at[window] : 8 - own_at[window]] = halo[window]
                if q % 2:
                    at = at_of(3, side, window, q // 2)
                    r_ref[at : at + 8] = w_ref[n - 1] + w_ref[n]
    u_ref[...] = sums_yz(d_ref[...])
    for k in range(3):
        for side in range(2):
            for window in range(2):
                rows = []
                for q in range(3):
                    parts = []
                    for o in range(2):
                        at = spilled_at(k, side, window, o, 0)
                        part = -2.0 * sums_x(
                            lambda i: u_ref[at + 8 * (i + 1) : at + 8 * (i + 2)], q, -1, 1
                        )
                        if q < 2:
                            part = part + 16.5 * d_ref[at + 8 * (q + 1) : at + 8 * (q + 2)]
                        parts.append(part)
                    n = (side * 2 + window) * 4 + q
                    rows.append(-w_ref[n] * jnp.where(own_part[window], parts[0], parts[1]))
                at = at_of(k, side, window, 0)
                r_ref[at : at + 8] = rows[0] + rows[1]
                r_ref[at + 8 : at + 16] = rows[2]
    q_ref[...] = exact_dot(r_ref[...], pair_table(DEPTH))
    sums = q_ref[pl.ds(0, 128, stride=2)] + q_ref[pl.ds(1, 128, stride=2)]
    visc = sums[96:]
    inverse = jnp.where(visc > 0.0, (4.0 * CG) / jnp.where(visc > 0.0, visc, 1.0), 0.0)
    for k in range(3):
        value = sums[32 * k : 32 * (k + 1)] * inverse
        for j in range(CROWS):
            low, high = from_sides(even_y, ca_ref[k, 4 * j : 4 * j + 4], cb_ref[k, 4 * j : 4 * j + 4])
            out_ref[k, j] = jnp.concatenate([low, gc_ref[k, j], high], 0)
            side, half = (0, j) if j < 2 else (1, CROWS - 1 - j)
            for window, first in enumerate((2, CWIDE - 6)):
                at = 4 * ((side * 2 + window) * 2 + half)
                out_ref[k, j, first : first + 4] = out_ref[k, j, first : first + 4] + value[at : at + 4]


def coarse_kernel(own_ref, partner_ref, cor_ref, edge_ref, c_ref):
    _, _, _, has_low, has_high = places()
    mask = column_mask((CWIDE, CDEPTH), CLEFT, CCOLS, has_low, has_high)
    total = 2 * CROWS
    for k in range(3):
        for r in range(CROWS):
            c_ref[k, r] = own_ref[k, r]
            c_ref[k, total - 1 - r] = partner_ref[k, r]
    rhs = c_ref[...]
    value = rhs
    for left in range(KC - 1, 0, -1):
        rows = CROWS + left
        u = sums_yz(value.reshape(3 * (rows + 1) * CWIDE, CDEPTH)).reshape(3, rows + 1, CWIDE, CDEPTH)
        before = jnp.concatenate([jnp.zeros((3, 1, CWIDE, CDEPTH), jnp.float32), u[:, : rows - 1]], 1)
        near = u[:, :rows] + 0.5 * (before + u[:, 1:])
        value = mask * (CA * value[:, :rows] + CB * near + rhs[:, :rows])
    cor_ref[...] = value
    edge_ref[...] = value[:, 0]


def ring_row(s_ref, ca_ref, cb_ref, part, v_ref, even_y, k, r):
    v_ref[...] = s_ref[k, r + 1] + part
    for side, slot in ((0, r + 1), (1, ROWS - r)):
        if 0 <= slot < 3:
            low, high = from_sides(
                even_y, corner_rows(ca_ref, k, side, slot), corner_rows(cb_ref, k, side, slot)
            )
            v_ref[LEFT - 1 : LEFT + 2] = v_ref[LEFT - 1 : LEFT + 2] + low
            v_ref[LEFT + COLS - 2 : LEFT + COLS + 1] = (
                v_ref[LEFT + COLS - 2 : LEFT + COLS + 1] + high
            )
    return sums_yz(v_ref[...])[LEFT : LEFT + COLS]


def inner_kernel(
    s_ref, cb_ref, ca_ref, cor_ref, g_ref, out_hbm, first_ref, o_ref, l_ref, v_ref, u_ref, sems
):
    core, _, even_y, _, _ = places()
    table = pair_table_t(DEPTH)
    begin = 1 - core

    def copy(k):
        return pltpu.make_async_copy(
            o_ref.at[k, pl.ds(begin, ROWS - 1)], out_hbm.at[k, pl.ds(begin, ROWS - 1)], sems.at[k]
        )

    for k in range(3):
        rows = [cor_ref[k, j] for j in range(CROWS + 1)]
        lifted = exact_dot(jnp.concatenate(rows, 0), table)
        for j in range(CROWS + 1):
            part = doubled_columns(l_ref, lifted[j * CWIDE : (j + 1) * CWIDE])
            for r in (2 * j, 2 * j + 1):
                if r <= ROWS:
                    u_ref[r] = ring_row(s_ref, ca_ref, cb_ref, part, v_ref, even_y, k, r)
                    if r < ROWS:
                        own = row_of(core, r)
                        o_ref[k, own] = CA * v_ref[LEFT : LEFT + COLS] + g_ref[k, r]
        for r in range(ROWS):
            own = row_of(core, r)
            value = o_ref[k, own] + CB * sums_x(lambda i: u_ref[i], r, 0, ROWS)
            if r:
                o_ref[k, own] = value
            else:
                first_ref[k] = value
        copy(k).start()
    for k in range(3):
        copy(k).wait()


def edge_kernel(s_ref, cb_ref, ca_ref, first_ref, edge_ref, _, out_hbm, o_ref, l_ref, v_ref, sem):
    core, _, even_y, _, _ = places()
    lifted = exact_dot(jnp.concatenate([edge_ref[k] for k in range(3)], 0), pair_table_t(DEPTH))
    for k in range(3):
        part = doubled_columns(l_ref, lifted[k * CWIDE : (k + 1) * CWIDE])
        total = ring_row(s_ref, ca_ref, cb_ref, part, v_ref, even_y, k, -1)
        o_ref[k] = first_ref[k] + (0.5 * CB) * total
    copy = pltpu.make_async_copy(o_ref, out_hbm.at[:, row_of(core, 0)], sem)
    copy.start()
    copy.wait()


def call(kernel, outs, scratch, *args, spaces=None, out_spaces=None, aliases=None):
    spaces = spaces or [pltpu.VMEM] * len(args)
    out_spaces = out_spaces or [pltpu.VMEM] * len(outs)
    return pl.pallas_call(
        kernel,
        out_shape=[jax.ShapeDtypeStruct(o, jnp.float32) for o in outs],
        in_specs=[pl.BlockSpec(memory_space=space) for space in spaces],
        out_specs=[pl.BlockSpec(memory_space=space) for space in out_spaces],
        scratch_shapes=[pltpu.VMEM(s, jnp.float32) if isinstance(s, tuple) else s for s in scratch],
        input_output_aliases=aliases or {},
        compiler_params=pltpu.CompilerParams(vmem_limit_bytes=24 * 2**20),
    )(*args)


def swap(value, axis, parity):
    pairs = []
    for i in range(parity, lax.axis_size(axis) - 1, 2):
        pairs += [(i, i + 1), (i + 1, i)]
    return lax.ppermute(value, axis, pairs)


def body(velocity, forcing, viscosity):
    tall = (3, ROWS + 2, WIDE, DEPTH)
    buffers = (ROWS + 2, WIDE, DEPTH)
    own, g, off, on, za, zb = call(
        sweeps_kernel,
        [tall, velocity.shape, XMSG, XMSG, ZMSG, ZMSG],
        [velocity.shape, forcing.shape, viscosity.shape, buffers, buffers, pltpu.SemaphoreType.DMA((7,))],
        *(pltpu.with_memory_space_constraint(a, pltpu.HBM) for a in (velocity, forcing, viscosity)),
        spaces=[pltpu.HBM] * 3,
    )
    off = swap(off, "gx", 1)
    zb = swap(zb, "gy", 1)
    za = swap(za, "gy", 0)
    on = swap(on, "gx", 0)
    smooth, gc, ca, cb = call(
        residual_kernel,
        [tall, (3, CROWS, CCOLS, CDEPTH), CMSG, CMSG],
        [(ROWS + 2, COLS, DEPTH), (2, COLS, CDEPTH), (4 * CROWS * CCOLS, DEPTH)],
        own, on, zb, za, off, g, viscosity,
    )
    cb = swap(cb, "gy", 1)
    ca = swap(ca, "gy", 0)
    (gcw,) = call(
        corner_kernel,
        [(3, CROWS, CWIDE, CDEPTH)],
        [(576, DEPTH), (576, DEPTH), (16, 8, DEPTH), (256, DEPTH), (256, CDEPTH)],
        gc, cb, ca, off, on, zb, za, viscosity,
    )
    partner = swap(gcw, "gx", 0)
    cor, cedge = call(
        coarse_kernel,
        [(3, CROWS + 1, CWIDE, CDEPTH), (3, CWIDE, CDEPTH)],
        [(3, 2 * CROWS, CWIDE, CDEPTH)],
        gcw, partner,
    )
    cedge = swap(cedge, "gx", 1)
    out, first = call(
        inner_kernel,
        [velocity.shape, (3, COLS, DEPTH)],
        [
            velocity.shape, (2, WIDE, CDEPTH), (WIDE, DEPTH), (ROWS + 1, COLS, DEPTH),
            pltpu.SemaphoreType.DMA((3,)),
        ],
        smooth, cb, ca, cor, g,
        out_spaces=[pltpu.HBM, pltpu.VMEM],
    )
    (out,) = call(
        edge_kernel,
        [velocity.shape],
        [(3, COLS, DEPTH), (2, WIDE, CDEPTH), (WIDE, DEPTH), pltpu.SemaphoreType.DMA],
        smooth, cb, ca, first, cedge, out,
        spaces=[pltpu.VMEM] * 5 + [pltpu.HBM],
        out_spaces=[pltpu.HBM],
        aliases={5: 0},
    )
    return out


def solution(mesh):
    placed = (P(None, "gx", "gy", None), P(None, "gx", "gy", None), P("gx", "gy", None))
    return jax.shard_map(
        body, mesh=mesh, in_specs=placed, out_specs=P(None, "gx", "gy", None), check_vma=False
    )
```

```python
import jax
import jax.numpy as jnp
from jax import lax
from jax.experimental import pallas as pl
from jax.experimental.pallas import tpu as pltpu
from jax.sharding import PartitionSpec as P

KC = 4
CA = 1.0 - 0.8 * 16.5 / 14.5
CB = 0.8 * 2.0 / 8.0 / 14.5
CG = 0.8 / 14.5

ROWS = 8
COLS = 32
DEPTH = 256
HALF = 128
WIDE = 48
LEFT = 8
END = LEFT + COLS
CROWS = 4
CCOLS = 16
CWIDE = 24
CLEFT = 4
XMSG = (3, 2, 112, HALF)
EDGES = 3 * COLS
ZMSG = (4, 2, 32, HALF)
CMSG = (3, 56, HALF)
TALL = (3, ROWS + 4, 2, WIDE, HALF)
GRID = (3, ROWS, 2, WIDE, HALF)


def places():
    index_x = lax.axis_index("gx")
    index_y = lax.axis_index("gy")
    core = index_x % 2
    has_off = jnp.logical_and(index_x != 0, index_x != lax.axis_size("gx") - 1)
    even_y = index_y % 2 == 0
    return core, has_off, even_y, index_y != 0, index_y != lax.axis_size("gy") - 1


def row_of(core, row):
    return row + core * (ROWS - 1 - 2 * row)


def halves(a):
    return a[:, :HALF], a[:, HALF:]


def sums_depth(first, second):
    lane = lax.broadcasted_iota(jnp.int32, first.shape, 1)
    start = lane == 0
    stop = lane == HALF - 1
    up = pltpu.roll(first, 1, 1), pltpu.roll(second, 1, 1)
    down = pltpu.roll(first, HALF - 1, 1), pltpu.roll(second, HALF - 1, 1)
    return (
        (first + first) + (jnp.where(start, 0.0, up[0]) + jnp.where(stop, down[1], down[0])),
        (second + second) + (jnp.where(start, up[0], up[1]) + jnp.where(stop, 0.0, down[1])),
    )


def sums_columns(ref, first, size):
    mid = ref[first : first + size]
    return (mid + mid) + (ref[first - 1 : first - 1 + size] + ref[first + 1 : first + 1 + size])


def sums_rows(get, row, first, last):
    near = [get(r) for r in (row - 1, row + 1) if first <= r <= last]
    total = None
    if near:
        total = near[0] if len(near) == 1 else near[0] + near[1]
    if first <= row <= last:
        mid = get(row)
        total = mid + mid if total is None else total + (mid + mid)
    return total


def from_sides(even_y, a, b):
    return jnp.where(even_y, b, a), jnp.where(even_y, a, b)


def exact_dot(a, table):
    parts = []
    for part in range(3):
        parts.append(a.astype(jnp.bfloat16))
        if part < 2:
            a = a - parts[-1].astype(jnp.float32)
    table = table.astype(jnp.bfloat16)
    return jnp.dot(
        jnp.concatenate(parts, 1), jnp.concatenate([table] * 3, 0), preferred_element_type=jnp.float32
    )


def depth_pairs(first, second):
    fine = lax.broadcasted_iota(jnp.int32, (DEPTH, HALF), 0) // 2
    coarse = lax.broadcasted_iota(jnp.int32, (DEPTH, HALF), 1)
    return exact_dot(jnp.concatenate([first, second], 1), jnp.where(fine == coarse, 1.0, 0.0))


def lift_tables():
    coarse = lax.broadcasted_iota(jnp.int32, (HALF, DEPTH), 0)
    fine = lax.broadcasted_iota(jnp.int32, (HALF, DEPTH), 1)
    same = coarse == fine // 2
    beside = coarse == fine // 2 + 2 * (fine % 2) - 1
    copied = jnp.where(same, 1.0, 0.0)
    return jnp.where(beside, 1.0, 3.0 * copied), copied


def sweeps_kernel(
    v_hbm, f_hbm, e_hbm, own_ref, g_ref, e_ref, off_ref, on_ref, za_ref, zb_ref,
    v_ref, f_ref, i_ref, z_ref, y_ref, w_ref, sems,
):
    def copies_v(k):
        return [
            pltpu.make_async_copy(
                v_hbm.at[k, :, :, pl.ds(HALF * h, HALF)],
                v_ref.at[k, :, h, pl.ds(LEFT, COLS)],
                sems.at[2 * k + h],
            )
            for h in range(2)
        ]

    def copy_f(k):
        return pltpu.make_async_copy(f_hbm.at[k], f_ref.at[k], sems.at[6 + k])

    copy_e = pltpu.make_async_copy(e_hbm, e_ref, sems.at[9])
    for copy in copies_v(0):
        copy.start()
    copy_e.start()
    copy_f(0).start()
    for k in range(1, 3):
        for copy in copies_v(k):
            copy.start()
        copy_f(k).start()
    core, has_off, even_y, has_low, has_high = places()
    none = jnp.zeros((LEFT, HALF), jnp.float32)
    for k in range(3):
        for h in range(2):
            for r in range(ROWS):
                for ref in (v_ref, g_ref, z_ref):
                    ref[k, r, h, :LEFT] = none
                    ref[k, r, h, END:] = none
            for r in range(ROWS + 2):
                w_ref[k, r, h, :LEFT] = none
                w_ref[k, r, h, WIDE:] = none
    for k in range(3):
        for copy in copies_v(k):
            copy.wait()
        for r in range(ROWS):
            pair = sums_depth(*(v_ref[k, row_of(core, r), h, LEFT:END] for h in range(2)))
            for h in range(2):
                z_ref[k, r, h, LEFT:END] = pair[h]
    copy_e.wait()
    for r in range(ROWS):
        own = row_of(core, r)
        i_ref[r] = CG / e_ref[own]
        for h in range(2):
            low = e_ref[own, :4, HALF * h : HALF * (h + 1)]
            high = e_ref[own, COLS - 4 :, HALF * h : HALF * (h + 1)]
            za_ref[3, h, 4 * r : 4 * r + 4] = jnp.where(even_y, high, low)
            zb_ref[3, h, 4 * r : 4 * r + 4] = jnp.where(even_y, low, high)
    for k in range(3):
        copy_f(k).wait()
        for r in range(ROWS):
            for h, part in enumerate(halves(f_ref[k, row_of(core, r)] * i_ref[r])):
                g_ref[k, r, h, LEFT:END] = part
    for k in range(3):
        for h in range(2):
            for r in range(ROWS):
                y_ref[k, r, h] = sums_columns(z_ref.at[k, r, h], LEFT - 4, COLS + 8)
            for r in range(-1, ROWS + 1):
                value = CB * sums_rows(lambda i: y_ref[k, i, h], r, 0, ROWS - 1)
                if 0 <= r < ROWS:
                    value = value + (
                        CA * v_ref[k, row_of(core, r), h, LEFT - 4 : END + 4]
                        + g_ref[k, r, h, LEFT - 4 : END + 4]
                    )
                w_ref[k, r + 1, h, LEFT:WIDE] = value

    @pl.when(jnp.logical_not(has_off))
    def _():
        w_ref[:, 0] = jnp.zeros((3, 2, WIDE + LEFT, HALF), jnp.float32)

    @pl.when(jnp.logical_not(has_low))
    def _():
        w_ref[:, :, :, LEFT : LEFT + 4] = jnp.zeros((3, ROWS + 2, 2, 4, HALF), jnp.float32)

    @pl.when(jnp.logical_not(has_high))
    def _():
        w_ref[:, :, :, WIDE - 4 : WIDE] = jnp.zeros((3, ROWS + 2, 2, 4, HALF), jnp.float32)

    for k in range(3):
        for r in range(ROWS + 2):
            pair = sums_depth(*(sums_columns(w_ref.at[k, r, h], LEFT, COLS + 8) for h in range(2)))
            for h in range(2):
                y_ref[k, r, h] = pair[h]
    for k in range(3):
        for h in range(2):
            for r in range(-2, ROWS + 2):
                value = CB * sums_rows(lambda i: y_ref[k, i + 1, h], r, -1, ROWS)
                if -1 <= r <= ROWS:
                    value = value + CA * w_ref[k, r + 1, h, LEFT:WIDE]
                if 0 <= r < ROWS:
                    value = value + g_ref[k, r, h, LEFT - 4 : END + 4]
                own_ref[k, r + 2, h, LEFT - 4 : END + 4] = value

    @pl.when(jnp.logical_not(has_off))
    def _():
        own_ref[:, :2] = jnp.zeros((3, 2, 2, WIDE, HALF), jnp.float32)

    @pl.when(jnp.logical_not(has_low))
    def _():
        own_ref[:, :, :, LEFT - 4 : LEFT] = jnp.zeros((3, ROWS + 4, 2, 4, HALF), jnp.float32)

    @pl.when(jnp.logical_not(has_high))
    def _():
        own_ref[:, :, :, END : END + 4] = jnp.zeros((3, ROWS + 4, 2, 4, HALF), jnp.float32)

    for k in range(3):
        for h in range(2):
            for ref, rows in ((off_ref, (0, -1, -2)), (on_ref, (ROWS - 1, ROWS, ROWS + 1))):
                for slot, r in enumerate(rows):
                    ref[k, h, COLS * slot : COLS * (slot + 1)] = own_ref[k, r + 2, h, LEFT:END]
                    at = EDGES + 4 * slot
                    ref[k, h, at : at + 2] = own_ref[k, r + 2, h, LEFT - 2 : LEFT]
                    ref[k, h, at + 2 : at + 4] = own_ref[k, r + 2, h, END : END + 2]
            for r in range(-1, ROWS + 1):
                at = 3 * (r + 1)
                low = own_ref[k, r + 2, h, LEFT - 2 : LEFT + 1]
                high = own_ref[k, r + 2, h, END - 1 : END + 2]
                za_ref[k, h, at : at + 3] = jnp.where(even_y, high, low)
                zb_ref[k, h, at : at + 3] = jnp.where(even_y, low, high)


def spill(ref, k, h, slot):
    at = EDGES + 4 * slot
    low = jnp.concatenate([ref[k, h, at : at + 2], ref[k, h, COLS * slot : COLS * slot + 1]], 0)
    high = jnp.concatenate(
        [ref[k, h, COLS * (slot + 1) - 1 : COLS * (slot + 1)], ref[k, h, at + 2 : at + 4]], 0
    )
    return low, high


def paired_columns(ref, value):
    ref[...] = value
    return ref[pl.ds(0, CCOLS, stride=2)] + ref[pl.ds(1, CCOLS, stride=2)]


def residual_kernel(
    _, on_ref, zb_ref, za_ref, off_ref, g_ref, e_ref, s_ref, u_ref, gc_ref, ca_ref, cb_ref, r_ref, q_ref
):
    core, _, even_y, _, _ = places()
    for k in range(3):
        for h in range(2):
            for r in range(-1, ROWS + 1):
                row = s_ref.at[k, r + 2, h]
                at = 3 * (r + 1)
                low, high = from_sides(even_y, za_ref[k, h, at : at + 3], zb_ref[k, h, at : at + 3])
                row[LEFT - 1 : LEFT + 2] = row[LEFT - 1 : LEFT + 2] + low
                row[END - 2 : END + 1] = row[END - 2 : END + 1] + high
                for ref, slot in ((off_ref, r + 1), (on_ref, ROWS - r)):
                    if 0 <= slot < 3:
                        at = EDGES + 4 * slot
                        row[LEFT:END] = row[LEFT:END] + ref[k, h, COLS * slot : COLS * (slot + 1)]
                        row[LEFT - 1 : LEFT] = row[LEFT - 1 : LEFT] + ref[k, h, at + 1 : at + 2]
                        row[END : END + 1] = row[END : END + 1] + ref[k, h, at + 2 : at + 3]
    for k in range(3):
        for r in range(ROWS + 2):
            pair = sums_depth(*(sums_columns(s_ref.at[k, r + 1, h], LEFT, COLS) for h in range(2)))
            for h in range(2):
                u_ref[k, r, h] = pair[h]
    for j in range(CROWS):
        value = halves(e_ref[row_of(core, 2 * j)] + e_ref[row_of(core, 2 * j + 1)])
        for h in range(2):
            at = CCOLS * (3 * CROWS + j)
            q_ref[h, at : at + CCOLS] = paired_columns(r_ref.at[3, j, h], value[h])
        for k in range(3):
            for h in range(2):
                total = None
                for r in (2 * j, 2 * j + 1):
                    near = sums_rows(lambda i: u_ref[k, i + 1, h], r, -1, ROWS)
                    value_r = e_ref[row_of(core, r), :, HALF * h : HALF * (h + 1)] * (
                        g_ref[k, r, h, LEFT:END]
                        - (16.5 * CG) * s_ref[k, r + 2, h, LEFT:END]
                        + (2.0 / 8.0 * CG) * near
                    )
                    total = value_r if total is None else total + value_r
                at = CCOLS * (k * CROWS + j)
                q_ref[h, at : at + CCOLS] = paired_columns(r_ref.at[k, j, h], total)
    for k in range(3):
        for h in range(2):
            for side, ref in enumerate((off_ref, on_ref)):
                for slot in range(3):
                    low, high = spill(ref, k, h, slot)
                    at = 16 + 18 * h + 9 * side + 3 * slot
                    ca_ref[k, at : at + 3] = jnp.where(even_y, high, low)
                    cb_ref[k, at : at + 3] = jnp.where(even_y, low, high)
    sums = depth_pairs(q_ref[0], q_ref[1])
    size = CROWS * CCOLS
    inverse = 4.0 / sums[3 * size :]
    for k in range(3):
        value = sums[k * size : (k + 1) * size] * inverse
        for j in range(CROWS):
            row = value[j * CCOLS : (j + 1) * CCOLS]
            gc_ref[k, j] = row
            low = row[:4]
            high = row[CCOLS - 4 :]
            ca_ref[k, 4 * j : 4 * j + 4] = jnp.where(even_y, high, low)
            cb_ref[k, 4 * j : 4 * j + 4] = jnp.where(even_y, low, high)


OWN_AT = (4, 0)
MINE_AT = (3, 2)
THEIRS_AT = (2, 3)


def window_at(k, side, window):
    return 16 * ((k * 2 + side) * 2 + window)


def spilled_at(k, side, window, slot):
    return 8 * (((k * 2 + side) * 2 + window) * 3 + slot)


def corner_residuals(d_ref, u_ref, w_ref, keep, put):
    size = d_ref.shape[1]
    for h in range(2):
        value = d_ref[h]
        u_ref[h] = (value + value) + (pltpu.roll(value, 1, 0) + pltpu.roll(value, size - 1, 0))
    sums = sums_depth(u_ref[0], u_ref[1])
    for h in range(2):
        u_ref[h] = sums[h]
    for k in range(3):
        for side in range(2):
            for window in range(2):
                for h in range(2):
                    rows = []
                    at = spilled_at(k, side, window, 0)
                    for q in range(3):
                        part = (-2.0 / 8.0) * sums_rows(
                            lambda i: u_ref[h, at + 8 * (i + 1) : at + 8 * (i + 2)], q, -1, 1
                        )
                        if q < 2:
                            part = part + 16.5 * d_ref[h, at + 8 * (q + 1) : at + 8 * (q + 2)]
                        n = (side * 2 + window) * 4 + q
                        rows.append(jnp.where(keep[window], -w_ref[n, h] * part, 0.0))
                    put(h, window_at(k, side, window), rows[0] + rows[1], rows[2])


def own_places():
    place = lax.broadcasted_iota(jnp.int32, (8, HALF), 0)
    return place >= 4, place < 4


def spilled_kernel(
    on_ref, zb_ref, za_ref, off_ref, e_ref, s_ref, near_ref, g_ref,
    w_ref, r_ref, inverse_ref, base_ref, d_ref, u_ref, q_ref,
):
    core, _, even_y, _, _ = places()
    d_ref[...] = jnp.zeros_like(d_ref)
    for h in range(2):
        for side, ref in enumerate((off_ref, on_ref)):
            for k in range(3):
                for slot in range(3):
                    theirs = spill(ref, k, h, slot)
                    for window in range(2):
                        at = spilled_at(k, side, window, slot) + THEIRS_AT[window]
                        d_ref[h, at : at + 3] = theirs[window]
            for q in range(4):
                r = q if side == 0 else ROWS - 1 - q
                halo = from_sides(
                    even_y, za_ref[3, h, 4 * r : 4 * r + 4], zb_ref[3, h, 4 * r : 4 * r + 4]
                )
                for window, first in enumerate((0, COLS - 4)):
                    n = (side * 2 + window) * 4 + q
                    at = OWN_AT[window]
                    w_ref[n, h, at : at + 4] = e_ref[
                        row_of(core, r), first : first + 4, HALF * h : HALF * (h + 1)
                    ]
                    w_ref[n, h, 4 - at : 8 - at] = halo[window]
                    if q % 2:
                        at = window_at(0, side, window) + 8 * (q // 2)
                        q_ref[h, at : at + 8] = w_ref[n - 1, h] + w_ref[n, h]

    def put(h, at, first, second):
        r_ref[h, at : at + 8] = first
        r_ref[h, at + 8 : at + 16] = second

    own = own_places()
    corner_residuals(d_ref, u_ref, w_ref, (jnp.logical_not(own[0]), jnp.logical_not(own[1])), put)
    q_ref[0, :64] = depth_pairs(q_ref[0], q_ref[1])
    visc = q_ref[0, pl.ds(0, 32, stride=2)] + q_ref[0, pl.ds(1, 32, stride=2)]
    inverse_ref[...] = jnp.where(visc > 0.0, (4.0 * CG) / jnp.where(visc > 0.0, visc, 1.0), 0.0)
    for k in range(3):
        for h in range(2):
            for r in range(ROWS):
                base_ref[k, r, h] = (
                    CA * s_ref[k, r + 2, h, LEFT:END]
                    + g_ref[k, r, h, LEFT:END]
                    + CB * sums_rows(lambda i: near_ref[k, i + 1, h], r, -1, ROWS)
                )


def corner_kernel(
    gc_ref, cb_ref, ca_ref, w_ref, s_ref, inverse_ref, out_ref, edge_ref, d_ref, u_ref, r_ref, q_ref
):
    _, _, even_y, has_low, has_high = places()
    d_ref[...] = jnp.zeros_like(d_ref)
    for h in range(2):
        for side in range(2):
            for k in range(3):
                for slot in range(3):
                    mine = corner_rows(ca_ref, cb_ref, even_y, k, h, side, slot)
                    for window in range(2):
                        at = spilled_at(k, side, window, slot) + MINE_AT[window]
                        d_ref[h, at : at + 3] = mine[window]

    def put(h, at, first, second):
        r_ref[h, at : at + 8] = first + s_ref[h, at : at + 8]
        r_ref[h, at + 8 : at + 16] = second + s_ref[h, at + 8 : at + 16]

    corner_residuals(d_ref, u_ref, w_ref, own_places(), put)
    q_ref[...] = depth_pairs(r_ref[0], r_ref[1])
    sums = q_ref[pl.ds(0, 96, stride=2)] + q_ref[pl.ds(1, 96, stride=2)]
    for k in range(3):
        value = sums[32 * k : 32 * (k + 1)] * inverse_ref[...]
        for j in range(CROWS):
            low, high = from_sides(even_y, ca_ref[k, 4 * j : 4 * j + 4], cb_ref[k, 4 * j : 4 * j + 4])
            out_ref[k, j] = jnp.concatenate([low, gc_ref[k, j], high], 0)
            side, half = (0, j) if j < 2 else (1, CROWS - 1 - j)
            for window, first in enumerate((2, CWIDE - 6)):
                at = 4 * ((side * 2 + window) * 2 + half)
                out_ref[k, j, first : first + 4] = out_ref[k, j, first : first + 4] + value[at : at + 4]
    mask = column_mask((CWIDE, HALF), CLEFT, CCOLS, has_low, has_high)
    edge_ref[...] = coarse_sweeps(out_ref[...], 0, mask)[:, 0]


def corner_rows(ca_ref, cb_ref, even_y, k, h, side, slot):
    at = 16 + 18 * h + 9 * side + 3 * slot
    return from_sides(even_y, ca_ref[k, at : at + 3], cb_ref[k, at : at + 3])


def column_mask(shape, left, width, has_low, has_high):
    place = lax.broadcasted_iota(jnp.int32, shape, 0)
    keep = jnp.logical_and(
        jnp.logical_or(place >= left, has_low), jnp.logical_or(place < left + width, has_high)
    )
    return jnp.where(keep, 1.0, 0.0)


def coarse_sweeps(rhs, last, mask):
    value = rhs
    for left in range(KC - 2, -1, -1):
        rows = min(last + 1 + left, rhs.shape[1])
        given = min(rows + 1, rhs.shape[1])
        u = value[:, :given].reshape(3 * given * CWIDE, HALF)
        size = u.shape[0]
        u = (u + u) + (pltpu.roll(u, 1, 0) + pltpu.roll(u, size - 1, 0))
        lane = lax.broadcasted_iota(jnp.int32, u.shape, 1)
        u = (u + u) + (
            jnp.where(lane == 0, 0.0, pltpu.roll(u, 1, 1))
            + jnp.where(lane == HALF - 1, 0.0, pltpu.roll(u, HALF - 1, 1))
        )
        u = u.reshape(3, given, CWIDE, HALF)
        none = jnp.zeros((3, 1, CWIDE, HALF), jnp.float32)
        before = jnp.concatenate([none, u[:, : rows - 1]], 1) if rows > 1 else none
        after = u[:, 1:given]
        if given == rows:
            after = jnp.concatenate([after, none], 1)
        near = (u[:, :rows] + u[:, :rows]) + (before + after)
        value = mask * (CA * value[:, :rows] + CB * near + rhs[:, :rows])
    return value


def coarse_kernel(own_ref, partner_ref, cor_ref, c_ref):
    _, _, _, has_low, has_high = places()
    mask = column_mask((CWIDE, HALF), CLEFT, CCOLS, has_low, has_high)
    for k in range(3):
        for r in range(CROWS):
            c_ref[k, r] = own_ref[k, r]
            c_ref[k, 2 * CROWS - 1 - r] = partner_ref[k, r]
    cor_ref[...] = coarse_sweeps(c_ref[...], CROWS, mask)


def lifted_columns(ref, value):
    mid = 3.0 * value[CLEFT : CLEFT + CCOLS]
    ref[pl.ds(0, CCOLS, stride=2)] = mid + value[CLEFT - 1 : CLEFT - 1 + CCOLS]
    ref[pl.ds(1, CCOLS, stride=2)] = mid + value[CLEFT + 1 : CLEFT + 1 + CCOLS]


def inner_kernel(base_ref, d_ref, u_ref, cor_ref, o_ref, z_ref, p_ref, l_ref):
    core, _, _, _, _ = places()
    sums, copies = lift_tables()
    sums = exact_dot(cor_ref[...].reshape(3 * (CROWS + 1) * CWIDE, HALF), sums)
    copies = exact_dot(
        cor_ref[:, :CROWS, CLEFT : CLEFT + CCOLS].reshape(3 * CROWS * CCOLS, HALF), copies
    )
    for k in range(3):
        for h in range(2):
            lanes = slice(HALF * h, HALF * (h + 1))
            for j in range(CROWS + 1):
                at = (k * (CROWS + 1) + j) * CWIDE
                z_ref[k, j, h] = sums[at : at + CWIDE, lanes]
                lifted_columns(p_ref.at[k, j, h], z_ref.at[k, j, h])
                if j < CROWS:
                    at = (k * CROWS + j) * CCOLS
                    l_ref[k, j, h, pl.ds(0, CCOLS, stride=2)] = copies[at : at + CCOLS, lanes]
                    l_ref[k, j, h, pl.ds(1, CCOLS, stride=2)] = copies[at : at + CCOLS, lanes]
            for r in range(ROWS):
                j = r // 2
                beside = j + 2 * (r % 2) - 1
                total = 3.0 * p_ref[k, j, h]
                if beside >= 0:
                    total = total + p_ref[k, beside, h]
                row = o_ref.at[k, h, row_of(core, r)]
                row[...] = base_ref[k, r, h] + (CA * l_ref[k, j, h] + CB * total)
                side, q = (0, r) if r < 3 else (1, ROWS - 1 - r)
                if q < 3:
                    for window, first in enumerate((0, COLS - 4)):
                        at = spilled_at(k, side, window, 0)
                        fix = CB * sums_rows(
                            lambda i: u_ref[h, at + 8 * (i + 1) : at + 8 * (i + 2)], q, -1, 1
                        )
                        if q < 2:
                            fix = fix + CA * d_ref[h, at + 8 * (q + 1) : at + 8 * (q + 2)]
                        fix = fix[OWN_AT[window] : OWN_AT[window] + 4]
                        row[first : first + 4] = row[first : first + 4] + fix


def edge_kernel(inner_ref, next_ref, out_hbm, o_ref, z_ref, p_ref, sems):
    core, _, _, _, _ = places()
    begin = 1 - core
    copies = []

    def copy(source, target):
        copies.append(pltpu.make_async_copy(source, target, sems.at[len(copies)]))
        copies[-1].start()

    for k in range(3):
        for h in range(2):
            rows = pl.ds(begin, ROWS - 1)
            copy(inner_ref.at[k, h, rows], out_hbm.at[k, rows, :, pl.ds(HALF * h, HALF)])
    lifted = exact_dot(next_ref[...].reshape(3 * CWIDE, HALF), lift_tables()[0])
    own = row_of(core, 0)
    for k in range(3):
        for h in range(2):
            z_ref[k, h] = lifted[k * CWIDE : (k + 1) * CWIDE, HALF * h : HALF * (h + 1)]
            lifted_columns(p_ref.at[k, h], z_ref.at[k, h])
            o_ref[k, h] = inner_ref[k, h, own] + CB * p_ref[k, h]
            copy(o_ref.at[k, h], out_hbm.at[k, own, :, pl.ds(HALF * h, HALF)])
    for started in copies:
        started.wait()


def call(kernel, outs, scratch, *args, spaces=None, out_spaces=None, aliases=None):
    spaces = spaces or [pltpu.VMEM] * len(args)
    out_spaces = out_spaces or [pltpu.VMEM] * len(outs)
    return pl.pallas_call(
        kernel,
        out_shape=[jax.ShapeDtypeStruct(o, jnp.float32) for o in outs],
        in_specs=[pl.BlockSpec(memory_space=space) for space in spaces],
        out_specs=[pl.BlockSpec(memory_space=space) for space in out_spaces],
        scratch_shapes=[pltpu.VMEM(s, jnp.float32) if isinstance(s, tuple) else s for s in scratch],
        input_output_aliases=aliases or {},
        compiler_params=pltpu.CompilerParams(vmem_limit_bytes=24 * 2**20),
    )(*args)


def swap(value, axis, parity):
    pairs = []
    for i in range(parity, lax.axis_size(axis) - 1, 2):
        pairs += [(i, i + 1), (i + 1, i)]
    return lax.ppermute(value, axis, pairs)


def body(velocity, forcing, viscosity):
    own, g, visc, off, on, za, zb = call(
        sweeps_kernel,
        [TALL, GRID, viscosity.shape, XMSG, XMSG, ZMSG, ZMSG],
        [
            GRID, forcing.shape, viscosity.shape, GRID,
            (3, ROWS + 2, 2, COLS + 8, HALF), (3, ROWS + 2, 2, WIDE + LEFT, HALF),
            pltpu.SemaphoreType.DMA((10,)),
        ],
        *(pltpu.with_memory_space_constraint(a, pltpu.HBM) for a in (velocity, forcing, viscosity)),
        spaces=[pltpu.HBM] * 3,
    )
    on = swap(on, "gx", 0)
    off = swap(off, "gx", 1)
    zb = swap(zb, "gy", 1)
    za = swap(za, "gy", 0)
    smooth, near, gc, ca, cb = call(
        residual_kernel,
        [TALL, (3, ROWS + 2, 2, COLS, HALF), (3, CROWS, CCOLS, HALF), CMSG, CMSG],
        [(4, CROWS, 2, COLS, HALF), (2, 4 * CROWS * CCOLS, HALF)],
        own, on, zb, za, off, g, visc,
        aliases={0: 0},
    )
    cb = swap(cb, "gy", 1)
    ca = swap(ca, "gy", 0)
    spilled = (2, 36 * 8, HALF)
    tile = (3, ROWS, 2, COLS, HALF)
    windows, sums, inverse, base = call(
        spilled_kernel,
        [(16, 2, 8, HALF), (2, 12 * 16, HALF), (32, HALF), tile],
        [spilled, spilled, (2, 64, HALF)],
        on, zb, za, off, visc, smooth, near, g,
    )
    rhs, edge, corner, around = call(
        corner_kernel,
        [(3, CROWS, CWIDE, HALF), (3, CWIDE, HALF), spilled, spilled],
        [(2, 12 * 16, HALF), (12 * 16, HALF)],
        gc, cb, ca, windows, sums, inverse,
    )
    beyond = swap(edge, "gx", 1)
    partner = swap(rhs, "gx", 0)
    (cor,) = call(
        coarse_kernel,
        [(3, CROWS + 1, CWIDE, HALF)],
        [(3, 2 * CROWS, CWIDE, HALF)],
        rhs, partner,
    )
    half_rows = (3, 2, COLS, HALF)
    (inner,) = call(
        inner_kernel,
        [(3, 2, ROWS, COLS, HALF)],
        [
            (3, CROWS + 1, 2, CWIDE, HALF), (3, CROWS + 1, 2, COLS, HALF), (3, CROWS, 2, COLS, HALF),
        ],
        base, corner, around, cor,
    )
    (out,) = call(
        edge_kernel,
        [velocity.shape],
        [half_rows, (3, 2, CWIDE, HALF), half_rows, pltpu.SemaphoreType.DMA((12,))],
        inner, beyond,
        out_spaces=[pltpu.HBM],
    )
    return out


def solution(mesh):
    placed = (P(None, "gx", "gy", None), P(None, "gx", "gy", None), P("gx", "gy", None))
    return jax.shard_map(
        body, mesh=mesh, in_specs=placed, out_specs=P(None, "gx", "gy", None), check_vma=False
    )
```

```python
import jax
import jax.numpy as jnp
from jax import lax
from jax.experimental import pallas as pl
from jax.experimental.pallas import tpu as pltpu
from jax.sharding import PartitionSpec as P

KC = 4
CA = 1.0 - 0.8 * 16.5 / 14.5
CB = 0.8 * 2.0 / 8.0 / 14.5
CG = 0.8 / 14.5

ROWS = 8
COLS = 32
DEPTH = 256
HALF = 128
WIDE = 48
LEFT = 8
END = LEFT + COLS
CROWS = 4
CCOLS = 16
CWIDE = 24
CLEFT = 4
XMSG = (3, 2, 112, HALF)
EDGES = 3 * COLS
ZMSG = (4, 2, 32, HALF)
CMSG = (3, 56, HALF)
TALL = (3, ROWS + 4, 2, WIDE, HALF)
GRID = (3, ROWS, 2, WIDE, HALF)


def places():
    index_x = lax.axis_index("gx")
    index_y = lax.axis_index("gy")
    core = index_x % 2
    has_off = jnp.logical_and(index_x != 0, index_x != lax.axis_size("gx") - 1)
    even_y = index_y % 2 == 0
    return core, has_off, even_y, index_y != 0, index_y != lax.axis_size("gy") - 1


def row_of(core, row):
    return row + core * (ROWS - 1 - 2 * row)


def halves(a):
    return a[:, :HALF], a[:, HALF:]


def sums_depth(first, second):
    lane = lax.broadcasted_iota(jnp.int32, first.shape, 1)
    start = lane == 0
    stop = lane == HALF - 1
    up = pltpu.roll(first, 1, 1), pltpu.roll(second, 1, 1)
    down = pltpu.roll(first, HALF - 1, 1), pltpu.roll(second, HALF - 1, 1)
    return (
        (first + first) + (jnp.where(start, 0.0, up[0]) + jnp.where(stop, down[1], down[0])),
        (second + second) + (jnp.where(start, up[0], up[1]) + jnp.where(stop, 0.0, down[1])),
    )


def sums_columns(ref, first, size):
    mid = ref[first : first + size]
    return (mid + mid) + (ref[first - 1 : first - 1 + size] + ref[first + 1 : first + 1 + size])


def sums_rows(get, row, first, last):
    near = [get(r) for r in (row - 1, row + 1) if first <= r <= last]
    total = None
    if near:
        total = near[0] if len(near) == 1 else near[0] + near[1]
    if first <= row <= last:
        mid = get(row)
        total = mid + mid if total is None else total + (mid + mid)
    return total


def from_sides(even_y, a, b):
    return jnp.where(even_y, b, a), jnp.where(even_y, a, b)


def exact_dot(a, table):
    parts = []
    for part in range(3):
        parts.append(a.astype(jnp.bfloat16))
        if part < 2:
            a = a - parts[-1].astype(jnp.float32)
    table = table.astype(jnp.bfloat16)
    return jnp.dot(
        jnp.concatenate(parts, 1), jnp.concatenate([table] * 3, 0), preferred_element_type=jnp.float32
    )


def depth_pairs(first, second):
    fine = lax.broadcasted_iota(jnp.int32, (DEPTH, HALF), 0) // 2
    coarse = lax.broadcasted_iota(jnp.int32, (DEPTH, HALF), 1)
    return exact_dot(jnp.concatenate([first, second], 1), jnp.where(fine == coarse, 1.0, 0.0))


def lift_tables():
    coarse = lax.broadcasted_iota(jnp.int32, (HALF, DEPTH), 0)
    fine = lax.broadcasted_iota(jnp.int32, (HALF, DEPTH), 1)
    same = coarse == fine // 2
    beside = coarse == fine // 2 + 2 * (fine % 2) - 1
    copied = jnp.where(same, 1.0, 0.0)
    return jnp.where(beside, 1.0, 3.0 * copied), copied


def sweeps_kernel(
    v_hbm, f_hbm, e_hbm, own_ref, g_ref, e_ref, off_ref, on_ref, za_ref, zb_ref,
    v_ref, f_ref, i_ref, z_ref, y_ref, w_ref, sems,
):
    def copies_v(k):
        return [
            pltpu.make_async_copy(
                v_hbm.at[k, :, :, pl.ds(HALF * h, HALF)],
                v_ref.at[k, :, h, pl.ds(LEFT, COLS)],
                sems.at[2 * k + h],
            )
            for h in range(2)
        ]

    def copy_f(k):
        return pltpu.make_async_copy(f_hbm.at[k], f_ref.at[k], sems.at[6 + k])

    copy_e = pltpu.make_async_copy(e_hbm, e_ref, sems.at[9])
    for k in range(3):
        for copy in copies_v(k):
            copy.start()
    copy_e.start()
    for k in range(3):
        copy_f(k).start()
    core, has_off, even_y, has_low, has_high = places()
    none = jnp.zeros((LEFT, HALF), jnp.float32)
    for k in range(3):
        for h in range(2):
            for r in range(ROWS):
                for ref in (v_ref, g_ref, z_ref):
                    ref[k, r, h, :LEFT] = none
                    ref[k, r, h, END:] = none
            for r in range(ROWS + 2):
                w_ref[k, r, h, :LEFT] = none
                w_ref[k, r, h, WIDE:] = none
    for k in range(3):
        for copy in copies_v(k):
            copy.wait()
        for r in range(ROWS):
            pair = sums_depth(*(v_ref[k, row_of(core, r), h, LEFT:END] for h in range(2)))
            for h in range(2):
                z_ref[k, r, h, LEFT:END] = pair[h]
    copy_e.wait()
    for r in range(ROWS):
        own = row_of(core, r)
        i_ref[r] = CG / e_ref[own]
        for h in range(2):
            low = e_ref[own, :4, HALF * h : HALF * (h + 1)]
            high = e_ref[own, COLS - 4 :, HALF * h : HALF * (h + 1)]
            za_ref[3, h, 4 * r : 4 * r + 4] = jnp.where(even_y, high, low)
            zb_ref[3, h, 4 * r : 4 * r + 4] = jnp.where(even_y, low, high)
    for k in range(3):
        copy_f(k).wait()
        for r in range(ROWS):
            for h, part in enumerate(halves(f_ref[k, row_of(core, r)] * i_ref[r])):
                g_ref[k, r, h, LEFT:END] = part
    for k in range(3):
        for h in range(2):
            for r in range(ROWS):
                y_ref[k, r, h] = sums_columns(z_ref.at[k, r, h], LEFT - 4, COLS + 8)
            for r in range(-1, ROWS + 1):
                value = CB * sums_rows(lambda i: y_ref[k, i, h], r, 0, ROWS - 1)
                if 0 <= r < ROWS:
                    value = value + (
                        CA * v_ref[k, row_of(core, r), h, LEFT - 4 : END + 4]
                        + g_ref[k, r, h, LEFT - 4 : END + 4]
                    )
                w_ref[k, r + 1, h, LEFT:WIDE] = value

    @pl.when(jnp.logical_not(has_off))
    def _():
        w_ref[:, 0] = jnp.zeros((3, 2, WIDE + LEFT, HALF), jnp.float32)

    @pl.when(jnp.logical_not(has_low))
    def _():
        w_ref[:, :, :, LEFT : LEFT + 4] = jnp.zeros((3, ROWS + 2, 2, 4, HALF), jnp.float32)

    @pl.when(jnp.logical_not(has_high))
    def _():
        w_ref[:, :, :, WIDE - 4 : WIDE] = jnp.zeros((3, ROWS + 2, 2, 4, HALF), jnp.float32)

    for k in range(3):
        for r in range(ROWS + 2):
            pair = sums_depth(*(sums_columns(w_ref.at[k, r, h], LEFT, COLS + 8) for h in range(2)))
            for h in range(2):
                y_ref[k, r, h] = pair[h]
    for k in range(3):
        for h in range(2):
            for r in range(-2, ROWS + 2):
                value = CB * sums_rows(lambda i: y_ref[k, i + 1, h], r, -1, ROWS)
                if -1 <= r <= ROWS:
                    value = value + CA * w_ref[k, r + 1, h, LEFT:WIDE]
                if 0 <= r < ROWS:
                    value = value + g_ref[k, r, h, LEFT - 4 : END + 4]
                own_ref[k, r + 2, h, LEFT - 4 : END + 4] = value

    @pl.when(jnp.logical_not(has_off))
    def _():
        own_ref[:, :2] = jnp.zeros((3, 2, 2, WIDE, HALF), jnp.float32)

    @pl.when(jnp.logical_not(has_low))
    def _():
        own_ref[:, :, :, LEFT - 4 : LEFT] = jnp.zeros((3, ROWS + 4, 2, 4, HALF), jnp.float32)

    @pl.when(jnp.logical_not(has_high))
    def _():
        own_ref[:, :, :, END : END + 4] = jnp.zeros((3, ROWS + 4, 2, 4, HALF), jnp.float32)

    for k in range(3):
        for h in range(2):
            for ref, rows in ((off_ref, (0, -1, -2)), (on_ref, (ROWS - 1, ROWS, ROWS + 1))):
                for slot, r in enumerate(rows):
                    ref[k, h, COLS * slot : COLS * (slot + 1)] = own_ref[k, r + 2, h, LEFT:END]
                    at = EDGES + 4 * slot
                    ref[k, h, at : at + 2] = own_ref[k, r + 2, h, LEFT - 2 : LEFT]
                    ref[k, h, at + 2 : at + 4] = own_ref[k, r + 2, h, END : END + 2]
            for r in range(-1, ROWS + 1):
                at = 3 * (r + 1)
                low = own_ref[k, r + 2, h, LEFT - 2 : LEFT + 1]
                high = own_ref[k, r + 2, h, END - 1 : END + 2]
                za_ref[k, h, at : at + 3] = jnp.where(even_y, high, low)
                zb_ref[k, h, at : at + 3] = jnp.where(even_y, low, high)


def spill(ref, k, h, slot):
    at = EDGES + 4 * slot
    low = jnp.concatenate([ref[k, h, at : at + 2], ref[k, h, COLS * slot : COLS * slot + 1]], 0)
    high = jnp.concatenate(
        [ref[k, h, COLS * (slot + 1) - 1 : COLS * (slot + 1)], ref[k, h, at + 2 : at + 4]], 0
    )
    return low, high


def paired_columns(ref, value):
    ref[...] = value
    return ref[pl.ds(0, CCOLS, stride=2)] + ref[pl.ds(1, CCOLS, stride=2)]


def residual_kernel(
    _, on_ref, zb_ref, za_ref, off_ref, g_ref, e_ref, s_ref, u_ref, gc_ref, ca_ref, cb_ref, r_ref, q_ref
):
    core, _, even_y, _, _ = places()
    for k in range(3):
        for h in range(2):
            for r in range(-1, ROWS + 1):
                row = s_ref.at[k, r + 2, h]
                at = 3 * (r + 1)
                low, high = from_sides(even_y, za_ref[k, h, at : at + 3], zb_ref[k, h, at : at + 3])
                row[LEFT - 1 : LEFT + 2] = row[LEFT - 1 : LEFT + 2] + low
                row[END - 2 : END + 1] = row[END - 2 : END + 1] + high
                for ref, slot in ((off_ref, r + 1), (on_ref, ROWS - r)):
                    if 0 <= slot < 3:
                        at = EDGES + 4 * slot
                        row[LEFT:END] = row[LEFT:END] + ref[k, h, COLS * slot : COLS * (slot + 1)]
                        row[LEFT - 1 : LEFT] = row[LEFT - 1 : LEFT] + ref[k, h, at + 1 : at + 2]
                        row[END : END + 1] = row[END : END + 1] + ref[k, h, at + 2 : at + 3]
    for k in range(3):
        for r in range(ROWS + 2):
            pair = sums_depth(*(sums_columns(s_ref.at[k, r + 1, h], LEFT, COLS) for h in range(2)))
            for h in range(2):
                u_ref[k, r, h] = pair[h]
    for j in range(CROWS):
        value = halves(e_ref[row_of(core, 2 * j)] + e_ref[row_of(core, 2 * j + 1)])
        for h in range(2):
            at = CCOLS * (3 * CROWS + j)
            q_ref[h, at : at + CCOLS] = paired_columns(r_ref.at[3, j, h], value[h])
        for k in range(3):
            for h in range(2):
                total = None
                for r in (2 * j, 2 * j + 1):
                    near = sums_rows(lambda i: u_ref[k, i + 1, h], r, -1, ROWS)
                    value_r = e_ref[row_of(core, r), :, HALF * h : HALF * (h + 1)] * (
                        g_ref[k, r, h, LEFT:END]
                        - (16.5 * CG) * s_ref[k, r + 2, h, LEFT:END]
                        + (2.0 / 8.0 * CG) * near
                    )
                    total = value_r if total is None else total + value_r
                at = CCOLS * (k * CROWS + j)
                q_ref[h, at : at + CCOLS] = paired_columns(r_ref.at[k, j, h], total)
    for k in range(3):
        for h in range(2):
            for side, ref in enumerate((off_ref, on_ref)):
                for slot in range(3):
                    low, high = spill(ref, k, h, slot)
                    at = 16 + 18 * h + 9 * side + 3 * slot
                    ca_ref[k, at : at + 3] = jnp.where(even_y, high, low)
                    cb_ref[k, at : at + 3] = jnp.where(even_y, low, high)
    sums = depth_pairs(q_ref[0], q_ref[1])
    size = CROWS * CCOLS
    inverse = 4.0 / sums[3 * size :]
    for k in range(3):
        value = sums[k * size : (k + 1) * size] * inverse
        for j in range(CROWS):
            row = value[j * CCOLS : (j + 1) * CCOLS]
            gc_ref[k, j] = row
            low = row[:4]
            high = row[CCOLS - 4 :]
            ca_ref[k, 4 * j : 4 * j + 4] = jnp.where(even_y, high, low)
            cb_ref[k, 4 * j : 4 * j + 4] = jnp.where(even_y, low, high)


OWN_AT = (4, 0)
MINE_AT = (3, 2)
THEIRS_AT = (2, 3)


def window_at(k, side, window):
    return 16 * ((k * 2 + side) * 2 + window)


def spilled_at(k, side, window, slot):
    return 8 * (((k * 2 + side) * 2 + window) * 3 + slot)


def corner_residuals(d_ref, u_ref, w_ref, keep, put):
    size = d_ref.shape[1]
    for h in range(2):
        value = d_ref[h]
        u_ref[h] = (value + value) + (pltpu.roll(value, 1, 0) + pltpu.roll(value, size - 1, 0))
    sums = sums_depth(u_ref[0], u_ref[1])
    for h in range(2):
        u_ref[h] = sums[h]
    for k in range(3):
        for side in range(2):
            for window in range(2):
                for h in range(2):
                    rows = []
                    at = spilled_at(k, side, window, 0)
                    for q in range(3):
                        part = (-2.0 / 8.0) * sums_rows(
                            lambda i: u_ref[h, at + 8 * (i + 1) : at + 8 * (i + 2)], q, -1, 1
                        )
                        if q < 2:
                            part = part + 16.5 * d_ref[h, at + 8 * (q + 1) : at + 8 * (q + 2)]
                        n = (side * 2 + window) * 4 + q
                        rows.append(jnp.where(keep[window], -w_ref[n, h] * part, 0.0))
                    put(h, window_at(k, side, window), rows[0] + rows[1], rows[2])


def own_places():
    place = lax.broadcasted_iota(jnp.int32, (8, HALF), 0)
    return place >= 4, place < 4


def spilled_kernel(
    on_ref, za_ref, zb_ref, off_ref, e_ref, s_ref, near_ref, g_ref,
    w_ref, r_ref, inverse_ref, base_ref, d_ref, u_ref, q_ref,
):
    core, _, even_y, _, _ = places()
    d_ref[...] = jnp.zeros_like(d_ref)
    for h in range(2):
        for side, ref in enumerate((off_ref, on_ref)):
            for k in range(3):
                for slot in range(3):
                    theirs = spill(ref, k, h, slot)
                    for window in range(2):
                        at = spilled_at(k, side, window, slot) + THEIRS_AT[window]
                        d_ref[h, at : at + 3] = theirs[window]
            for q in range(4):
                r = q if side == 0 else ROWS - 1 - q
                halo = from_sides(
                    even_y, za_ref[3, h, 4 * r : 4 * r + 4], zb_ref[3, h, 4 * r : 4 * r + 4]
                )
                for window, first in enumerate((0, COLS - 4)):
                    n = (side * 2 + window) * 4 + q
                    at = OWN_AT[window]
                    w_ref[n, h, at : at + 4] = e_ref[
                        row_of(core, r), first : first + 4, HALF * h : HALF * (h + 1)
                    ]
                    w_ref[n, h, 4 - at : 8 - at] = halo[window]
                    if q % 2:
                        at = window_at(0, side, window) + 8 * (q // 2)
                        q_ref[h, at : at + 8] = w_ref[n - 1, h] + w_ref[n, h]

    def put(h, at, first, second):
        r_ref[h, at : at + 8] = first
        r_ref[h, at + 8 : at + 16] = second

    own = own_places()
    corner_residuals(d_ref, u_ref, w_ref, (jnp.logical_not(own[0]), jnp.logical_not(own[1])), put)
    q_ref[0, :64] = depth_pairs(q_ref[0], q_ref[1])
    visc = q_ref[0, pl.ds(0, 32, stride=2)] + q_ref[0, pl.ds(1, 32, stride=2)]
    inverse_ref[...] = jnp.where(visc > 0.0, (4.0 * CG) / jnp.where(visc > 0.0, visc, 1.0), 0.0)
    for k in range(3):
        for h in range(2):
            for r in range(ROWS):
                base_ref[k, r, h] = (
                    CA * s_ref[k, r + 2, h, LEFT:END]
                    + g_ref[k, r, h, LEFT:END]
                    + CB * sums_rows(lambda i: near_ref[k, i + 1, h], r, -1, ROWS)
                )


def corner_kernel(
    gc_ref, ca_ref, cb_ref, w_ref, s_ref, inverse_ref, out_ref, edge_ref, d_ref, u_ref, r_ref, q_ref
):
    _, _, even_y, has_low, has_high = places()
    d_ref[...] = jnp.zeros_like(d_ref)
    for h in range(2):
        for side in range(2):
            for k in range(3):
                for slot in range(3):
                    mine = corner_rows(ca_ref, cb_ref, even_y, k, h, side, slot)
                    for window in range(2):
                        at = spilled_at(k, side, window, slot) + MINE_AT[window]
                        d_ref[h, at : at + 3] = mine[window]

    def put(h, at, first, second):
        r_ref[h, at : at + 8] = first + s_ref[h, at : at + 8]
        r_ref[h, at + 8 : at + 16] = second + s_ref[h, at + 8 : at + 16]

    corner_residuals(d_ref, u_ref, w_ref, own_places(), put)
    q_ref[...] = depth_pairs(r_ref[0], r_ref[1])
    sums = q_ref[pl.ds(0, 96, stride=2)] + q_ref[pl.ds(1, 96, stride=2)]
    for k in range(3):
        value = sums[32 * k : 32 * (k + 1)] * inverse_ref[...]
        for j in range(CROWS):
            low, high = from_sides(even_y, ca_ref[k, 4 * j : 4 * j + 4], cb_ref[k, 4 * j : 4 * j + 4])
            out_ref[k, j] = jnp.concatenate([low, gc_ref[k, j], high], 0)
            side, half = (0, j) if j < 2 else (1, CROWS - 1 - j)
            for window, first in enumerate((2, CWIDE - 6)):
                at = 4 * ((side * 2 + window) * 2 + half)
                out_ref[k, j, first : first + 4] = out_ref[k, j, first : first + 4] + value[at : at + 4]
    mask = column_mask((CWIDE, HALF), CLEFT, CCOLS, has_low, has_high)
    edge_ref[...] = coarse_sweeps(out_ref[...], 0, mask)[:, 0]


def corner_rows(ca_ref, cb_ref, even_y, k, h, side, slot):
    at = 16 + 18 * h + 9 * side + 3 * slot
    return from_sides(even_y, ca_ref[k, at : at + 3], cb_ref[k, at : at + 3])


def column_mask(shape, left, width, has_low, has_high):
    place = lax.broadcasted_iota(jnp.int32, shape, 0)
    keep = jnp.logical_and(
        jnp.logical_or(place >= left, has_low), jnp.logical_or(place < left + width, has_high)
    )
    return jnp.where(keep, 1.0, 0.0)


def coarse_sweeps(rhs, last, mask):
    value = rhs
    for left in range(KC - 2, -1, -1):
        rows = min(last + 1 + left, rhs.shape[1])
        given = min(rows + 1, rhs.shape[1])
        u = value[:, :given].reshape(3 * given * CWIDE, HALF)
        size = u.shape[0]
        u = (u + u) + (pltpu.roll(u, 1, 0) + pltpu.roll(u, size - 1, 0))
        lane = lax.broadcasted_iota(jnp.int32, u.shape, 1)
        u = (u + u) + (
            jnp.where(lane == 0, 0.0, pltpu.roll(u, 1, 1))
            + jnp.where(lane == HALF - 1, 0.0, pltpu.roll(u, HALF - 1, 1))
        )
        u = u.reshape(3, given, CWIDE, HALF)
        none = jnp.zeros((3, 1, CWIDE, HALF), jnp.float32)
        before = jnp.concatenate([none, u[:, : rows - 1]], 1) if rows > 1 else none
        after = u[:, 1:given]
        if given == rows:
            after = jnp.concatenate([after, none], 1)
        near = (u[:, :rows] + u[:, :rows]) + (before + after)
        value = mask * (CA * value[:, :rows] + CB * near + rhs[:, :rows])
    return value


def coarse_kernel(own_ref, partner_ref, cor_ref, c_ref):
    _, _, _, has_low, has_high = places()
    mask = column_mask((CWIDE, HALF), CLEFT, CCOLS, has_low, has_high)
    for k in range(3):
        for r in range(CROWS):
            c_ref[k, r] = own_ref[k, r]
            c_ref[k, 2 * CROWS - 1 - r] = partner_ref[k, r]
    cor_ref[...] = coarse_sweeps(c_ref[...], CROWS, mask)


def lifted_columns(ref, value):
    mid = 3.0 * value[CLEFT : CLEFT + CCOLS]
    ref[pl.ds(0, CCOLS, stride=2)] = mid + value[CLEFT - 1 : CLEFT - 1 + CCOLS]
    ref[pl.ds(1, CCOLS, stride=2)] = mid + value[CLEFT + 1 : CLEFT + 1 + CCOLS]


def inner_kernel(base_ref, d_ref, u_ref, cor_ref, o_ref, z_ref, p_ref, l_ref):
    core, _, _, _, _ = places()
    sums, copies = lift_tables()
    sums = exact_dot(cor_ref[...].reshape(3 * (CROWS + 1) * CWIDE, HALF), sums)
    copies = exact_dot(
        cor_ref[:, :CROWS, CLEFT : CLEFT + CCOLS].reshape(3 * CROWS * CCOLS, HALF), copies
    )
    for k in range(3):
        for h in range(2):
            lanes = slice(HALF * h, HALF * (h + 1))
            for j in range(CROWS + 1):
                at = (k * (CROWS + 1) + j) * CWIDE
                z_ref[k, j, h] = sums[at : at + CWIDE, lanes]
                lifted_columns(p_ref.at[k, j, h], z_ref.at[k, j, h])
                if j < CROWS:
                    at = (k * CROWS + j) * CCOLS
                    l_ref[k, j, h, pl.ds(0, CCOLS, stride=2)] = copies[at : at + CCOLS, lanes]
                    l_ref[k, j, h, pl.ds(1, CCOLS, stride=2)] = copies[at : at + CCOLS, lanes]
            for r in range(ROWS):
                j = r // 2
                beside = j + 2 * (r % 2) - 1
                total = 3.0 * p_ref[k, j, h]
                if beside >= 0:
                    total = total + p_ref[k, beside, h]
                row = o_ref.at[k, h, row_of(core, r)]
                row[...] = base_ref[k, r, h] + (CA * l_ref[k, j, h] + CB * total)
                side, q = (0, r) if r < 3 else (1, ROWS - 1 - r)
                if q < 3:
                    for window, first in enumerate((0, COLS - 4)):
                        at = spilled_at(k, side, window, 0)
                        fix = CB * sums_rows(
                            lambda i: u_ref[h, at + 8 * (i + 1) : at + 8 * (i + 2)], q, -1, 1
                        )
                        if q < 2:
                            fix = fix + CA * d_ref[h, at + 8 * (q + 1) : at + 8 * (q + 2)]
                        fix = fix[OWN_AT[window] : OWN_AT[window] + 4]
                        row[first : first + 4] = row[first : first + 4] + fix


def edge_kernel(inner_ref, next_ref, out_hbm, o_ref, z_ref, p_ref, sems):
    core, _, _, _, _ = places()
    begin = 1 - core
    copies = []

    def copy(source, target):
        copies.append(pltpu.make_async_copy(source, target, sems.at[len(copies)]))
        copies[-1].start()

    for k in range(3):
        for h in range(2):
            rows = pl.ds(begin, ROWS - 1)
            copy(inner_ref.at[k, h, rows], out_hbm.at[k, rows, :, pl.ds(HALF * h, HALF)])
    lifted = exact_dot(next_ref[...].reshape(3 * CWIDE, HALF), lift_tables()[0])
    own = row_of(core, 0)
    for k in range(3):
        for h in range(2):
            z_ref[k, h] = lifted[k * CWIDE : (k + 1) * CWIDE, HALF * h : HALF * (h + 1)]
            lifted_columns(p_ref.at[k, h], z_ref.at[k, h])
            o_ref[k, h] = inner_ref[k, h, own] + CB * p_ref[k, h]
            copy(o_ref.at[k, h], out_hbm.at[k, own, :, pl.ds(HALF * h, HALF)])
    for started in copies:
        started.wait()


def call(kernel, outs, scratch, *args, spaces=None, out_spaces=None, aliases=None):
    spaces = spaces or [pltpu.VMEM] * len(args)
    out_spaces = out_spaces or [pltpu.VMEM] * len(outs)
    return pl.pallas_call(
        kernel,
        out_shape=[jax.ShapeDtypeStruct(o, jnp.float32) for o in outs],
        in_specs=[pl.BlockSpec(memory_space=space) for space in spaces],
        out_specs=[pl.BlockSpec(memory_space=space) for space in out_spaces],
        scratch_shapes=[pltpu.VMEM(s, jnp.float32) if isinstance(s, tuple) else s for s in scratch],
        input_output_aliases=aliases or {},
        compiler_params=pltpu.CompilerParams(vmem_limit_bytes=24 * 2**20),
    )(*args)


def swap(value, axis, parity):
    pairs = []
    for i in range(parity, lax.axis_size(axis) - 1, 2):
        pairs += [(i, i + 1), (i + 1, i)]
    return lax.ppermute(value, axis, pairs)


def body(velocity, forcing, viscosity):
    own, g, visc, off, on, za, zb = call(
        sweeps_kernel,
        [TALL, GRID, viscosity.shape, XMSG, XMSG, ZMSG, ZMSG],
        [
            GRID, forcing.shape, viscosity.shape, GRID,
            (3, ROWS + 2, 2, COLS + 8, HALF), (3, ROWS + 2, 2, WIDE + LEFT, HALF),
            pltpu.SemaphoreType.DMA((10,)),
        ],
        *(pltpu.with_memory_space_constraint(a, pltpu.HBM) for a in (velocity, forcing, viscosity)),
        spaces=[pltpu.HBM] * 3,
    )
    on = swap(on, "gx", 0)
    off = swap(off, "gx", 1)
    zb = swap(zb, "gy", 1)
    za = swap(za, "gy", 0)
    smooth, near, gc, ca, cb = call(
        residual_kernel,
        [TALL, (3, ROWS + 2, 2, COLS, HALF), (3, CROWS, CCOLS, HALF), CMSG, CMSG],
        [(4, CROWS, 2, COLS, HALF), (2, 4 * CROWS * CCOLS, HALF)],
        own, on, zb, za, off, g, visc,
        aliases={0: 0},
    )
    cb = swap(cb, "gy", 1)
    ca = swap(ca, "gy", 0)
    spilled = (2, 36 * 8, HALF)
    tile = (3, ROWS, 2, COLS, HALF)
    windows, sums, inverse, base = call(
        spilled_kernel,
        [(16, 2, 8, HALF), (2, 12 * 16, HALF), (32, HALF), tile],
        [spilled, spilled, (2, 64, HALF)],
        on, za, zb, off, visc, smooth, near, g,
    )
    rhs, edge, corner, around = call(
        corner_kernel,
        [(3, CROWS, CWIDE, HALF), (3, CWIDE, HALF), spilled, spilled],
        [(2, 12 * 16, HALF), (12 * 16, HALF)],
        gc, ca, cb, windows, sums, inverse,
    )
    beyond = swap(edge, "gx", 1)
    partner = swap(rhs, "gx", 0)
    (cor,) = call(
        coarse_kernel,
        [(3, CROWS + 1, CWIDE, HALF)],
        [(3, 2 * CROWS, CWIDE, HALF)],
        rhs, partner,
    )
    half_rows = (3, 2, COLS, HALF)
    (inner,) = call(
        inner_kernel,
        [(3, 2, ROWS, COLS, HALF)],
        [
            (3, CROWS + 1, 2, CWIDE, HALF), (3, CROWS + 1, 2, COLS, HALF), (3, CROWS, 2, COLS, HALF),
        ],
        base, corner, around, cor,
    )
    (out,) = call(
        edge_kernel,
        [velocity.shape],
        [half_rows, (3, 2, CWIDE, HALF), half_rows, pltpu.SemaphoreType.DMA((12,))],
        inner, beyond,
        out_spaces=[pltpu.HBM],
    )
    return out


def solution(mesh):
    placed = (P(None, "gx", "gy", None), P(None, "gx", "gy", None), P("gx", "gy", None))
    return jax.shard_map(
        body, mesh=mesh, in_specs=placed, out_specs=P(None, "gx", "gy", None), check_vma=False
    )
```

```python
import jax
import jax.numpy as jnp
from jax import lax
from jax.experimental import pallas as pl
from jax.experimental.pallas import tpu as pltpu
from jax.sharding import PartitionSpec as P

KC = 4
CA = 1.0 - 0.8 * 16.5 / 14.5
CB = 0.8 * 2.0 / 8.0 / 14.5
CG = 0.8 / 14.5

ROWS = 8
COLS = 32
DEPTH = 256
HALF = 128
WIDE = 48
LEFT = 8
END = LEFT + COLS
CROWS = 4
CCOLS = 16
CWIDE = 24
CLEFT = 4
XMSG = (3, 2, 112, HALF)
EDGES = 3 * COLS
ZMSG = (2, 112, HALF)
ZEDGE = 96
CMSG = (104, HALF)
CEDGE = 48
TALL = (3, ROWS + 4, 2, WIDE, HALF)
GRID = (3, ROWS, 2, WIDE, HALF)


def places():
    index_x = lax.axis_index("gx")
    index_y = lax.axis_index("gy")
    core = index_x % 2
    has_off = jnp.logical_and(index_x != 0, index_x != lax.axis_size("gx") - 1)
    even_y = index_y % 2 == 0
    return core, has_off, even_y, index_y != 0, index_y != lax.axis_size("gy") - 1


def row_of(core, row):
    return row + core * (ROWS - 1 - 2 * row)


def halves(a):
    return a[:, :HALF], a[:, HALF:]


def sums_depth(first, second):
    lane = lax.broadcasted_iota(jnp.int32, first.shape, 1)
    start = lane == 0
    stop = lane == HALF - 1
    up = pltpu.roll(first, 1, 1), pltpu.roll(second, 1, 1)
    down = pltpu.roll(first, HALF - 1, 1), pltpu.roll(second, HALF - 1, 1)
    return (
        (first + first) + (jnp.where(start, 0.0, up[0]) + jnp.where(stop, down[1], down[0])),
        (second + second) + (jnp.where(start, up[0], up[1]) + jnp.where(stop, 0.0, down[1])),
    )


def sums_columns(ref, first, size):
    mid = ref[first : first + size]
    return (mid + mid) + (ref[first - 1 : first - 1 + size] + ref[first + 1 : first + 1 + size])


def sums_rows(get, row, first, last):
    near = [get(r) for r in (row - 1, row + 1) if first <= r <= last]
    total = None
    if near:
        total = near[0] if len(near) == 1 else near[0] + near[1]
    if first <= row <= last:
        mid = get(row)
        total = mid + mid if total is None else total + (mid + mid)
    return total


def from_sides(even_y, a, b):
    return jnp.where(even_y, b, a), jnp.where(even_y, a, b)


def exact_dot(a, table):
    parts = []
    for part in range(3):
        parts.append(a.astype(jnp.bfloat16))
        if part < 2:
            a = a - parts[-1].astype(jnp.float32)
    table = table.astype(jnp.bfloat16)
    return jnp.dot(
        jnp.concatenate(parts, 1), jnp.concatenate([table] * 3, 0), preferred_element_type=jnp.float32
    )


def depth_pairs(first, second):
    fine = lax.broadcasted_iota(jnp.int32, (DEPTH, HALF), 0) // 2
    coarse = lax.broadcasted_iota(jnp.int32, (DEPTH, HALF), 1)
    return exact_dot(jnp.concatenate([first, second], 1), jnp.where(fine == coarse, 1.0, 0.0))


def lift_tables():
    coarse = lax.broadcasted_iota(jnp.int32, (HALF, DEPTH), 0)
    fine = lax.broadcasted_iota(jnp.int32, (HALF, DEPTH), 1)
    same = coarse == fine // 2
    beside = coarse == fine // 2 + 2 * (fine % 2) - 1
    copied = jnp.where(same, 1.0, 0.0)
    return jnp.where(beside, 1.0, 3.0 * copied), copied


def sweeps_kernel(
    v_hbm, f_hbm, e_hbm, own_ref, g_ref, e_ref, off_ref, on_ref,
    v_ref, f_ref, i_ref, z_ref, y_ref, w_ref, sems,
):
    def copies_v(k):
        return [
            pltpu.make_async_copy(
                v_hbm.at[k, :, :, pl.ds(HALF * h, HALF)],
                v_ref.at[k, :, h, pl.ds(LEFT, COLS)],
                sems.at[2 * k + h],
            )
            for h in range(2)
        ]

    def copy_f(k):
        return pltpu.make_async_copy(f_hbm.at[k], f_ref.at[k], sems.at[6 + k])

    copy_e = pltpu.make_async_copy(e_hbm, e_ref, sems.at[9])
    for k in range(3):
        for copy in copies_v(k):
            copy.start()
    copy_e.start()
    for k in range(3):
        copy_f(k).start()
    core, has_off, _, has_low, has_high = places()
    none = jnp.zeros((LEFT, HALF), jnp.float32)
    for k in range(3):
        for h in range(2):
            for r in range(ROWS):
                for ref in (v_ref, g_ref, z_ref):
                    ref[k, r, h, :LEFT] = none
                    ref[k, r, h, END:] = none
            for r in range(ROWS + 2):
                w_ref[k, r, h, :LEFT] = none
                w_ref[k, r, h, WIDE:] = none
    for k in range(3):
        for copy in copies_v(k):
            copy.wait()
        for r in range(ROWS):
            pair = sums_depth(*(v_ref[k, row_of(core, r), h, LEFT:END] for h in range(2)))
            for h in range(2):
                z_ref[k, r, h, LEFT:END] = pair[h]
    copy_e.wait()
    for r in range(ROWS):
        own = row_of(core, r)
        i_ref[r] = CG / e_ref[own]
    for k in range(3):
        copy_f(k).wait()
        for r in range(ROWS):
            for h, part in enumerate(halves(f_ref[k, row_of(core, r)] * i_ref[r])):
                g_ref[k, r, h, LEFT:END] = part
    for k in range(3):
        for h in range(2):
            for r in range(ROWS):
                y_ref[k, r, h] = sums_columns(z_ref.at[k, r, h], LEFT - 4, COLS + 8)
            for r in range(-1, ROWS + 1):
                value = CB * sums_rows(lambda i: y_ref[k, i, h], r, 0, ROWS - 1)
                if 0 <= r < ROWS:
                    value = value + (
                        CA * v_ref[k, row_of(core, r), h, LEFT - 4 : END + 4]
                        + g_ref[k, r, h, LEFT - 4 : END + 4]
                    )
                w_ref[k, r + 1, h, LEFT:WIDE] = value

    @pl.when(jnp.logical_not(has_off))
    def _():
        w_ref[:, 0] = jnp.zeros((3, 2, WIDE + LEFT, HALF), jnp.float32)

    @pl.when(jnp.logical_not(has_low))
    def _():
        w_ref[:, :, :, LEFT : LEFT + 4] = jnp.zeros((3, ROWS + 2, 2, 4, HALF), jnp.float32)

    @pl.when(jnp.logical_not(has_high))
    def _():
        w_ref[:, :, :, WIDE - 4 : WIDE] = jnp.zeros((3, ROWS + 2, 2, 4, HALF), jnp.float32)

    for k in range(3):
        for r in range(ROWS + 2):
            pair = sums_depth(*(sums_columns(w_ref.at[k, r, h], LEFT, COLS + 8) for h in range(2)))
            for h in range(2):
                y_ref[k, r, h] = pair[h]
    for k in range(3):
        for h in range(2):
            for r in range(-2, ROWS + 2):
                value = CB * sums_rows(lambda i: y_ref[k, i + 1, h], r, -1, ROWS)
                if -1 <= r <= ROWS:
                    value = value + CA * w_ref[k, r + 1, h, LEFT:WIDE]
                if 0 <= r < ROWS:
                    value = value + g_ref[k, r, h, LEFT - 4 : END + 4]
                own_ref[k, r + 2, h, LEFT - 4 : END + 4] = value

    @pl.when(jnp.logical_not(has_off))
    def _():
        own_ref[:, :2] = jnp.zeros((3, 2, 2, WIDE, HALF), jnp.float32)

    @pl.when(jnp.logical_not(has_low))
    def _():
        own_ref[:, :, :, LEFT - 4 : LEFT] = jnp.zeros((3, ROWS + 4, 2, 4, HALF), jnp.float32)

    @pl.when(jnp.logical_not(has_high))
    def _():
        own_ref[:, :, :, END : END + 4] = jnp.zeros((3, ROWS + 4, 2, 4, HALF), jnp.float32)

    for k in range(3):
        for h in range(2):
            for ref, rows in ((off_ref, (0, -1, -2)), (on_ref, (ROWS - 1, ROWS, ROWS + 1))):
                for slot, r in enumerate(rows):
                    ref[k, h, COLS * slot : COLS * (slot + 1)] = own_ref[k, r + 2, h, LEFT:END]
                    at = EDGES + 4 * slot
                    ref[k, h, at : at + 2] = own_ref[k, r + 2, h, LEFT - 2 : LEFT]
                    ref[k, h, at + 2 : at + 4] = own_ref[k, r + 2, h, END : END + 2]


def spill(ref, k, h, slot):
    at = EDGES + 4 * slot
    low = jnp.concatenate([ref[k, h, at : at + 2], ref[k, h, COLS * slot : COLS * slot + 1]], 0)
    high = jnp.concatenate(
        [ref[k, h, COLS * (slot + 1) - 1 : COLS * (slot + 1)], ref[k, h, at + 2 : at + 4]], 0
    )
    return low, high


def columns_kernel(own_ref, on_ref, e_ref, za_ref, zb_ref):
    core, _, even_y, _, _ = places()
    for h in range(2):
        for k in range(3):
            for r in range(-1, ROWS + 1):
                at = 32 * k + 3 * (r + 1)
                low = own_ref[k, r + 2, h, LEFT - 2 : LEFT + 1]
                high = own_ref[k, r + 2, h, END - 1 : END + 2]
                if ROWS - r < 3:
                    more = spill(on_ref, k, h, ROWS - r)
                    low = low + more[0]
                    high = high + more[1]
                za_ref[h, at : at + 3] = jnp.where(even_y, high, low)
                zb_ref[h, at : at + 3] = jnp.where(even_y, low, high)
        for r in range(4):
            at = ZEDGE + 4 * r
            low = e_ref[row_of(core, r), :4, HALF * h : HALF * (h + 1)]
            high = e_ref[row_of(core, r), COLS - 4 :, HALF * h : HALF * (h + 1)]
            za_ref[h, at : at + 4] = jnp.where(even_y, high, low)
            zb_ref[h, at : at + 4] = jnp.where(even_y, low, high)


def paired_columns(ref, value):
    ref[...] = value
    return ref[pl.ds(0, CCOLS, stride=2)] + ref[pl.ds(1, CCOLS, stride=2)]


def residual_kernel(
    _, on_ref, zb_ref, za_ref, off_ref, g_ref, e_ref, s_ref, u_ref, gc_ref, ca_ref, cb_ref, r_ref, q_ref
):
    core, _, even_y, _, _ = places()
    for k in range(3):
        for h in range(2):
            for r in range(-1, ROWS + 1):
                row = s_ref.at[k, r + 2, h]
                at = 32 * k + 3 * (r + 1)
                low, high = from_sides(even_y, za_ref[h, at : at + 3], zb_ref[h, at : at + 3])
                row[LEFT - 1 : LEFT + 2] = row[LEFT - 1 : LEFT + 2] + low
                row[END - 2 : END + 1] = row[END - 2 : END + 1] + high
                for ref, slot in ((off_ref, r + 1), (on_ref, ROWS - r)):
                    if 0 <= slot < 3:
                        at = EDGES + 4 * slot
                        row[LEFT:END] = row[LEFT:END] + ref[k, h, COLS * slot : COLS * (slot + 1)]
                        row[LEFT - 1 : LEFT] = row[LEFT - 1 : LEFT] + ref[k, h, at + 1 : at + 2]
                        row[END : END + 1] = row[END : END + 1] + ref[k, h, at + 2 : at + 3]
    for k in range(3):
        for r in range(ROWS + 2):
            pair = sums_depth(*(sums_columns(s_ref.at[k, r + 1, h], LEFT, COLS) for h in range(2)))
            for h in range(2):
                u_ref[k, r, h] = pair[h]
    for j in range(CROWS):
        value = halves(e_ref[row_of(core, 2 * j)] + e_ref[row_of(core, 2 * j + 1)])
        for h in range(2):
            at = CCOLS * (3 * CROWS + j)
            q_ref[h, at : at + CCOLS] = paired_columns(r_ref.at[3, j, h], value[h])
        for k in range(3):
            for h in range(2):
                total = None
                for r in (2 * j, 2 * j + 1):
                    near = sums_rows(lambda i: u_ref[k, i + 1, h], r, -1, ROWS)
                    value_r = e_ref[row_of(core, r), :, HALF * h : HALF * (h + 1)] * (
                        g_ref[k, r, h, LEFT:END]
                        - (16.5 * CG) * s_ref[k, r + 2, h, LEFT:END]
                        + (2.0 / 8.0 * CG) * near
                    )
                    total = value_r if total is None else total + value_r
                at = CCOLS * (k * CROWS + j)
                q_ref[h, at : at + CCOLS] = paired_columns(r_ref.at[k, j, h], total)
    for k in range(3):
        for h in range(2):
            for slot in range(3):
                low, high = spill(off_ref, k, h, slot)
                at = CEDGE + 18 * k + 9 * h + 3 * slot
                ca_ref[at : at + 3] = jnp.where(even_y, high, low)
                cb_ref[at : at + 3] = jnp.where(even_y, low, high)
    sums = depth_pairs(q_ref[0], q_ref[1])
    size = CROWS * CCOLS
    inverse = 4.0 / sums[3 * size :]
    for k in range(3):
        value = sums[k * size : (k + 1) * size] * inverse
        for j in range(CROWS):
            row = value[j * CCOLS : (j + 1) * CCOLS]
            gc_ref[k, j] = row
            low = row[:4]
            high = row[CCOLS - 4 :]
            at = CCOLS * k + 4 * j
            ca_ref[at : at + 4] = jnp.where(even_y, high, low)
            cb_ref[at : at + 4] = jnp.where(even_y, low, high)


OWN_AT = (4, 0)
MINE_AT = (3, 2)
THEIRS_AT = (2, 3)


def window_at(k, window):
    return 16 * (k * 2 + window)


def spilled_at(k, window, slot):
    return 8 * ((k * 2 + window) * 3 + slot)


def corner_residuals(d_ref, u_ref, w_ref, keep, put):
    size = d_ref.shape[1]
    for h in range(2):
        value = d_ref[h]
        u_ref[h] = (value + value) + (pltpu.roll(value, 1, 0) + pltpu.roll(value, size - 1, 0))
    sums = sums_depth(u_ref[0], u_ref[1])
    for h in range(2):
        u_ref[h] = sums[h]
    for k in range(3):
        for window in range(2):
            for h in range(2):
                rows = []
                at = spilled_at(k, window, 0)
                for q in range(3):
                    part = (-2.0 / 8.0) * sums_rows(
                        lambda i: u_ref[h, at + 8 * (i + 1) : at + 8 * (i + 2)], q, -1, 1
                    )
                    if q < 2:
                        part = part + 16.5 * d_ref[h, at + 8 * (q + 1) : at + 8 * (q + 2)]
                    rows.append(jnp.where(keep[window], -w_ref[window * 4 + q, h] * part, 0.0))
                put(h, window_at(k, window), rows[0] + rows[1], rows[2])


def own_places():
    place = lax.broadcasted_iota(jnp.int32, (8, HALF), 0)
    return place >= 4, place < 4


def spilled_kernel(
    za_ref, zb_ref, off_ref, e_ref, s_ref, near_ref, g_ref,
    w_ref, r_ref, inverse_ref, base_ref, d_ref, u_ref, q_ref,
):
    core, _, even_y, _, _ = places()
    d_ref[...] = jnp.zeros_like(d_ref)
    for h in range(2):
        for k in range(3):
            for slot in range(3):
                theirs = spill(off_ref, k, h, slot)
                for window in range(2):
                    at = spilled_at(k, window, slot) + THEIRS_AT[window]
                    d_ref[h, at : at + 3] = theirs[window]
        for r in range(4):
            at = ZEDGE + 4 * r
            halo = from_sides(even_y, za_ref[h, at : at + 4], zb_ref[h, at : at + 4])
            for window, first in enumerate((0, COLS - 4)):
                n = window * 4 + r
                at = OWN_AT[window]
                w_ref[n, h, at : at + 4] = e_ref[
                    row_of(core, r), first : first + 4, HALF * h : HALF * (h + 1)
                ]
                w_ref[n, h, 4 - at : 8 - at] = halo[window]
                if r % 2:
                    at = window_at(0, window) + 8 * (r // 2)
                    q_ref[h, at : at + 8] = w_ref[n - 1, h] + w_ref[n, h]

    def put(h, at, first, second):
        r_ref[h, at : at + 8] = first
        r_ref[h, at + 8 : at + 16] = second

    own = own_places()
    corner_residuals(d_ref, u_ref, w_ref, (jnp.logical_not(own[0]), jnp.logical_not(own[1])), put)
    q_ref[0] = depth_pairs(q_ref[0], q_ref[1])
    visc = q_ref[0, pl.ds(0, 16, stride=2)] + q_ref[0, pl.ds(1, 16, stride=2)]
    inverse_ref[...] = jnp.where(visc > 0.0, (4.0 * CG) / jnp.where(visc > 0.0, visc, 1.0), 0.0)
    for k in range(3):
        for h in range(2):
            for r in range(ROWS):
                base_ref[k, r, h] = (
                    CA * s_ref[k, r + 2, h, LEFT:END]
                    + g_ref[k, r, h, LEFT:END]
                    + CB * sums_rows(lambda i: near_ref[k, i + 1, h], r, -1, ROWS)
                )


def corner_kernel(
    gc_ref, ca_ref, cb_ref, w_ref, s_ref, inverse_ref, out_ref, edge_ref, d_ref, u_ref, r_ref, q_ref
):
    _, _, even_y, has_low, has_high = places()
    d_ref[...] = jnp.zeros_like(d_ref)
    for h in range(2):
        for k in range(3):
            for slot in range(3):
                at = CEDGE + 18 * k + 9 * h + 3 * slot
                mine = from_sides(even_y, ca_ref[at : at + 3], cb_ref[at : at + 3])
                for window in range(2):
                    at = spilled_at(k, window, slot) + MINE_AT[window]
                    d_ref[h, at : at + 3] = mine[window]

    def put(h, at, first, second):
        r_ref[h, at : at + 8] = first + s_ref[h, at : at + 8]
        r_ref[h, at + 8 : at + 16] = second + s_ref[h, at + 8 : at + 16]

    corner_residuals(d_ref, u_ref, w_ref, own_places(), put)
    q_ref[...] = depth_pairs(r_ref[0], r_ref[1])
    sums = q_ref[pl.ds(0, 48, stride=2)] + q_ref[pl.ds(1, 48, stride=2)]
    for k in range(3):
        value = sums[16 * k : 16 * (k + 1)] * inverse_ref[...]
        for j in range(CROWS):
            at = CCOLS * k + 4 * j
            low, high = from_sides(even_y, ca_ref[at : at + 4], cb_ref[at : at + 4])
            out_ref[k, j] = jnp.concatenate([low, gc_ref[k, j], high], 0)
            if j < 2:
                for window, first in enumerate((2, CWIDE - 6)):
                    at = 4 * (window * 2 + j)
                    out_ref[k, j, first : first + 4] = (
                        out_ref[k, j, first : first + 4] + value[at : at + 4]
                    )
    mask = column_mask((CWIDE, HALF), CLEFT, CCOLS, has_low, has_high)
    edge_ref[...] = coarse_sweeps(out_ref[...], 0, mask)[:, 0]


def column_mask(shape, left, width, has_low, has_high):
    place = lax.broadcasted_iota(jnp.int32, shape, 0)
    keep = jnp.logical_and(
        jnp.logical_or(place >= left, has_low), jnp.logical_or(place < left + width, has_high)
    )
    return jnp.where(keep, 1.0, 0.0)


def coarse_sweeps(rhs, last, mask):
    value = rhs
    for left in range(KC - 2, -1, -1):
        rows = min(last + 1 + left, rhs.shape[1])
        given = min(rows + 1, rhs.shape[1])
        u = value[:, :given].reshape(3 * given * CWIDE, HALF)
        size = u.shape[0]
        u = (u + u) + (pltpu.roll(u, 1, 0) + pltpu.roll(u, size - 1, 0))
        lane = lax.broadcasted_iota(jnp.int32, u.shape, 1)
        u = (u + u) + (
            jnp.where(lane == 0, 0.0, pltpu.roll(u, 1, 1))
            + jnp.where(lane == HALF - 1, 0.0, pltpu.roll(u, HALF - 1, 1))
        )
        u = u.reshape(3, given, CWIDE, HALF)
        none = jnp.zeros((3, 1, CWIDE, HALF), jnp.float32)
        before = jnp.concatenate([none, u[:, : rows - 1]], 1) if rows > 1 else none
        after = u[:, 1:given]
        if given == rows:
            after = jnp.concatenate([after, none], 1)
        near = (u[:, :rows] + u[:, :rows]) + (before + after)
        value = mask * (CA * value[:, :rows] + CB * near + rhs[:, :rows])
    return value


def coarse_kernel(own_ref, partner_ref, cor_ref, c_ref):
    _, _, _, has_low, has_high = places()
    mask = column_mask((CWIDE, HALF), CLEFT, CCOLS, has_low, has_high)
    for k in range(3):
        for r in range(CROWS):
            c_ref[k, r] = own_ref[k, r]
            c_ref[k, 2 * CROWS - 1 - r] = partner_ref[k, r]
    cor_ref[...] = coarse_sweeps(c_ref[...], CROWS, mask)


def lifted_columns(ref, value):
    mid = 3.0 * value[CLEFT : CLEFT + CCOLS]
    ref[pl.ds(0, CCOLS, stride=2)] = mid + value[CLEFT - 1 : CLEFT - 1 + CCOLS]
    ref[pl.ds(1, CCOLS, stride=2)] = mid + value[CLEFT + 1 : CLEFT + 1 + CCOLS]


def inner_kernel(base_ref, d_ref, u_ref, cor_ref, o_ref, z_ref, p_ref, l_ref):
    core, _, _, _, _ = places()
    sums, copies = lift_tables()
    sums = exact_dot(cor_ref[...].reshape(3 * (CROWS + 1) * CWIDE, HALF), sums)
    copies = exact_dot(
        cor_ref[:, :CROWS, CLEFT : CLEFT + CCOLS].reshape(3 * CROWS * CCOLS, HALF), copies
    )
    for k in range(3):
        for h in range(2):
            lanes = slice(HALF * h, HALF * (h + 1))
            for j in range(CROWS + 1):
                at = (k * (CROWS + 1) + j) * CWIDE
                z_ref[k, j, h] = sums[at : at + CWIDE, lanes]
                lifted_columns(p_ref.at[k, j, h], z_ref.at[k, j, h])
                if j < CROWS:
                    at = (k * CROWS + j) * CCOLS
                    l_ref[k, j, h, pl.ds(0, CCOLS, stride=2)] = copies[at : at + CCOLS, lanes]
                    l_ref[k, j, h, pl.ds(1, CCOLS, stride=2)] = copies[at : at + CCOLS, lanes]
            for r in range(ROWS):
                j = r // 2
                beside = j + 2 * (r % 2) - 1
                total = 3.0 * p_ref[k, j, h]
                if beside >= 0:
                    total = total + p_ref[k, beside, h]
                row = o_ref.at[k, h, row_of(core, r)]
                row[...] = base_ref[k, r, h] + (CA * l_ref[k, j, h] + CB * total)
                if r < 3:
                    for window, first in enumerate((0, COLS - 4)):
                        at = spilled_at(k, window, 0)
                        fix = CB * sums_rows(
                            lambda i: u_ref[h, at + 8 * (i + 1) : at + 8 * (i + 2)], r, -1, 1
                        )
                        if r < 2:
                            fix = fix + CA * d_ref[h, at + 8 * (r + 1) : at + 8 * (r + 2)]
                        fix = fix[OWN_AT[window] : OWN_AT[window] + 4]
                        row[first : first + 4] = row[first : first + 4] + fix


def edge_kernel(inner_ref, next_ref, out_hbm, o_ref, z_ref, p_ref, sems):
    core, _, _, _, _ = places()
    begin = 1 - core
    copies = []

    def copy(source, target):
        copies.append(pltpu.make_async_copy(source, target, sems.at[len(copies)]))
        copies[-1].start()

    for k in range(3):
        for h in range(2):
            rows = pl.ds(begin, ROWS - 1)
            copy(inner_ref.at[k, h, rows], out_hbm.at[k, rows, :, pl.ds(HALF * h, HALF)])
    lifted = exact_dot(next_ref[...].reshape(3 * CWIDE, HALF), lift_tables()[0])
    own = row_of(core, 0)
    for k in range(3):
        for h in range(2):
            z_ref[k, h] = lifted[k * CWIDE : (k + 1) * CWIDE, HALF * h : HALF * (h + 1)]
            lifted_columns(p_ref.at[k, h], z_ref.at[k, h])
            o_ref[k, h] = inner_ref[k, h, own] + CB * p_ref[k, h]
            copy(o_ref.at[k, h], out_hbm.at[k, own, :, pl.ds(HALF * h, HALF)])
    for started in copies:
        started.wait()


def call(kernel, outs, scratch, *args, spaces=None, out_spaces=None, aliases=None):
    spaces = spaces or [pltpu.VMEM] * len(args)
    out_spaces = out_spaces or [pltpu.VMEM] * len(outs)
    return pl.pallas_call(
        kernel,
        out_shape=[jax.ShapeDtypeStruct(o, jnp.float32) for o in outs],
        in_specs=[pl.BlockSpec(memory_space=space) for space in spaces],
        out_specs=[pl.BlockSpec(memory_space=space) for space in out_spaces],
        scratch_shapes=[pltpu.VMEM(s, jnp.float32) if isinstance(s, tuple) else s for s in scratch],
        input_output_aliases=aliases or {},
        compiler_params=pltpu.CompilerParams(vmem_limit_bytes=24 * 2**20),
    )(*args)


def swap(value, axis, parity):
    pairs = []
    for i in range(parity, lax.axis_size(axis) - 1, 2):
        pairs += [(i, i + 1), (i + 1, i)]
    return lax.ppermute(value, axis, pairs)


def body(velocity, forcing, viscosity):
    own, g, visc, off, on = call(
        sweeps_kernel,
        [TALL, GRID, viscosity.shape, XMSG, XMSG],
        [
            GRID, forcing.shape, viscosity.shape, GRID,
            (3, ROWS + 2, 2, COLS + 8, HALF), (3, ROWS + 2, 2, WIDE + LEFT, HALF),
            pltpu.SemaphoreType.DMA((10,)),
        ],
        *(pltpu.with_memory_space_constraint(a, pltpu.HBM) for a in (velocity, forcing, viscosity)),
        spaces=[pltpu.HBM] * 3,
    )
    on = swap(on, "gx", 0)
    off = swap(off, "gx", 1)
    za, zb = call(columns_kernel, [ZMSG, ZMSG], [], own, on, visc)
    zb = swap(zb, "gy", 1)
    za = swap(za, "gy", 0)
    smooth, near, gc, ca, cb = call(
        residual_kernel,
        [TALL, (3, ROWS + 2, 2, COLS, HALF), (3, CROWS, CCOLS, HALF), CMSG, CMSG],
        [(4, CROWS, 2, COLS, HALF), (2, 4 * CROWS * CCOLS, HALF)],
        own, on, zb, za, off, g, visc,
        aliases={0: 0},
    )
    cb = swap(cb, "gy", 1)
    ca = swap(ca, "gy", 0)
    spilled = (2, 18 * 8, HALF)
    tile = (3, ROWS, 2, COLS, HALF)
    windows, sums, inverse, base = call(
        spilled_kernel,
        [(8, 2, 8, HALF), (2, 6 * 16, HALF), (16, HALF), tile],
        [spilled, spilled, (2, 32, HALF)],
        za, zb, off, visc, smooth, near, g,
    )
    rhs, edge, corner, around = call(
        corner_kernel,
        [(3, CROWS, CWIDE, HALF), (3, CWIDE, HALF), spilled, spilled],
        [(2, 6 * 16, HALF), (6 * 16, HALF)],
        gc, ca, cb, windows, sums, inverse,
    )
    beyond = swap(edge, "gx", 1)
    partner = swap(rhs, "gx", 0)
    (cor,) = call(
        coarse_kernel,
        [(3, CROWS + 1, CWIDE, HALF)],
        [(3, 2 * CROWS, CWIDE, HALF)],
        rhs, partner,
    )
    half_rows = (3, 2, COLS, HALF)
    (inner,) = call(
        inner_kernel,
        [(3, 2, ROWS, COLS, HALF)],
        [
            (3, CROWS + 1, 2, CWIDE, HALF), (3, CROWS + 1, 2, COLS, HALF), (3, CROWS, 2, COLS, HALF),
        ],
        base, corner, around, cor,
    )
    (out,) = call(
        edge_kernel,
        [velocity.shape],
        [half_rows, (3, 2, CWIDE, HALF), half_rows, pltpu.SemaphoreType.DMA((12,))],
        inner, beyond,
        out_spaces=[pltpu.HBM],
    )
    return out


def solution(mesh):
    placed = (P(None, "gx", "gy", None), P(None, "gx", "gy", None), P("gx", "gy", None))
    return jax.shard_map(
        body, mesh=mesh, in_specs=placed, out_specs=P(None, "gx", "gy", None), check_vma=False
    )
```

```python
import jax
import jax.numpy as jnp
from jax import lax
from jax.experimental import pallas as pl
from jax.experimental.pallas import tpu as pltpu
from jax.sharding import PartitionSpec as P

KC = 4
CA = 1.0 - 0.8 * 16.5 / 14.5
CB = 0.8 * 2.0 / 8.0 / 14.5
CG = 0.8 / 14.5

ROWS = 8
COLS = 32
DEPTH = 256
HALF = 128
WIDE = 48
LEFT = 8
END = LEFT + COLS
CROWS = 4
CCOLS = 16
CWIDE = 24
CLEFT = 4
XMSG = (3, 2, 112, HALF)
EDGES = 3 * COLS
ZMSG = (2, 112, HALF)
ZEDGE = 96
CMSG = (104, HALF)
CEDGE = 48
TALL = (3, ROWS + 4, 2, WIDE, HALF)
GRID = (3, ROWS, 2, WIDE, HALF)


def places():
    index_x = lax.axis_index("gx")
    index_y = lax.axis_index("gy")
    core = index_x % 2
    has_off = jnp.logical_and(index_x != 0, index_x != lax.axis_size("gx") - 1)
    even_y = index_y % 2 == 0
    return core, has_off, even_y, index_y != 0, index_y != lax.axis_size("gy") - 1


def row_of(core, row):
    return row + core * (ROWS - 1 - 2 * row)


def halves(a):
    return a[:, :HALF], a[:, HALF:]


def sums_depth(first, second):
    lane = lax.broadcasted_iota(jnp.int32, first.shape, 1)
    start = lane == 0
    stop = lane == HALF - 1
    up = pltpu.roll(first, 1, 1), pltpu.roll(second, 1, 1)
    down = pltpu.roll(first, HALF - 1, 1), pltpu.roll(second, HALF - 1, 1)
    return (
        (first + first) + (jnp.where(start, 0.0, up[0]) + jnp.where(stop, down[1], down[0])),
        (second + second) + (jnp.where(start, up[0], up[1]) + jnp.where(stop, 0.0, down[1])),
    )


def sums_columns(ref, first, size):
    mid = ref[first : first + size]
    return (mid + mid) + (ref[first - 1 : first - 1 + size] + ref[first + 1 : first + 1 + size])


def sums_rows(get, row, first, last):
    near = [get(r) for r in (row - 1, row + 1) if first <= r <= last]
    total = None
    if near:
        total = near[0] if len(near) == 1 else near[0] + near[1]
    if first <= row <= last:
        mid = get(row)
        total = mid + mid if total is None else total + (mid + mid)
    return total


def from_sides(even_y, a, b):
    return jnp.where(even_y, b, a), jnp.where(even_y, a, b)


def exact_dot(a, table):
    parts = []
    for part in range(3):
        parts.append(a.astype(jnp.bfloat16))
        if part < 2:
            a = a - parts[-1].astype(jnp.float32)
    table = table.astype(jnp.bfloat16)
    return jnp.dot(
        jnp.concatenate(parts, 1), jnp.concatenate([table] * 3, 0), preferred_element_type=jnp.float32
    )


def depth_pairs(first, second):
    fine = lax.broadcasted_iota(jnp.int32, (DEPTH, HALF), 0) // 2
    coarse = lax.broadcasted_iota(jnp.int32, (DEPTH, HALF), 1)
    return exact_dot(jnp.concatenate([first, second], 1), jnp.where(fine == coarse, 1.0, 0.0))


def lift_tables():
    coarse = lax.broadcasted_iota(jnp.int32, (HALF, DEPTH), 0)
    fine = lax.broadcasted_iota(jnp.int32, (HALF, DEPTH), 1)
    same = coarse == fine // 2
    beside = coarse == fine // 2 + 2 * (fine % 2) - 1
    copied = jnp.where(same, 1.0, 0.0)
    return jnp.where(beside, 1.0, 3.0 * copied), copied


def sweeps_kernel(
    v_hbm, f_hbm, e_hbm, own_ref, g_ref, e_ref, off_ref, on_ref,
    v_ref, f_ref, i_ref, z_ref, y_ref, w_ref, sems,
):
    def copies_v(k):
        return [
            pltpu.make_async_copy(
                v_hbm.at[k, :, :, pl.ds(HALF * h, HALF)],
                v_ref.at[k, :, h, pl.ds(LEFT, COLS)],
                sems.at[2 * k + h],
            )
            for h in range(2)
        ]

    def copy_f(k):
        return pltpu.make_async_copy(f_hbm.at[k], f_ref.at[k], sems.at[6 + k])

    copy_e = pltpu.make_async_copy(e_hbm, e_ref, sems.at[9])
    for k in range(3):
        for copy in copies_v(k):
            copy.start()
    copy_e.start()
    for k in range(3):
        copy_f(k).start()
    core, has_off, _, has_low, has_high = places()
    none = jnp.zeros((LEFT, HALF), jnp.float32)
    for k in range(3):
        for h in range(2):
            for r in range(ROWS):
                for ref in (v_ref, g_ref, z_ref):
                    ref[k, r, h, :LEFT] = none
                    ref[k, r, h, END:] = none
            for r in range(ROWS + 2):
                w_ref[k, r, h, :LEFT] = none
                w_ref[k, r, h, WIDE:] = none
    for k in range(3):
        for copy in copies_v(k):
            copy.wait()
        for r in range(ROWS):
            pair = sums_depth(*(v_ref[k, row_of(core, r), h, LEFT:END] for h in range(2)))
            for h in range(2):
                z_ref[k, r, h, LEFT:END] = pair[h]
    copy_e.wait()
    for r in range(ROWS):
        own = row_of(core, r)
        i_ref[r] = CG / e_ref[own]
    for k in range(3):
        copy_f(k).wait()
        for r in range(ROWS):
            for h, part in enumerate(halves(f_ref[k, row_of(core, r)] * i_ref[r])):
                g_ref[k, r, h, LEFT:END] = part
    for k in range(3):
        for h in range(2):
            for r in range(ROWS):
                y_ref[k, r, h] = sums_columns(z_ref.at[k, r, h], LEFT - 4, COLS + 8)
            for r in range(-1, ROWS + 1):
                value = CB * sums_rows(lambda i: y_ref[k, i, h], r, 0, ROWS - 1)
                if 0 <= r < ROWS:
                    value = value + (
                        CA * v_ref[k, row_of(core, r), h, LEFT - 4 : END + 4]
                        + g_ref[k, r, h, LEFT - 4 : END + 4]
                    )
                w_ref[k, r + 1, h, LEFT:WIDE] = value

    @pl.when(jnp.logical_not(has_off))
    def _():
        w_ref[:, 0] = jnp.zeros((3, 2, WIDE + LEFT, HALF), jnp.float32)

    @pl.when(jnp.logical_not(has_low))
    def _():
        w_ref[:, :, :, LEFT : LEFT + 4] = jnp.zeros((3, ROWS + 2, 2, 4, HALF), jnp.float32)

    @pl.when(jnp.logical_not(has_high))
    def _():
        w_ref[:, :, :, WIDE - 4 : WIDE] = jnp.zeros((3, ROWS + 2, 2, 4, HALF), jnp.float32)

    for k in range(3):
        for r in range(ROWS + 2):
            pair = sums_depth(*(sums_columns(w_ref.at[k, r, h], LEFT, COLS + 8) for h in range(2)))
            for h in range(2):
                y_ref[k, r, h] = pair[h]
    for k in range(3):
        for h in range(2):
            for r in range(-2, ROWS + 2):
                value = CB * sums_rows(lambda i: y_ref[k, i + 1, h], r, -1, ROWS)
                if -1 <= r <= ROWS:
                    value = value + CA * w_ref[k, r + 1, h, LEFT:WIDE]
                if 0 <= r < ROWS:
                    value = value + g_ref[k, r, h, LEFT - 4 : END + 4]
                own_ref[k, r + 2, h, LEFT - 4 : END + 4] = value

    @pl.when(jnp.logical_not(has_off))
    def _():
        own_ref[:, :2] = jnp.zeros((3, 2, 2, WIDE, HALF), jnp.float32)

    @pl.when(jnp.logical_not(has_low))
    def _():
        own_ref[:, :, :, LEFT - 4 : LEFT] = jnp.zeros((3, ROWS + 4, 2, 4, HALF), jnp.float32)

    @pl.when(jnp.logical_not(has_high))
    def _():
        own_ref[:, :, :, END : END + 4] = jnp.zeros((3, ROWS + 4, 2, 4, HALF), jnp.float32)

    for k in range(3):
        for h in range(2):
            for ref, rows in ((off_ref, (0, -1, -2)), (on_ref, (ROWS - 1, ROWS, ROWS + 1))):
                for slot, r in enumerate(rows):
                    ref[k, h, COLS * slot : COLS * (slot + 1)] = own_ref[k, r + 2, h, LEFT:END]
                    at = EDGES + 4 * slot
                    ref[k, h, at : at + 2] = own_ref[k, r + 2, h, LEFT - 2 : LEFT]
                    ref[k, h, at + 2 : at + 4] = own_ref[k, r + 2, h, END : END + 2]


def spill(ref, k, h, slot):
    at = EDGES + 4 * slot
    low = jnp.concatenate([ref[k, h, at : at + 2], ref[k, h, COLS * slot : COLS * slot + 1]], 0)
    high = jnp.concatenate(
        [ref[k, h, COLS * (slot + 1) - 1 : COLS * (slot + 1)], ref[k, h, at + 2 : at + 4]], 0
    )
    return low, high


def add_row(s_ref, ref, k, h, r, slot):
    row = s_ref.at[k, r + 2, h]
    at = EDGES + 4 * slot
    row[LEFT:END] = row[LEFT:END] + ref[k, h, COLS * slot : COLS * (slot + 1)]
    row[LEFT - 1 : LEFT] = row[LEFT - 1 : LEFT] + ref[k, h, at + 1 : at + 2]
    row[END : END + 1] = row[END : END + 1] + ref[k, h, at + 2 : at + 3]


def columns_kernel(own_ref, on_ref, e_ref, za_ref, zb_ref):
    core, _, even_y, _, _ = places()
    for h in range(2):
        for k in range(3):
            for r in range(-1, ROWS + 1):
                at = 32 * k + 3 * (r + 1)
                low = own_ref[k, r + 2, h, LEFT - 2 : LEFT + 1]
                high = own_ref[k, r + 2, h, END - 1 : END + 2]
                if ROWS - r < 3:
                    more = spill(on_ref, k, h, ROWS - r)
                    low = low + more[0]
                    high = high + more[1]
                za_ref[h, at : at + 3] = jnp.where(even_y, high, low)
                zb_ref[h, at : at + 3] = jnp.where(even_y, low, high)
        for r in range(4):
            at = ZEDGE + 4 * r
            low = e_ref[row_of(core, r), :4, HALF * h : HALF * (h + 1)]
            high = e_ref[row_of(core, r), COLS - 4 :, HALF * h : HALF * (h + 1)]
            za_ref[h, at : at + 4] = jnp.where(even_y, high, low)
            zb_ref[h, at : at + 4] = jnp.where(even_y, low, high)


def paired_columns(ref, value):
    ref[...] = value
    return ref[pl.ds(0, CCOLS, stride=2)] + ref[pl.ds(1, CCOLS, stride=2)]


def waiting_kernel(_, on_ref, e_ref, __, s_ref, inverse_ref, r_ref, q_ref):
    core, _, _, _, _ = places()
    for j in range(CROWS):
        value = halves(e_ref[row_of(core, 2 * j)] + e_ref[row_of(core, 2 * j + 1)])
        for h in range(2):
            q_ref[h, CCOLS * j : CCOLS * (j + 1)] = paired_columns(r_ref.at[j, h], value[h])
    inverse_ref[...] = 4.0 / depth_pairs(q_ref[0], q_ref[1])
    for k in range(3):
        for h in range(2):
            for slot in range(3):
                add_row(s_ref, on_ref, k, h, ROWS - slot, slot)


def residual_kernel(
    _, zb_ref, za_ref, off_ref, g_ref, e_ref, inverse_ref, s_ref, u_ref, gc_ref, ca_ref, cb_ref, r_ref, q_ref
):
    core, _, even_y, _, _ = places()
    for k in range(3):
        for h in range(2):
            for r in range(-1, ROWS + 1):
                row = s_ref.at[k, r + 2, h]
                at = 32 * k + 3 * (r + 1)
                low, high = from_sides(even_y, za_ref[h, at : at + 3], zb_ref[h, at : at + 3])
                row[LEFT - 1 : LEFT + 2] = row[LEFT - 1 : LEFT + 2] + low
                row[END - 2 : END + 1] = row[END - 2 : END + 1] + high
                if r < 2:
                    add_row(s_ref, off_ref, k, h, r, r + 1)
    for k in range(3):
        for r in range(ROWS + 2):
            pair = sums_depth(*(sums_columns(s_ref.at[k, r + 1, h], LEFT, COLS) for h in range(2)))
            for h in range(2):
                u_ref[k, r, h] = pair[h]
    for j in range(CROWS):
        for k in range(3):
            for h in range(2):
                total = None
                for r in (2 * j, 2 * j + 1):
                    near = sums_rows(lambda i: u_ref[k, i + 1, h], r, -1, ROWS)
                    value_r = e_ref[row_of(core, r), :, HALF * h : HALF * (h + 1)] * (
                        g_ref[k, r, h, LEFT:END]
                        - (16.5 * CG) * s_ref[k, r + 2, h, LEFT:END]
                        + (2.0 / 8.0 * CG) * near
                    )
                    total = value_r if total is None else total + value_r
                at = CCOLS * (k * CROWS + j)
                q_ref[h, at : at + CCOLS] = paired_columns(r_ref.at[k, j, h], total)
    for k in range(3):
        for h in range(2):
            for slot in range(3):
                low, high = spill(off_ref, k, h, slot)
                at = CEDGE + 18 * k + 9 * h + 3 * slot
                ca_ref[at : at + 3] = jnp.where(even_y, high, low)
                cb_ref[at : at + 3] = jnp.where(even_y, low, high)
    sums = depth_pairs(q_ref[0], q_ref[1])
    size = CROWS * CCOLS
    for k in range(3):
        value = sums[k * size : (k + 1) * size] * inverse_ref[...]
        for j in range(CROWS):
            row = value[j * CCOLS : (j + 1) * CCOLS]
            gc_ref[k, j] = row
            low = row[:4]
            high = row[CCOLS - 4 :]
            at = CCOLS * k + 4 * j
            ca_ref[at : at + 4] = jnp.where(even_y, high, low)
            cb_ref[at : at + 4] = jnp.where(even_y, low, high)


OWN_AT = (4, 0)
MINE_AT = (3, 2)
THEIRS_AT = (2, 3)


def window_at(k, window):
    return 16 * (k * 2 + window)


def spilled_at(k, window, slot):
    return 8 * ((k * 2 + window) * 3 + slot)


def corner_residuals(d_ref, u_ref, w_ref, keep, put):
    size = d_ref.shape[1]
    for h in range(2):
        value = d_ref[h]
        u_ref[h] = (value + value) + (pltpu.roll(value, 1, 0) + pltpu.roll(value, size - 1, 0))
    sums = sums_depth(u_ref[0], u_ref[1])
    for h in range(2):
        u_ref[h] = sums[h]
    for k in range(3):
        for window in range(2):
            for h in range(2):
                rows = []
                at = spilled_at(k, window, 0)
                for q in range(3):
                    part = (-2.0 / 8.0) * sums_rows(
                        lambda i: u_ref[h, at + 8 * (i + 1) : at + 8 * (i + 2)], q, -1, 1
                    )
                    if q < 2:
                        part = part + 16.5 * d_ref[h, at + 8 * (q + 1) : at + 8 * (q + 2)]
                    rows.append(jnp.where(keep[window], -w_ref[window * 4 + q, h] * part, 0.0))
                put(h, window_at(k, window), rows[0] + rows[1], rows[2])


def own_places():
    place = lax.broadcasted_iota(jnp.int32, (8, HALF), 0)
    return place >= 4, place < 4


def spilled_kernel(
    za_ref, zb_ref, off_ref, e_ref, s_ref, near_ref, g_ref,
    w_ref, r_ref, inverse_ref, base_ref, d_ref, u_ref, q_ref,
):
    core, _, even_y, _, _ = places()
    d_ref[...] = jnp.zeros_like(d_ref)
    for h in range(2):
        for k in range(3):
            for slot in range(3):
                theirs = spill(off_ref, k, h, slot)
                for window in range(2):
                    at = spilled_at(k, window, slot) + THEIRS_AT[window]
                    d_ref[h, at : at + 3] = theirs[window]
        for r in range(4):
            at = ZEDGE + 4 * r
            halo = from_sides(even_y, za_ref[h, at : at + 4], zb_ref[h, at : at + 4])
            for window, first in enumerate((0, COLS - 4)):
                n = window * 4 + r
                at = OWN_AT[window]
                w_ref[n, h, at : at + 4] = e_ref[
                    row_of(core, r), first : first + 4, HALF * h : HALF * (h + 1)
                ]
                w_ref[n, h, 4 - at : 8 - at] = halo[window]
                if r % 2:
                    at = window_at(0, window) + 8 * (r // 2)
                    q_ref[h, at : at + 8] = w_ref[n - 1, h] + w_ref[n, h]

    def put(h, at, first, second):
        r_ref[h, at : at + 8] = first
        r_ref[h, at + 8 : at + 16] = second

    own = own_places()
    corner_residuals(d_ref, u_ref, w_ref, (jnp.logical_not(own[0]), jnp.logical_not(own[1])), put)
    q_ref[0] = depth_pairs(q_ref[0], q_ref[1])
    visc = q_ref[0, pl.ds(0, 16, stride=2)] + q_ref[0, pl.ds(1, 16, stride=2)]
    inverse_ref[...] = jnp.where(visc > 0.0, (4.0 * CG) / jnp.where(visc > 0.0, visc, 1.0), 0.0)
    for k in range(3):
        for h in range(2):
            for r in range(ROWS):
                base_ref[k, r, h] = (
                    CA * s_ref[k, r + 2, h, LEFT:END]
                    + g_ref[k, r, h, LEFT:END]
                    + CB * sums_rows(lambda i: near_ref[k, i + 1, h], r, -1, ROWS)
                )


def corner_kernel(
    gc_ref, ca_ref, cb_ref, w_ref, s_ref, inverse_ref, out_ref, edge_ref, d_ref, u_ref, r_ref, q_ref
):
    _, _, even_y, has_low, has_high = places()
    d_ref[...] = jnp.zeros_like(d_ref)
    for h in range(2):
        for k in range(3):
            for slot in range(3):
                at = CEDGE + 18 * k + 9 * h + 3 * slot
                mine = from_sides(even_y, ca_ref[at : at + 3], cb_ref[at : at + 3])
                for window in range(2):
                    at = spilled_at(k, window, slot) + MINE_AT[window]
                    d_ref[h, at : at + 3] = mine[window]

    def put(h, at, first, second):
        r_ref[h, at : at + 8] = first + s_ref[h, at : at + 8]
        r_ref[h, at + 8 : at + 16] = second + s_ref[h, at + 8 : at + 16]

    corner_residuals(d_ref, u_ref, w_ref, own_places(), put)
    q_ref[...] = depth_pairs(r_ref[0], r_ref[1])
    sums = q_ref[pl.ds(0, 48, stride=2)] + q_ref[pl.ds(1, 48, stride=2)]
    for k in range(3):
        value = sums[16 * k : 16 * (k + 1)] * inverse_ref[...]
        for j in range(CROWS):
            at = CCOLS * k + 4 * j
            low, high = from_sides(even_y, ca_ref[at : at + 4], cb_ref[at : at + 4])
            out_ref[k, j] = jnp.concatenate([low, gc_ref[k, j], high], 0)
            if j < 2:
                for window, first in enumerate((2, CWIDE - 6)):
                    at = 4 * (window * 2 + j)
                    out_ref[k, j, first : first + 4] = (
                        out_ref[k, j, first : first + 4] + value[at : at + 4]
                    )
    mask = column_mask((CWIDE, HALF), CLEFT, CCOLS, has_low, has_high)
    edge_ref[...] = coarse_sweeps(out_ref[...], 0, mask)[:, 0]


def column_mask(shape, left, width, has_low, has_high):
    place = lax.broadcasted_iota(jnp.int32, shape, 0)
    keep = jnp.logical_and(
        jnp.logical_or(place >= left, has_low), jnp.logical_or(place < left + width, has_high)
    )
    return jnp.where(keep, 1.0, 0.0)


def coarse_sweeps(rhs, last, mask):
    value = rhs
    for left in range(KC - 2, -1, -1):
        rows = min(last + 1 + left, rhs.shape[1])
        given = min(rows + 1, rhs.shape[1])
        u = value[:, :given].reshape(3 * given * CWIDE, HALF)
        size = u.shape[0]
        u = (u + u) + (pltpu.roll(u, 1, 0) + pltpu.roll(u, size - 1, 0))
        lane = lax.broadcasted_iota(jnp.int32, u.shape, 1)
        u = (u + u) + (
            jnp.where(lane == 0, 0.0, pltpu.roll(u, 1, 1))
            + jnp.where(lane == HALF - 1, 0.0, pltpu.roll(u, HALF - 1, 1))
        )
        u = u.reshape(3, given, CWIDE, HALF)
        none = jnp.zeros((3, 1, CWIDE, HALF), jnp.float32)
        before = jnp.concatenate([none, u[:, : rows - 1]], 1) if rows > 1 else none
        after = u[:, 1:given]
        if given == rows:
            after = jnp.concatenate([after, none], 1)
        near = (u[:, :rows] + u[:, :rows]) + (before + after)
        value = mask * (CA * value[:, :rows] + CB * near + rhs[:, :rows])
    return value


def coarse_kernel(own_ref, partner_ref, cor_ref, c_ref):
    _, _, _, has_low, has_high = places()
    mask = column_mask((CWIDE, HALF), CLEFT, CCOLS, has_low, has_high)
    for k in range(3):
        for r in range(CROWS):
            c_ref[k, r] = own_ref[k, r]
            c_ref[k, 2 * CROWS - 1 - r] = partner_ref[k, r]
    cor_ref[...] = coarse_sweeps(c_ref[...], CROWS, mask)


def lifted_columns(ref, value):
    mid = 3.0 * value[CLEFT : CLEFT + CCOLS]
    ref[pl.ds(0, CCOLS, stride=2)] = mid + value[CLEFT - 1 : CLEFT - 1 + CCOLS]
    ref[pl.ds(1, CCOLS, stride=2)] = mid + value[CLEFT + 1 : CLEFT + 1 + CCOLS]


def inner_kernel(base_ref, d_ref, u_ref, cor_ref, o_ref, z_ref, p_ref, l_ref):
    core, _, _, _, _ = places()
    sums, copies = lift_tables()
    sums = exact_dot(cor_ref[...].reshape(3 * (CROWS + 1) * CWIDE, HALF), sums)
    copies = exact_dot(
        cor_ref[:, :CROWS, CLEFT : CLEFT + CCOLS].reshape(3 * CROWS * CCOLS, HALF), copies
    )
    for k in range(3):
        for h in range(2):
            lanes = slice(HALF * h, HALF * (h + 1))
            for j in range(CROWS + 1):
                at = (k * (CROWS + 1) + j) * CWIDE
                z_ref[k, j, h] = sums[at : at + CWIDE, lanes]
                lifted_columns(p_ref.at[k, j, h], z_ref.at[k, j, h])
                if j < CROWS:
                    at = (k * CROWS + j) * CCOLS
                    l_ref[k, j, h, pl.ds(0, CCOLS, stride=2)] = copies[at : at + CCOLS, lanes]
                    l_ref[k, j, h, pl.ds(1, CCOLS, stride=2)] = copies[at : at + CCOLS, lanes]
            for r in range(ROWS):
                j = r // 2
                beside = j + 2 * (r % 2) - 1
                total = 3.0 * p_ref[k, j, h]
                if beside >= 0:
                    total = total + p_ref[k, beside, h]
                row = o_ref.at[k, h, row_of(core, r)]
                row[...] = base_ref[k, r, h] + (CA * l_ref[k, j, h] + CB * total)
                if r < 3:
                    for window, first in enumerate((0, COLS - 4)):
                        at = spilled_at(k, window, 0)
                        fix = CB * sums_rows(
                            lambda i: u_ref[h, at + 8 * (i + 1) : at + 8 * (i + 2)], r, -1, 1
                        )
                        if r < 2:
                            fix = fix + CA * d_ref[h, at + 8 * (r + 1) : at + 8 * (r + 2)]
                        fix = fix[OWN_AT[window] : OWN_AT[window] + 4]
                        row[first : first + 4] = row[first : first + 4] + fix


def edge_kernel(inner_ref, next_ref, out_hbm, o_ref, z_ref, p_ref, sems):
    core, _, _, _, _ = places()
    begin = 1 - core
    copies = []

    def copy(source, target):
        copies.append(pltpu.make_async_copy(source, target, sems.at[len(copies)]))
        copies[-1].start()

    for k in range(3):
        for h in range(2):
            rows = pl.ds(begin, ROWS - 1)
            copy(inner_ref.at[k, h, rows], out_hbm.at[k, rows, :, pl.ds(HALF * h, HALF)])
    lifted = exact_dot(next_ref[...].reshape(3 * CWIDE, HALF), lift_tables()[0])
    own = row_of(core, 0)
    for k in range(3):
        for h in range(2):
            z_ref[k, h] = lifted[k * CWIDE : (k + 1) * CWIDE, HALF * h : HALF * (h + 1)]
            lifted_columns(p_ref.at[k, h], z_ref.at[k, h])
            o_ref[k, h] = inner_ref[k, h, own] + CB * p_ref[k, h]
            copy(o_ref.at[k, h], out_hbm.at[k, own, :, pl.ds(HALF * h, HALF)])
    for started in copies:
        started.wait()


def call(kernel, outs, scratch, *args, spaces=None, out_spaces=None, aliases=None):
    spaces = spaces or [pltpu.VMEM] * len(args)
    out_spaces = out_spaces or [pltpu.VMEM] * len(outs)
    return pl.pallas_call(
        kernel,
        out_shape=[jax.ShapeDtypeStruct(o, jnp.float32) for o in outs],
        in_specs=[pl.BlockSpec(memory_space=space) for space in spaces],
        out_specs=[pl.BlockSpec(memory_space=space) for space in out_spaces],
        scratch_shapes=[pltpu.VMEM(s, jnp.float32) if isinstance(s, tuple) else s for s in scratch],
        input_output_aliases=aliases or {},
        compiler_params=pltpu.CompilerParams(vmem_limit_bytes=24 * 2**20),
    )(*args)


def swap(value, axis, parity):
    pairs = []
    for i in range(parity, lax.axis_size(axis) - 1, 2):
        pairs += [(i, i + 1), (i + 1, i)]
    return lax.ppermute(value, axis, pairs)


def body(velocity, forcing, viscosity):
    own, g, visc, off, on = call(
        sweeps_kernel,
        [TALL, GRID, viscosity.shape, XMSG, XMSG],
        [
            GRID, forcing.shape, viscosity.shape, GRID,
            (3, ROWS + 2, 2, COLS + 8, HALF), (3, ROWS + 2, 2, WIDE + LEFT, HALF),
            pltpu.SemaphoreType.DMA((10,)),
        ],
        *(pltpu.with_memory_space_constraint(a, pltpu.HBM) for a in (velocity, forcing, viscosity)),
        spaces=[pltpu.HBM] * 3,
    )
    on = swap(on, "gx", 0)
    off = swap(off, "gx", 1)
    za, zb = call(columns_kernel, [ZMSG, ZMSG], [], own, on, visc)
    coarse_cells = CROWS * CCOLS
    own, scale = call(
        waiting_kernel,
        [TALL, (coarse_cells, HALF)],
        [(CROWS, 2, COLS, HALF), (2, coarse_cells, HALF)],
        own, on, visc, zb,
        aliases={0: 0},
    )
    zb = swap(zb, "gy", 1)
    za = swap(za, "gy", 0)
    smooth, near, gc, ca, cb = call(
        residual_kernel,
        [TALL, (3, ROWS + 2, 2, COLS, HALF), (3, CROWS, CCOLS, HALF), CMSG, CMSG],
        [(3, CROWS, 2, COLS, HALF), (2, 3 * CROWS * CCOLS, HALF)],
        own, zb, za, off, g, visc, scale,
        aliases={0: 0},
    )
    cb = swap(cb, "gy", 1)
    ca = swap(ca, "gy", 0)
    spilled = (2, 18 * 8, HALF)
    tile = (3, ROWS, 2, COLS, HALF)
    windows, sums, inverse, base = call(
        spilled_kernel,
        [(8, 2, 8, HALF), (2, 6 * 16, HALF), (16, HALF), tile],
        [spilled, spilled, (2, 32, HALF)],
        za, zb, off, visc, smooth, near, g,
    )
    rhs, edge, corner, around = call(
        corner_kernel,
        [(3, CROWS, CWIDE, HALF), (3, CWIDE, HALF), spilled, spilled],
        [(2, 6 * 16, HALF), (6 * 16, HALF)],
        gc, ca, cb, windows, sums, inverse,
    )
    beyond = swap(edge, "gx", 1)
    partner = swap(rhs, "gx", 0)
    (cor,) = call(
        coarse_kernel,
        [(3, CROWS + 1, CWIDE, HALF)],
        [(3, 2 * CROWS, CWIDE, HALF)],
        rhs, partner,
    )
    half_rows = (3, 2, COLS, HALF)
    (inner,) = call(
        inner_kernel,
        [(3, 2, ROWS, COLS, HALF)],
        [
            (3, CROWS + 1, 2, CWIDE, HALF), (3, CROWS + 1, 2, COLS, HALF), (3, CROWS, 2, COLS, HALF),
        ],
        base, corner, around, cor,
    )
    (out,) = call(
        edge_kernel,
        [velocity.shape],
        [half_rows, (3, 2, CWIDE, HALF), half_rows, pltpu.SemaphoreType.DMA((12,))],
        inner, beyond,
        out_spaces=[pltpu.HBM],
    )
    return out


def solution(mesh):
    placed = (P(None, "gx", "gy", None), P(None, "gx", "gy", None), P("gx", "gy", None))
    return jax.shard_map(
        body, mesh=mesh, in_specs=placed, out_specs=P(None, "gx", "gy", None), check_vma=False
    )
```

```python
import jax
import jax.numpy as jnp
from jax import lax
from jax.experimental import pallas as pl
from jax.experimental.pallas import tpu as pltpu
from jax.sharding import PartitionSpec as P

KC = 4
CA = 1.0 - 0.8 * 16.5 / 14.5
CB = 0.8 * 2.0 / 8.0 / 14.5
CG = 0.8 / 14.5

ROWS = 8
COLS = 32
DEPTH = 256
HALF = 128
WIDE = 48
LEFT = 8
END = LEFT + COLS
CROWS = 4
CCOLS = 16
CWIDE = 24
CLEFT = 4
XMSG = (3, 2, 112, HALF)
EDGES = 3 * COLS
ZMSG = (2, 112, HALF)
ZEDGE = 96
CMSG = (104, HALF)
CEDGE = 48
TALL = (3, ROWS + 4, 2, WIDE, HALF)
GRID = (3, ROWS, 2, WIDE, HALF)


def places():
    index_x = lax.axis_index("gx")
    index_y = lax.axis_index("gy")
    core = index_x % 2
    has_off = jnp.logical_and(index_x != 0, index_x != lax.axis_size("gx") - 1)
    even_y = index_y % 2 == 0
    return core, has_off, even_y, index_y != 0, index_y != lax.axis_size("gy") - 1


def row_of(core, row):
    return row + core * (ROWS - 1 - 2 * row)


def halves(a):
    return a[:, :HALF], a[:, HALF:]


def sums_depth(first, second):
    lane = lax.broadcasted_iota(jnp.int32, first.shape, 1)
    start = lane == 0
    stop = lane == HALF - 1
    up = pltpu.roll(first, 1, 1), pltpu.roll(second, 1, 1)
    down = pltpu.roll(first, HALF - 1, 1), pltpu.roll(second, HALF - 1, 1)
    return (
        (first + first) + (jnp.where(start, 0.0, up[0]) + jnp.where(stop, down[1], down[0])),
        (second + second) + (jnp.where(start, up[0], up[1]) + jnp.where(stop, 0.0, down[1])),
    )


def sums_columns(ref, first, size):
    mid = ref[first : first + size]
    return (mid + mid) + (ref[first - 1 : first - 1 + size] + ref[first + 1 : first + 1 + size])


def sums_rows(get, row, first, last):
    near = [get(r) for r in (row - 1, row + 1) if first <= r <= last]
    total = None
    if near:
        total = near[0] if len(near) == 1 else near[0] + near[1]
    if first <= row <= last:
        mid = get(row)
        total = mid + mid if total is None else total + (mid + mid)
    return total


def from_sides(even_y, a, b):
    return jnp.where(even_y, b, a), jnp.where(even_y, a, b)


def exact_dot(a, table):
    parts = []
    for part in range(3):
        parts.append(a.astype(jnp.bfloat16))
        if part < 2:
            a = a - parts[-1].astype(jnp.float32)
    table = table.astype(jnp.bfloat16)
    return jnp.dot(
        jnp.concatenate(parts, 1), jnp.concatenate([table] * 3, 0), preferred_element_type=jnp.float32
    )


def depth_pairs(first, second):
    fine = lax.broadcasted_iota(jnp.int32, (DEPTH, HALF), 0) // 2
    coarse = lax.broadcasted_iota(jnp.int32, (DEPTH, HALF), 1)
    return exact_dot(jnp.concatenate([first, second], 1), jnp.where(fine == coarse, 1.0, 0.0))


def lift_tables():
    coarse = lax.broadcasted_iota(jnp.int32, (HALF, DEPTH), 0)
    fine = lax.broadcasted_iota(jnp.int32, (HALF, DEPTH), 1)
    same = coarse == fine // 2
    beside = coarse == fine // 2 + 2 * (fine % 2) - 1
    copied = jnp.where(same, 1.0, 0.0)
    return jnp.where(beside, 1.0, 3.0 * copied), copied


def sweeps_kernel(
    v_hbm, f_hbm, e_hbm, own_ref, g_ref, e_ref, off_ref, on_ref,
    v_ref, f_ref, i_ref, z_ref, y_ref, w_ref, sems,
):
    def copies_v(k):
        return [
            pltpu.make_async_copy(
                v_hbm.at[k, :, :, pl.ds(HALF * h, HALF)],
                v_ref.at[k, :, h, pl.ds(LEFT, COLS)],
                sems.at[2 * k + h],
            )
            for h in range(2)
        ]

    def copy_f(k):
        return pltpu.make_async_copy(f_hbm.at[k], f_ref.at[k], sems.at[6 + k])

    copy_e = pltpu.make_async_copy(e_hbm, e_ref, sems.at[9])
    for k in range(3):
        for copy in copies_v(k):
            copy.start()
    copy_e.start()
    for k in range(3):
        copy_f(k).start()
    core, has_off, _, has_low, has_high = places()
    none = jnp.zeros((LEFT, HALF), jnp.float32)
    for k in range(3):
        for h in range(2):
            for r in range(ROWS):
                for ref in (v_ref, g_ref, z_ref):
                    ref[k, r, h, :LEFT] = none
                    ref[k, r, h, END:] = none
            for r in range(ROWS + 2):
                w_ref[k, r, h, :LEFT] = none
                w_ref[k, r, h, WIDE:] = none
    for k in range(3):
        for copy in copies_v(k):
            copy.wait()
        for r in range(ROWS):
            pair = sums_depth(*(v_ref[k, row_of(core, r), h, LEFT:END] for h in range(2)))
            for h in range(2):
                z_ref[k, r, h, LEFT:END] = pair[h]
    copy_e.wait()
    for r in range(ROWS):
        own = row_of(core, r)
        i_ref[r] = CG / e_ref[own]
    for k in range(3):
        copy_f(k).wait()
        for r in range(ROWS):
            for h, part in enumerate(halves(f_ref[k, row_of(core, r)] * i_ref[r])):
                g_ref[k, r, h, LEFT:END] = part
    for k in range(3):
        for h in range(2):
            for r in range(ROWS):
                y_ref[k, r, h] = sums_columns(z_ref.at[k, r, h], LEFT - 4, COLS + 8)
            for r in range(-1, ROWS + 1):
                value = CB * sums_rows(lambda i: y_ref[k, i, h], r, 0, ROWS - 1)
                if 0 <= r < ROWS:
                    value = value + (
                        CA * v_ref[k, row_of(core, r), h, LEFT - 4 : END + 4]
                        + g_ref[k, r, h, LEFT - 4 : END + 4]
                    )
                w_ref[k, r + 1, h, LEFT:WIDE] = value

    @pl.when(jnp.logical_not(has_off))
    def _():
        w_ref[:, 0] = jnp.zeros((3, 2, WIDE + LEFT, HALF), jnp.float32)

    @pl.when(jnp.logical_not(has_low))
    def _():
        w_ref[:, :, :, LEFT : LEFT + 4] = jnp.zeros((3, ROWS + 2, 2, 4, HALF), jnp.float32)

    @pl.when(jnp.logical_not(has_high))
    def _():
        w_ref[:, :, :, WIDE - 4 : WIDE] = jnp.zeros((3, ROWS + 2, 2, 4, HALF), jnp.float32)

    for k in range(3):
        for r in range(ROWS + 2):
            pair = sums_depth(*(sums_columns(w_ref.at[k, r, h], LEFT, COLS + 8) for h in range(2)))
            for h in range(2):
                y_ref[k, r, h] = pair[h]
    for k in range(3):
        for h in range(2):
            for r in range(-2, ROWS + 2):
                value = CB * sums_rows(lambda i: y_ref[k, i + 1, h], r, -1, ROWS)
                if -1 <= r <= ROWS:
                    value = value + CA * w_ref[k, r + 1, h, LEFT:WIDE]
                if 0 <= r < ROWS:
                    value = value + g_ref[k, r, h, LEFT - 4 : END + 4]
                own_ref[k, r + 2, h, LEFT - 4 : END + 4] = value

    @pl.when(jnp.logical_not(has_off))
    def _():
        own_ref[:, :2] = jnp.zeros((3, 2, 2, WIDE, HALF), jnp.float32)

    @pl.when(jnp.logical_not(has_low))
    def _():
        own_ref[:, :, :, LEFT - 4 : LEFT] = jnp.zeros((3, ROWS + 4, 2, 4, HALF), jnp.float32)

    @pl.when(jnp.logical_not(has_high))
    def _():
        own_ref[:, :, :, END : END + 4] = jnp.zeros((3, ROWS + 4, 2, 4, HALF), jnp.float32)

    for k in range(3):
        for h in range(2):
            for ref, rows in ((off_ref, (0, -1, -2)), (on_ref, (ROWS - 1, ROWS, ROWS + 1))):
                for slot, r in enumerate(rows):
                    ref[k, h, COLS * slot : COLS * (slot + 1)] = own_ref[k, r + 2, h, LEFT:END]
                    at = EDGES + 4 * slot
                    ref[k, h, at : at + 2] = own_ref[k, r + 2, h, LEFT - 2 : LEFT]
                    ref[k, h, at + 2 : at + 4] = own_ref[k, r + 2, h, END : END + 2]


def spill(ref, k, h, slot):
    at = EDGES + 4 * slot
    low = jnp.concatenate([ref[k, h, at : at + 2], ref[k, h, COLS * slot : COLS * slot + 1]], 0)
    high = jnp.concatenate(
        [ref[k, h, COLS * (slot + 1) - 1 : COLS * (slot + 1)], ref[k, h, at + 2 : at + 4]], 0
    )
    return low, high


def add_row(s_ref, ref, k, h, r, slot):
    row = s_ref.at[k, r + 2, h]
    at = EDGES + 4 * slot
    row[LEFT:END] = row[LEFT:END] + ref[k, h, COLS * slot : COLS * (slot + 1)]
    row[LEFT - 1 : LEFT] = row[LEFT - 1 : LEFT] + ref[k, h, at + 1 : at + 2]
    row[END : END + 1] = row[END : END + 1] + ref[k, h, at + 2 : at + 3]


def columns_kernel(own_ref, on_ref, e_ref, za_ref, zb_ref):
    core, _, even_y, _, _ = places()
    for h in range(2):
        for k in range(3):
            for r in range(-1, ROWS + 1):
                at = 32 * k + 3 * (r + 1)
                low = own_ref[k, r + 2, h, LEFT - 2 : LEFT + 1]
                high = own_ref[k, r + 2, h, END - 1 : END + 2]
                if ROWS - r < 3:
                    more = spill(on_ref, k, h, ROWS - r)
                    low = low + more[0]
                    high = high + more[1]
                za_ref[h, at : at + 3] = jnp.where(even_y, high, low)
                zb_ref[h, at : at + 3] = jnp.where(even_y, low, high)
        for r in range(4):
            at = ZEDGE + 4 * r
            low = e_ref[row_of(core, r), :4, HALF * h : HALF * (h + 1)]
            high = e_ref[row_of(core, r), COLS - 4 :, HALF * h : HALF * (h + 1)]
            za_ref[h, at : at + 4] = jnp.where(even_y, high, low)
            zb_ref[h, at : at + 4] = jnp.where(even_y, low, high)


def paired_columns(ref, value):
    ref[...] = value
    return ref[pl.ds(0, CCOLS, stride=2)] + ref[pl.ds(1, CCOLS, stride=2)]


def waiting_kernel(_, on_ref, e_ref, __, s_ref, inverse_ref, r_ref, q_ref):
    core, _, _, _, _ = places()
    for j in range(CROWS):
        value = halves(e_ref[row_of(core, 2 * j)] + e_ref[row_of(core, 2 * j + 1)])
        for h in range(2):
            q_ref[h, CCOLS * j : CCOLS * (j + 1)] = paired_columns(r_ref.at[j, h], value[h])
    inverse_ref[...] = 4.0 / depth_pairs(q_ref[0], q_ref[1])
    for k in range(3):
        for h in range(2):
            for slot in range(3):
                add_row(s_ref, on_ref, k, h, ROWS - slot, slot)


def residual_kernel(
    _, zb_ref, za_ref, off_ref, g_ref, e_ref, inverse_ref, s_ref, u_ref, gc_ref, ca_ref, cb_ref, r_ref, q_ref
):
    core, _, even_y, _, _ = places()
    for k in range(3):
        for h in range(2):
            for r in range(-1, ROWS + 1):
                row = s_ref.at[k, r + 2, h]
                at = 32 * k + 3 * (r + 1)
                low, high = from_sides(even_y, za_ref[h, at : at + 3], zb_ref[h, at : at + 3])
                row[LEFT - 1 : LEFT + 2] = row[LEFT - 1 : LEFT + 2] + low
                row[END - 2 : END + 1] = row[END - 2 : END + 1] + high
                if r < 2:
                    add_row(s_ref, off_ref, k, h, r, r + 1)
    for k in range(3):
        for r in range(ROWS + 2):
            pair = sums_depth(*(sums_columns(s_ref.at[k, r + 1, h], LEFT, COLS) for h in range(2)))
            for h in range(2):
                u_ref[k, r, h] = pair[h]
    for j in range(CROWS):
        for k in range(3):
            for h in range(2):
                total = None
                for r in (2 * j, 2 * j + 1):
                    near = sums_rows(lambda i: u_ref[k, i + 1, h], r, -1, ROWS)
                    value_r = e_ref[row_of(core, r), :, HALF * h : HALF * (h + 1)] * (
                        g_ref[k, r, h, LEFT:END]
                        - (16.5 * CG) * s_ref[k, r + 2, h, LEFT:END]
                        + (2.0 / 8.0 * CG) * near
                    )
                    total = value_r if total is None else total + value_r
                at = CCOLS * (k * CROWS + j)
                q_ref[h, at : at + CCOLS] = paired_columns(r_ref.at[k, j, h], total)
    for k in range(3):
        for h in range(2):
            for slot in range(3):
                low, high = spill(off_ref, k, h, slot)
                at = CEDGE + 18 * k + 9 * h + 3 * slot
                ca_ref[at : at + 3] = jnp.where(even_y, high, low)
                cb_ref[at : at + 3] = jnp.where(even_y, low, high)
    sums = depth_pairs(q_ref[0], q_ref[1])
    size = CROWS * CCOLS
    for k in range(3):
        value = sums[k * size : (k + 1) * size] * inverse_ref[...]
        for j in range(CROWS):
            row = value[j * CCOLS : (j + 1) * CCOLS]
            gc_ref[k, j] = row
            low = row[:4]
            high = row[CCOLS - 4 :]
            at = CCOLS * k + 4 * j
            ca_ref[at : at + 4] = jnp.where(even_y, high, low)
            cb_ref[at : at + 4] = jnp.where(even_y, low, high)


OWN_AT = (4, 0)
MINE_AT = (3, 2)
THEIRS_AT = (2, 3)


def window_at(k, window):
    return 16 * (k * 2 + window)


def spilled_at(k, window, slot):
    return 8 * ((k * 2 + window) * 3 + slot)


def corner_residuals(d_ref, u_ref, w_ref, keep, put):
    size = d_ref.shape[1]
    for h in range(2):
        value = d_ref[h]
        u_ref[h] = (value + value) + (pltpu.roll(value, 1, 0) + pltpu.roll(value, size - 1, 0))
    sums = sums_depth(u_ref[0], u_ref[1])
    for h in range(2):
        u_ref[h] = sums[h]
    for k in range(3):
        for window in range(2):
            for h in range(2):
                rows = []
                at = spilled_at(k, window, 0)
                for q in range(3):
                    part = (-2.0 / 8.0) * sums_rows(
                        lambda i: u_ref[h, at + 8 * (i + 1) : at + 8 * (i + 2)], q, -1, 1
                    )
                    if q < 2:
                        part = part + 16.5 * d_ref[h, at + 8 * (q + 1) : at + 8 * (q + 2)]
                    rows.append(jnp.where(keep[window], -w_ref[window * 4 + q, h] * part, 0.0))
                put(h, window_at(k, window), rows[0] + rows[1], rows[2])


def own_places():
    place = lax.broadcasted_iota(jnp.int32, (8, HALF), 0)
    return place >= 4, place < 4


def spilled_kernel(
    za_ref, zb_ref, off_ref, e_ref, s_ref, near_ref, g_ref,
    w_ref, r_ref, inverse_ref, base_ref, d_ref, u_ref, q_ref,
):
    core, _, even_y, _, _ = places()
    d_ref[...] = jnp.zeros_like(d_ref)
    for h in range(2):
        for k in range(3):
            for slot in range(3):
                theirs = spill(off_ref, k, h, slot)
                for window in range(2):
                    at = spilled_at(k, window, slot) + THEIRS_AT[window]
                    d_ref[h, at : at + 3] = theirs[window]
        for r in range(4):
            at = ZEDGE + 4 * r
            halo = from_sides(even_y, za_ref[h, at : at + 4], zb_ref[h, at : at + 4])
            for window, first in enumerate((0, COLS - 4)):
                n = window * 4 + r
                at = OWN_AT[window]
                w_ref[n, h, at : at + 4] = e_ref[
                    row_of(core, r), first : first + 4, HALF * h : HALF * (h + 1)
                ]
                w_ref[n, h, 4 - at : 8 - at] = halo[window]
                if r % 2:
                    at = window_at(0, window) + 8 * (r // 2)
                    q_ref[h, at : at + 8] = w_ref[n - 1, h] + w_ref[n, h]

    def put(h, at, first, second):
        r_ref[h, at : at + 8] = first
        r_ref[h, at + 8 : at + 16] = second

    own = own_places()
    corner_residuals(d_ref, u_ref, w_ref, (jnp.logical_not(own[0]), jnp.logical_not(own[1])), put)
    q_ref[0] = depth_pairs(q_ref[0], q_ref[1])
    visc = q_ref[0, pl.ds(0, 16, stride=2)] + q_ref[0, pl.ds(1, 16, stride=2)]
    inverse_ref[...] = jnp.where(visc > 0.0, (4.0 * CG) / jnp.where(visc > 0.0, visc, 1.0), 0.0)
    for k in range(3):
        for h in range(2):
            for r in range(ROWS):
                base_ref[k, r, h] = (
                    CA * s_ref[k, r + 2, h, LEFT:END]
                    + g_ref[k, r, h, LEFT:END]
                    + CB * sums_rows(lambda i: near_ref[k, i + 1, h], r, -1, ROWS)
                )


def corner_kernel(
    gc_ref, ca_ref, cb_ref, w_ref, s_ref, inverse_ref, out_ref, edge_ref, d_ref, u_ref, r_ref, q_ref
):
    _, _, even_y, has_low, has_high = places()
    d_ref[...] = jnp.zeros_like(d_ref)
    for h in range(2):
        for k in range(3):
            for slot in range(3):
                at = CEDGE + 18 * k + 9 * h + 3 * slot
                mine = from_sides(even_y, ca_ref[at : at + 3], cb_ref[at : at + 3])
                for window in range(2):
                    at = spilled_at(k, window, slot) + MINE_AT[window]
                    d_ref[h, at : at + 3] = mine[window]

    def put(h, at, first, second):
        r_ref[h, at : at + 8] = first + s_ref[h, at : at + 8]
        r_ref[h, at + 8 : at + 16] = second + s_ref[h, at + 8 : at + 16]

    corner_residuals(d_ref, u_ref, w_ref, own_places(), put)
    q_ref[...] = depth_pairs(r_ref[0], r_ref[1])
    sums = q_ref[pl.ds(0, 48, stride=2)] + q_ref[pl.ds(1, 48, stride=2)]
    for k in range(3):
        value = sums[16 * k : 16 * (k + 1)] * inverse_ref[...]
        for j in range(CROWS):
            at = CCOLS * k + 4 * j
            low, high = from_sides(even_y, ca_ref[at : at + 4], cb_ref[at : at + 4])
            out_ref[k, j] = jnp.concatenate([low, gc_ref[k, j], high], 0)
            if j < 2:
                for window, first in enumerate((2, CWIDE - 6)):
                    at = 4 * (window * 2 + j)
                    out_ref[k, j, first : first + 4] = (
                        out_ref[k, j, first : first + 4] + value[at : at + 4]
                    )
    mask = column_mask((CWIDE, HALF), CLEFT, CCOLS, has_low, has_high)
    edge_ref[...] = coarse_sweeps(out_ref[...], 0, mask)[:, 0]


def column_mask(shape, left, width, has_low, has_high):
    place = lax.broadcasted_iota(jnp.int32, shape, 0)
    keep = jnp.logical_and(
        jnp.logical_or(place >= left, has_low), jnp.logical_or(place < left + width, has_high)
    )
    return jnp.where(keep, 1.0, 0.0)


def coarse_sweeps(rhs, last, mask):
    value = rhs
    for left in range(KC - 2, -1, -1):
        rows = min(last + 1 + left, rhs.shape[1])
        given = min(rows + 1, rhs.shape[1])
        u = value[:, :given].reshape(3 * given * CWIDE, HALF)
        size = u.shape[0]
        u = (u + u) + (pltpu.roll(u, 1, 0) + pltpu.roll(u, size - 1, 0))
        lane = lax.broadcasted_iota(jnp.int32, u.shape, 1)
        u = (u + u) + (
            jnp.where(lane == 0, 0.0, pltpu.roll(u, 1, 1))
            + jnp.where(lane == HALF - 1, 0.0, pltpu.roll(u, HALF - 1, 1))
        )
        u = u.reshape(3, given, CWIDE, HALF)
        none = jnp.zeros((3, 1, CWIDE, HALF), jnp.float32)
        before = jnp.concatenate([none, u[:, : rows - 1]], 1) if rows > 1 else none
        after = u[:, 1:given]
        if given == rows:
            after = jnp.concatenate([after, none], 1)
        near = (u[:, :rows] + u[:, :rows]) + (before + after)
        value = mask * (CA * value[:, :rows] + CB * near + rhs[:, :rows])
    return value


def coarse_kernel(own_ref, partner_ref, cor_ref, c_ref):
    _, _, _, has_low, has_high = places()
    mask = column_mask((CWIDE, HALF), CLEFT, CCOLS, has_low, has_high)
    for k in range(3):
        for r in range(CROWS):
            c_ref[k, r] = own_ref[k, r]
            c_ref[k, 2 * CROWS - 1 - r] = partner_ref[k, r]
    cor_ref[...] = coarse_sweeps(c_ref[...], CROWS, mask)


def lifted_columns(ref, value):
    mid = 3.0 * value[CLEFT : CLEFT + CCOLS]
    ref[pl.ds(0, CCOLS, stride=2)] = mid + value[CLEFT - 1 : CLEFT - 1 + CCOLS]
    ref[pl.ds(1, CCOLS, stride=2)] = mid + value[CLEFT + 1 : CLEFT + 1 + CCOLS]


def inner_kernel(base_ref, d_ref, u_ref, cor_ref, o_ref, z_ref, p_ref, l_ref):
    core, _, _, _, _ = places()
    sums, copies = lift_tables()
    sums = exact_dot(cor_ref[...].reshape(3 * (CROWS + 1) * CWIDE, HALF), sums)
    copies = exact_dot(
        cor_ref[:, :CROWS, CLEFT : CLEFT + CCOLS].reshape(3 * CROWS * CCOLS, HALF), copies
    )
    for k in range(3):
        for h in range(2):
            lanes = slice(HALF * h, HALF * (h + 1))
            for j in range(CROWS + 1):
                at = (k * (CROWS + 1) + j) * CWIDE
                z_ref[k, j, h] = sums[at : at + CWIDE, lanes]
                lifted_columns(p_ref.at[k, j, h], z_ref.at[k, j, h])
                if j < CROWS:
                    at = (k * CROWS + j) * CCOLS
                    l_ref[k, j, h, pl.ds(0, CCOLS, stride=2)] = copies[at : at + CCOLS, lanes]
                    l_ref[k, j, h, pl.ds(1, CCOLS, stride=2)] = copies[at : at + CCOLS, lanes]
            for r in range(ROWS):
                j = r // 2
                beside = j + 2 * (r % 2) - 1
                total = 3.0 * p_ref[k, j, h]
                if beside >= 0:
                    total = total + p_ref[k, beside, h]
                row = o_ref.at[k, row_of(core, r), :, pl.ds(HALF * h, HALF)]
                row[...] = base_ref[k, r, h] + (CA * l_ref[k, j, h] + CB * total)
                if r < 3:
                    for window, first in enumerate((0, COLS - 4)):
                        at = spilled_at(k, window, 0)
                        fix = CB * sums_rows(
                            lambda i: u_ref[h, at + 8 * (i + 1) : at + 8 * (i + 2)], r, -1, 1
                        )
                        if r < 2:
                            fix = fix + CA * d_ref[h, at + 8 * (r + 1) : at + 8 * (r + 2)]
                        fix = fix[OWN_AT[window] : OWN_AT[window] + 4]
                        row[first : first + 4] = row[first : first + 4] + fix


def edge_kernel(inner_ref, next_ref, out_hbm, o_ref, z_ref, p_ref, sems):
    core, _, _, _, _ = places()
    begin = 1 - core
    copies = []

    def copy(source, target):
        copies.append(pltpu.make_async_copy(source, target, sems.at[len(copies)]))
        copies[-1].start()

    rows = pl.ds(begin, ROWS - 1)
    for k in range(3):
        copy(inner_ref.at[k, rows], out_hbm.at[k, rows])
    lifted = exact_dot(next_ref[...].reshape(3 * CWIDE, HALF), lift_tables()[0])
    own = row_of(core, 0)
    for k in range(3):
        for h in range(2):
            z_ref[k, h] = lifted[k * CWIDE : (k + 1) * CWIDE, HALF * h : HALF * (h + 1)]
            lifted_columns(p_ref.at[k, h], z_ref.at[k, h])
            lanes = slice(HALF * h, HALF * (h + 1))
            o_ref[k, :, lanes] = inner_ref[k, own, :, lanes] + CB * p_ref[k, h]
        copy(o_ref.at[k], out_hbm.at[k, own])
    for started in copies:
        started.wait()


def call(kernel, outs, scratch, *args, spaces=None, out_spaces=None, aliases=None):
    spaces = spaces or [pltpu.VMEM] * len(args)
    out_spaces = out_spaces or [pltpu.VMEM] * len(outs)
    return pl.pallas_call(
        kernel,
        out_shape=[jax.ShapeDtypeStruct(o, jnp.float32) for o in outs],
        in_specs=[pl.BlockSpec(memory_space=space) for space in spaces],
        out_specs=[pl.BlockSpec(memory_space=space) for space in out_spaces],
        scratch_shapes=[pltpu.VMEM(s, jnp.float32) if isinstance(s, tuple) else s for s in scratch],
        input_output_aliases=aliases or {},
        compiler_params=pltpu.CompilerParams(vmem_limit_bytes=24 * 2**20),
    )(*args)


def swap(value, axis, parity):
    pairs = []
    for i in range(parity, lax.axis_size(axis) - 1, 2):
        pairs += [(i, i + 1), (i + 1, i)]
    return lax.ppermute(value, axis, pairs)


def body(velocity, forcing, viscosity):
    own, g, visc, off, on = call(
        sweeps_kernel,
        [TALL, GRID, viscosity.shape, XMSG, XMSG],
        [
            GRID, forcing.shape, viscosity.shape, GRID,
            (3, ROWS + 2, 2, COLS + 8, HALF), (3, ROWS + 2, 2, WIDE + LEFT, HALF),
            pltpu.SemaphoreType.DMA((10,)),
        ],
        *(pltpu.with_memory_space_constraint(a, pltpu.HBM) for a in (velocity, forcing, viscosity)),
        spaces=[pltpu.HBM] * 3,
    )
    on = swap(on, "gx", 0)
    off = swap(off, "gx", 1)
    za, zb = call(columns_kernel, [ZMSG, ZMSG], [], own, on, visc)
    coarse_cells = CROWS * CCOLS
    own, scale = call(
        waiting_kernel,
        [TALL, (coarse_cells, HALF)],
        [(CROWS, 2, COLS, HALF), (2, coarse_cells, HALF)],
        own, on, visc, zb,
        aliases={0: 0},
    )
    zb = swap(zb, "gy", 1)
    za = swap(za, "gy", 0)
    smooth, near, gc, ca, cb = call(
        residual_kernel,
        [TALL, (3, ROWS + 2, 2, COLS, HALF), (3, CROWS, CCOLS, HALF), CMSG, CMSG],
        [(3, CROWS, 2, COLS, HALF), (2, 3 * CROWS * CCOLS, HALF)],
        own, zb, za, off, g, visc, scale,
        aliases={0: 0},
    )
    cb = swap(cb, "gy", 1)
    ca = swap(ca, "gy", 0)
    spilled = (2, 18 * 8, HALF)
    tile = (3, ROWS, 2, COLS, HALF)
    windows, sums, inverse, base = call(
        spilled_kernel,
        [(8, 2, 8, HALF), (2, 6 * 16, HALF), (16, HALF), tile],
        [spilled, spilled, (2, 32, HALF)],
        za, zb, off, visc, smooth, near, g,
    )
    rhs, edge, corner, around = call(
        corner_kernel,
        [(3, CROWS, CWIDE, HALF), (3, CWIDE, HALF), spilled, spilled],
        [(2, 6 * 16, HALF), (6 * 16, HALF)],
        gc, ca, cb, windows, sums, inverse,
    )
    beyond = swap(edge, "gx", 1)
    partner = swap(rhs, "gx", 0)
    (cor,) = call(
        coarse_kernel,
        [(3, CROWS + 1, CWIDE, HALF)],
        [(3, 2 * CROWS, CWIDE, HALF)],
        rhs, partner,
    )
    half_rows = (3, 2, COLS, HALF)
    (inner,) = call(
        inner_kernel,
        [velocity.shape],
        [
            (3, CROWS + 1, 2, CWIDE, HALF), (3, CROWS + 1, 2, COLS, HALF), (3, CROWS, 2, COLS, HALF),
        ],
        base, corner, around, cor,
    )
    (out,) = call(
        edge_kernel,
        [velocity.shape],
        [(3, COLS, DEPTH), (3, 2, CWIDE, HALF), half_rows, pltpu.SemaphoreType.DMA((6,))],
        inner, beyond,
        out_spaces=[pltpu.HBM],
    )
    return out


def solution(mesh):
    placed = (P(None, "gx", "gy", None), P(None, "gx", "gy", None), P("gx", "gy", None))
    return jax.shard_map(
        body, mesh=mesh, in_specs=placed, out_specs=P(None, "gx", "gy", None), check_vma=False
    )
```

```python
import jax
import jax.numpy as jnp
from jax import lax
from jax.experimental import pallas as pl
from jax.experimental.pallas import tpu as pltpu
from jax.sharding import PartitionSpec as P

KC = 4
CA = 1.0 - 0.8 * 16.5 / 14.5
CB = 0.8 * 2.0 / 8.0 / 14.5
CG = 0.8 / 14.5

ROWS = 8
COLS = 32
DEPTH = 256
HALF = 128
WIDE = 48
LEFT = 8
END = LEFT + COLS
CROWS = 4
CCOLS = 16
CWIDE = 24
CLEFT = 4
XMSG = (3, 2, 112, HALF)
EDGES = 3 * COLS
ZMSG = (2, 112, HALF)
ZEDGE = 96
CMSG = (104, HALF)
CEDGE = 48
TALL = (3, ROWS + 4, 2, WIDE, HALF)
GRID = (3, ROWS, 2, WIDE, HALF)


def places():
    index_x = lax.axis_index("gx")
    index_y = lax.axis_index("gy")
    core = index_x % 2
    has_off = jnp.logical_and(index_x != 0, index_x != lax.axis_size("gx") - 1)
    even_y = index_y % 2 == 0
    return core, has_off, even_y, index_y != 0, index_y != lax.axis_size("gy") - 1


def row_of(core, row):
    return row + core * (ROWS - 1 - 2 * row)


def halves(a):
    return a[:, :HALF], a[:, HALF:]


def sums_depth(first, second):
    lane = lax.broadcasted_iota(jnp.int32, first.shape, 1)
    start = lane == 0
    stop = lane == HALF - 1
    up = pltpu.roll(first, 1, 1), pltpu.roll(second, 1, 1)
    down = pltpu.roll(first, HALF - 1, 1), pltpu.roll(second, HALF - 1, 1)
    return (
        (first + first) + (jnp.where(start, 0.0, up[0]) + jnp.where(stop, down[1], down[0])),
        (second + second) + (jnp.where(start, up[0], up[1]) + jnp.where(stop, 0.0, down[1])),
    )


def sums_columns(ref, first, size):
    mid = ref[first : first + size]
    return (mid + mid) + (ref[first - 1 : first - 1 + size] + ref[first + 1 : first + 1 + size])


def sums_rows(get, row, first, last):
    near = [get(r) for r in (row - 1, row + 1) if first <= r <= last]
    total = None
    if near:
        total = near[0] if len(near) == 1 else near[0] + near[1]
    if first <= row <= last:
        mid = get(row)
        total = mid + mid if total is None else total + (mid + mid)
    return total


def from_sides(even_y, a, b):
    return jnp.where(even_y, b, a), jnp.where(even_y, a, b)


def exact_dot(a, table):
    parts = []
    for part in range(3):
        parts.append(a.astype(jnp.bfloat16))
        if part < 2:
            a = a - parts[-1].astype(jnp.float32)
    table = table.astype(jnp.bfloat16)
    return jnp.dot(
        jnp.concatenate(parts, 1), jnp.concatenate([table] * 3, 0), preferred_element_type=jnp.float32
    )


def depth_pairs(first, second):
    fine = lax.broadcasted_iota(jnp.int32, (DEPTH, HALF), 0) // 2
    coarse = lax.broadcasted_iota(jnp.int32, (DEPTH, HALF), 1)
    return exact_dot(jnp.concatenate([first, second], 1), jnp.where(fine == coarse, 1.0, 0.0))


def lift_tables():
    coarse = lax.broadcasted_iota(jnp.int32, (HALF, DEPTH), 0)
    fine = lax.broadcasted_iota(jnp.int32, (HALF, DEPTH), 1)
    same = coarse == fine // 2
    beside = coarse == fine // 2 + 2 * (fine % 2) - 1
    copied = jnp.where(same, 1.0, 0.0)
    return jnp.where(beside, 1.0, 3.0 * copied), copied


def sweeps_kernel(
    v_hbm, f_hbm, e_hbm, own_ref, g_ref, e_ref, off_ref, on_ref,
    v_ref, f_ref, i_ref, z_ref, y_ref, w_ref, sems,
):
    def copies_v(k):
        return [
            pltpu.make_async_copy(
                v_hbm.at[k, :, :, pl.ds(HALF * h, HALF)],
                v_ref.at[k, :, h, pl.ds(LEFT, COLS)],
                sems.at[2 * k + h],
            )
            for h in range(2)
        ]

    def copy_f(k):
        return pltpu.make_async_copy(f_hbm.at[k], f_ref.at[k], sems.at[6 + k])

    copy_e = pltpu.make_async_copy(e_hbm, e_ref, sems.at[9])
    for k in range(3):
        for copy in copies_v(k):
            copy.start()
    copy_e.start()
    for k in range(3):
        copy_f(k).start()
    core, has_off, _, has_low, has_high = places()
    none = jnp.zeros((LEFT, HALF), jnp.float32)
    for k in range(3):
        for h in range(2):
            for r in range(ROWS):
                for ref in (v_ref, g_ref, z_ref):
                    ref[k, r, h, :LEFT] = none
                    ref[k, r, h, END:] = none
            for r in range(ROWS + 2):
                w_ref[k, r, h, :LEFT] = none
                w_ref[k, r, h, WIDE:] = none
    for k in range(3):
        for copy in copies_v(k):
            copy.wait()
        for r in range(ROWS):
            pair = sums_depth(*(v_ref[k, row_of(core, r), h, LEFT:END] for h in range(2)))
            for h in range(2):
                z_ref[k, r, h, LEFT:END] = pair[h]
    copy_e.wait()
    for r in range(ROWS):
        own = row_of(core, r)
        i_ref[r] = CG / e_ref[own]
    for k in range(3):
        copy_f(k).wait()
        for r in range(ROWS):
            for h, part in enumerate(halves(f_ref[k, row_of(core, r)] * i_ref[r])):
                g_ref[k, r, h, LEFT:END] = part
    for k in range(3):
        for h in range(2):
            for r in range(ROWS):
                y_ref[k, r, h] = sums_columns(z_ref.at[k, r, h], LEFT - 4, COLS + 8)
            for r in range(-1, ROWS + 1):
                value = CB * sums_rows(lambda i: y_ref[k, i, h], r, 0, ROWS - 1)
                if 0 <= r < ROWS:
                    value = value + (
                        CA * v_ref[k, row_of(core, r), h, LEFT - 4 : END + 4]
                        + g_ref[k, r, h, LEFT - 4 : END + 4]
                    )
                w_ref[k, r + 1, h, LEFT:WIDE] = value

    @pl.when(jnp.logical_not(has_off))
    def _():
        w_ref[:, 0] = jnp.zeros((3, 2, WIDE + LEFT, HALF), jnp.float32)

    @pl.when(jnp.logical_not(has_low))
    def _():
        w_ref[:, :, :, LEFT : LEFT + 4] = jnp.zeros((3, ROWS + 2, 2, 4, HALF), jnp.float32)

    @pl.when(jnp.logical_not(has_high))
    def _():
        w_ref[:, :, :, WIDE - 4 : WIDE] = jnp.zeros((3, ROWS + 2, 2, 4, HALF), jnp.float32)

    for k in range(3):
        for r in range(ROWS + 2):
            pair = sums_depth(*(sums_columns(w_ref.at[k, r, h], LEFT, COLS + 8) for h in range(2)))
            for h in range(2):
                y_ref[k, r, h] = pair[h]
    for k in range(3):
        for h in range(2):
            for r in range(-2, ROWS + 2):
                value = CB * sums_rows(lambda i: y_ref[k, i + 1, h], r, -1, ROWS)
                if -1 <= r <= ROWS:
                    value = value + CA * w_ref[k, r + 1, h, LEFT:WIDE]
                if 0 <= r < ROWS:
                    value = value + g_ref[k, r, h, LEFT - 4 : END + 4]
                own_ref[k, r + 2, h, LEFT - 4 : END + 4] = value

    @pl.when(jnp.logical_not(has_off))
    def _():
        own_ref[:, :2] = jnp.zeros((3, 2, 2, WIDE, HALF), jnp.float32)

    @pl.when(jnp.logical_not(has_low))
    def _():
        own_ref[:, :, :, LEFT - 4 : LEFT] = jnp.zeros((3, ROWS + 4, 2, 4, HALF), jnp.float32)

    @pl.when(jnp.logical_not(has_high))
    def _():
        own_ref[:, :, :, END : END + 4] = jnp.zeros((3, ROWS + 4, 2, 4, HALF), jnp.float32)

    for k in range(3):
        for h in range(2):
            for ref, rows in ((off_ref, (0, -1, -2)), (on_ref, (ROWS - 1, ROWS, ROWS + 1))):
                for slot, r in enumerate(rows):
                    ref[k, h, COLS * slot : COLS * (slot + 1)] = own_ref[k, r + 2, h, LEFT:END]
                    at = EDGES + 4 * slot
                    ref[k, h, at : at + 2] = own_ref[k, r + 2, h, LEFT - 2 : LEFT]
                    ref[k, h, at + 2 : at + 4] = own_ref[k, r + 2, h, END : END + 2]


def spill(ref, k, h, slot):
    at = EDGES + 4 * slot
    low = jnp.concatenate([ref[k, h, at : at + 2], ref[k, h, COLS * slot : COLS * slot + 1]], 0)
    high = jnp.concatenate(
        [ref[k, h, COLS * (slot + 1) - 1 : COLS * (slot + 1)], ref[k, h, at + 2 : at + 4]], 0
    )
    return low, high


def add_row(s_ref, ref, k, h, r, slot):
    row = s_ref.at[k, r + 2, h]
    at = EDGES + 4 * slot
    row[LEFT:END] = row[LEFT:END] + ref[k, h, COLS * slot : COLS * (slot + 1)]
    row[LEFT - 1 : LEFT] = row[LEFT - 1 : LEFT] + ref[k, h, at + 1 : at + 2]
    row[END : END + 1] = row[END : END + 1] + ref[k, h, at + 2 : at + 3]


def columns_kernel(own_ref, on_ref, e_ref, za_ref, zb_ref):
    core, _, even_y, _, _ = places()
    for h in range(2):
        for k in range(3):
            for r in range(-1, ROWS + 1):
                at = 32 * k + 3 * (r + 1)
                low = own_ref[k, r + 2, h, LEFT - 2 : LEFT + 1]
                high = own_ref[k, r + 2, h, END - 1 : END + 2]
                if ROWS - r < 3:
                    more = spill(on_ref, k, h, ROWS - r)
                    low = low + more[0]
                    high = high + more[1]
                za_ref[h, at : at + 3] = jnp.where(even_y, high, low)
                zb_ref[h, at : at + 3] = jnp.where(even_y, low, high)
        for r in range(4):
            at = ZEDGE + 4 * r
            low = e_ref[row_of(core, r), :4, HALF * h : HALF * (h + 1)]
            high = e_ref[row_of(core, r), COLS - 4 :, HALF * h : HALF * (h + 1)]
            za_ref[h, at : at + 4] = jnp.where(even_y, high, low)
            zb_ref[h, at : at + 4] = jnp.where(even_y, low, high)


def paired_columns(ref, value):
    ref[...] = value
    return ref[pl.ds(0, CCOLS, stride=2)] + ref[pl.ds(1, CCOLS, stride=2)]


def waiting_kernel(_, on_ref, e_ref, __, s_ref, inverse_ref, r_ref, q_ref):
    core, _, _, _, _ = places()
    for j in range(CROWS):
        value = halves(e_ref[row_of(core, 2 * j)] + e_ref[row_of(core, 2 * j + 1)])
        for h in range(2):
            q_ref[h, CCOLS * j : CCOLS * (j + 1)] = paired_columns(r_ref.at[j, h], value[h])
    inverse_ref[...] = 4.0 / depth_pairs(q_ref[0], q_ref[1])
    for k in range(3):
        for h in range(2):
            for slot in range(3):
                add_row(s_ref, on_ref, k, h, ROWS - slot, slot)


def off_kernel(_, off_ref, s_ref, ca_ref, cb_ref):
    _, _, even_y, _, _ = places()
    for k in range(3):
        for h in range(2):
            for slot in range(3):
                low, high = spill(off_ref, k, h, slot)
                at = CEDGE + 18 * k + 9 * h + 3 * slot
                ca_ref[at : at + 3] = jnp.where(even_y, high, low)
                cb_ref[at : at + 3] = jnp.where(even_y, low, high)
                add_row(s_ref, off_ref, k, h, slot - 1, slot)


def residual_kernel(
    _, _a, _b, zb_ref, za_ref, g_ref, e_ref, inverse_ref, s_ref, u_ref, gc_ref, ca_ref, cb_ref, r_ref, q_ref
):
    core, _, even_y, _, _ = places()
    for k in range(3):
        for h in range(2):
            for r in range(-1, ROWS + 1):
                row = s_ref.at[k, r + 2, h]
                at = 32 * k + 3 * (r + 1)
                low, high = from_sides(even_y, za_ref[h, at : at + 3], zb_ref[h, at : at + 3])
                row[LEFT - 1 : LEFT + 2] = row[LEFT - 1 : LEFT + 2] + low
                row[END - 2 : END + 1] = row[END - 2 : END + 1] + high
    for k in range(3):
        for r in range(ROWS + 2):
            pair = sums_depth(*(sums_columns(s_ref.at[k, r + 1, h], LEFT, COLS) for h in range(2)))
            for h in range(2):
                u_ref[k, r, h] = pair[h]
    for j in range(CROWS):
        for k in range(3):
            for h in range(2):
                total = None
                for r in (2 * j, 2 * j + 1):
                    near = sums_rows(lambda i: u_ref[k, i + 1, h], r, -1, ROWS)
                    value_r = e_ref[row_of(core, r), :, HALF * h : HALF * (h + 1)] * (
                        g_ref[k, r, h, LEFT:END]
                        - (16.5 * CG) * s_ref[k, r + 2, h, LEFT:END]
                        + (2.0 / 8.0 * CG) * near
                    )
                    total = value_r if total is None else total + value_r
                at = CCOLS * (k * CROWS + j)
                q_ref[h, at : at + CCOLS] = paired_columns(r_ref.at[k, j, h], total)
    sums = depth_pairs(q_ref[0], q_ref[1])
    size = CROWS * CCOLS
    for k in range(3):
        value = sums[k * size : (k + 1) * size] * inverse_ref[...]
        for j in range(CROWS):
            row = value[j * CCOLS : (j + 1) * CCOLS]
            gc_ref[k, j] = row
            low = row[:4]
            high = row[CCOLS - 4 :]
            at = CCOLS * k + 4 * j
            ca_ref[at : at + 4] = jnp.where(even_y, high, low)
            cb_ref[at : at + 4] = jnp.where(even_y, low, high)


OWN_AT = (4, 0)
MINE_AT = (3, 2)
THEIRS_AT = (2, 3)


def window_at(k, window):
    return 16 * (k * 2 + window)


def spilled_at(k, window, slot):
    return 8 * ((k * 2 + window) * 3 + slot)


def corner_residuals(d_ref, u_ref, w_ref, keep, put):
    size = d_ref.shape[1]
    for h in range(2):
        value = d_ref[h]
        u_ref[h] = (value + value) + (pltpu.roll(value, 1, 0) + pltpu.roll(value, size - 1, 0))
    sums = sums_depth(u_ref[0], u_ref[1])
    for h in range(2):
        u_ref[h] = sums[h]
    for k in range(3):
        for window in range(2):
            for h in range(2):
                rows = []
                at = spilled_at(k, window, 0)
                for q in range(3):
                    part = (-2.0 / 8.0) * sums_rows(
                        lambda i: u_ref[h, at + 8 * (i + 1) : at + 8 * (i + 2)], q, -1, 1
                    )
                    if q < 2:
                        part = part + 16.5 * d_ref[h, at + 8 * (q + 1) : at + 8 * (q + 2)]
                    rows.append(jnp.where(keep[window], -w_ref[window * 4 + q, h] * part, 0.0))
                put(h, window_at(k, window), rows[0] + rows[1], rows[2])


def own_places():
    place = lax.broadcasted_iota(jnp.int32, (8, HALF), 0)
    return place >= 4, place < 4


def spilled_kernel(
    za_ref, zb_ref, off_ref, e_ref, s_ref, near_ref, g_ref,
    w_ref, r_ref, inverse_ref, base_ref, d_ref, u_ref, q_ref,
):
    core, _, even_y, _, _ = places()
    d_ref[...] = jnp.zeros_like(d_ref)
    for h in range(2):
        for k in range(3):
            for slot in range(3):
                theirs = spill(off_ref, k, h, slot)
                for window in range(2):
                    at = spilled_at(k, window, slot) + THEIRS_AT[window]
                    d_ref[h, at : at + 3] = theirs[window]
        for r in range(4):
            at = ZEDGE + 4 * r
            halo = from_sides(even_y, za_ref[h, at : at + 4], zb_ref[h, at : at + 4])
            for window, first in enumerate((0, COLS - 4)):
                n = window * 4 + r
                at = OWN_AT[window]
                w_ref[n, h, at : at + 4] = e_ref[
                    row_of(core, r), first : first + 4, HALF * h : HALF * (h + 1)
                ]
                w_ref[n, h, 4 - at : 8 - at] = halo[window]
                if r % 2:
                    at = window_at(0, window) + 8 * (r // 2)
                    q_ref[h, at : at + 8] = w_ref[n - 1, h] + w_ref[n, h]

    def put(h, at, first, second):
        r_ref[h, at : at + 8] = first
        r_ref[h, at + 8 : at + 16] = second

    own = own_places()
    corner_residuals(d_ref, u_ref, w_ref, (jnp.logical_not(own[0]), jnp.logical_not(own[1])), put)
    q_ref[0] = depth_pairs(q_ref[0], q_ref[1])
    visc = q_ref[0, pl.ds(0, 16, stride=2)] + q_ref[0, pl.ds(1, 16, stride=2)]
    inverse_ref[...] = jnp.where(visc > 0.0, (4.0 * CG) / jnp.where(visc > 0.0, visc, 1.0), 0.0)
    for k in range(3):
        for h in range(2):
            for r in range(ROWS):
                base_ref[k, r, h] = (
                    CA * s_ref[k, r + 2, h, LEFT:END]
                    + g_ref[k, r, h, LEFT:END]
                    + CB * sums_rows(lambda i: near_ref[k, i + 1, h], r, -1, ROWS)
                )


def corner_kernel(
    gc_ref, ca_ref, cb_ref, w_ref, s_ref, inverse_ref, out_ref, edge_ref, d_ref, u_ref, r_ref, q_ref
):
    _, _, even_y, has_low, has_high = places()
    d_ref[...] = jnp.zeros_like(d_ref)
    for h in range(2):
        for k in range(3):
            for slot in range(3):
                at = CEDGE + 18 * k + 9 * h + 3 * slot
                mine = from_sides(even_y, ca_ref[at : at + 3], cb_ref[at : at + 3])
                for window in range(2):
                    at = spilled_at(k, window, slot) + MINE_AT[window]
                    d_ref[h, at : at + 3] = mine[window]

    def put(h, at, first, second):
        r_ref[h, at : at + 8] = first + s_ref[h, at : at + 8]
        r_ref[h, at + 8 : at + 16] = second + s_ref[h, at + 8 : at + 16]

    corner_residuals(d_ref, u_ref, w_ref, own_places(), put)
    q_ref[...] = depth_pairs(r_ref[0], r_ref[1])
    sums = q_ref[pl.ds(0, 48, stride=2)] + q_ref[pl.ds(1, 48, stride=2)]
    for k in range(3):
        value = sums[16 * k : 16 * (k + 1)] * inverse_ref[...]
        for j in range(CROWS):
            at = CCOLS * k + 4 * j
            low, high = from_sides(even_y, ca_ref[at : at + 4], cb_ref[at : at + 4])
            out_ref[k, j] = jnp.concatenate([low, gc_ref[k, j], high], 0)
            if j < 2:
                for window, first in enumerate((2, CWIDE - 6)):
                    at = 4 * (window * 2 + j)
                    out_ref[k, j, first : first + 4] = (
                        out_ref[k, j, first : first + 4] + value[at : at + 4]
                    )
    mask = column_mask((CWIDE, HALF), CLEFT, CCOLS, has_low, has_high)
    edge_ref[...] = coarse_sweeps(out_ref[...], 0, mask)[:, 0]


def column_mask(shape, left, width, has_low, has_high):
    place = lax.broadcasted_iota(jnp.int32, shape, 0)
    keep = jnp.logical_and(
        jnp.logical_or(place >= left, has_low), jnp.logical_or(place < left + width, has_high)
    )
    return jnp.where(keep, 1.0, 0.0)


def coarse_sweeps(rhs, last, mask):
    value = rhs
    for left in range(KC - 2, -1, -1):
        rows = min(last + 1 + left, rhs.shape[1])
        given = min(rows + 1, rhs.shape[1])
        u = value[:, :given].reshape(3 * given * CWIDE, HALF)
        size = u.shape[0]
        u = (u + u) + (pltpu.roll(u, 1, 0) + pltpu.roll(u, size - 1, 0))
        lane = lax.broadcasted_iota(jnp.int32, u.shape, 1)
        u = (u + u) + (
            jnp.where(lane == 0, 0.0, pltpu.roll(u, 1, 1))
            + jnp.where(lane == HALF - 1, 0.0, pltpu.roll(u, HALF - 1, 1))
        )
        u = u.reshape(3, given, CWIDE, HALF)
        none = jnp.zeros((3, 1, CWIDE, HALF), jnp.float32)
        before = jnp.concatenate([none, u[:, : rows - 1]], 1) if rows > 1 else none
        after = u[:, 1:given]
        if given == rows:
            after = jnp.concatenate([after, none], 1)
        near = (u[:, :rows] + u[:, :rows]) + (before + after)
        value = mask * (CA * value[:, :rows] + CB * near + rhs[:, :rows])
    return value


def coarse_kernel(own_ref, partner_ref, cor_ref, c_ref):
    _, _, _, has_low, has_high = places()
    mask = column_mask((CWIDE, HALF), CLEFT, CCOLS, has_low, has_high)
    for k in range(3):
        for r in range(CROWS):
            c_ref[k, r] = own_ref[k, r]
            c_ref[k, 2 * CROWS - 1 - r] = partner_ref[k, r]
    cor_ref[...] = coarse_sweeps(c_ref[...], CROWS, mask)


def lifted_columns(ref, value):
    mid = 3.0 * value[CLEFT : CLEFT + CCOLS]
    ref[pl.ds(0, CCOLS, stride=2)] = mid + value[CLEFT - 1 : CLEFT - 1 + CCOLS]
    ref[pl.ds(1, CCOLS, stride=2)] = mid + value[CLEFT + 1 : CLEFT + 1 + CCOLS]


def inner_kernel(base_ref, d_ref, u_ref, cor_ref, o_ref, z_ref, p_ref, l_ref):
    core, _, _, _, _ = places()
    sums, copies = lift_tables()
    sums = exact_dot(cor_ref[...].reshape(3 * (CROWS + 1) * CWIDE, HALF), sums)
    copies = exact_dot(
        cor_ref[:, :CROWS, CLEFT : CLEFT + CCOLS].reshape(3 * CROWS * CCOLS, HALF), copies
    )
    for k in range(3):
        for h in range(2):
            lanes = slice(HALF * h, HALF * (h + 1))
            for j in range(CROWS + 1):
                at = (k * (CROWS + 1) + j) * CWIDE
                z_ref[k, j, h] = sums[at : at + CWIDE, lanes]
                lifted_columns(p_ref.at[k, j, h], z_ref.at[k, j, h])
                if j < CROWS:
                    at = (k * CROWS + j) * CCOLS
                    l_ref[k, j, h, pl.ds(0, CCOLS, stride=2)] = copies[at : at + CCOLS, lanes]
                    l_ref[k, j, h, pl.ds(1, CCOLS, stride=2)] = copies[at : at + CCOLS, lanes]
            for r in range(ROWS):
                j = r // 2
                beside = j + 2 * (r % 2) - 1
                total = 3.0 * p_ref[k, j, h]
                if beside >= 0:
                    total = total + p_ref[k, beside, h]
                row = o_ref.at[k, h, row_of(core, r)]
                row[...] = base_ref[k, r, h] + (CA * l_ref[k, j, h] + CB * total)
                if r < 3:
                    for window, first in enumerate((0, COLS - 4)):
                        at = spilled_at(k, window, 0)
                        fix = CB * sums_rows(
                            lambda i: u_ref[h, at + 8 * (i + 1) : at + 8 * (i + 2)], r, -1, 1
                        )
                        if r < 2:
                            fix = fix + CA * d_ref[h, at + 8 * (r + 1) : at + 8 * (r + 2)]
                        fix = fix[OWN_AT[window] : OWN_AT[window] + 4]
                        row[first : first + 4] = row[first : first + 4] + fix


def edge_kernel(inner_ref, next_ref, out_hbm, o_ref, z_ref, p_ref, sems):
    core, _, _, _, _ = places()
    begin = 1 - core
    copies = []

    def copy(source, target):
        copies.append(pltpu.make_async_copy(source, target, sems.at[len(copies)]))
        copies[-1].start()

    for k in range(3):
        for h in range(2):
            rows = pl.ds(begin, ROWS - 1)
            copy(inner_ref.at[k, h, rows], out_hbm.at[k, rows, :, pl.ds(HALF * h, HALF)])
    lifted = exact_dot(next_ref[...].reshape(3 * CWIDE, HALF), lift_tables()[0])
    own = row_of(core, 0)
    for k in range(3):
        for h in range(2):
            z_ref[k, h] = lifted[k * CWIDE : (k + 1) * CWIDE, HALF * h : HALF * (h + 1)]
            lifted_columns(p_ref.at[k, h], z_ref.at[k, h])
            o_ref[k, h] = inner_ref[k, h, own] + CB * p_ref[k, h]
            copy(o_ref.at[k, h], out_hbm.at[k, own, :, pl.ds(HALF * h, HALF)])
    for started in copies:
        started.wait()


def call(kernel, outs, scratch, *args, spaces=None, out_spaces=None, aliases=None):
    spaces = spaces or [pltpu.VMEM] * len(args)
    out_spaces = out_spaces or [pltpu.VMEM] * len(outs)
    return pl.pallas_call(
        kernel,
        out_shape=[jax.ShapeDtypeStruct(o, jnp.float32) for o in outs],
        in_specs=[pl.BlockSpec(memory_space=space) for space in spaces],
        out_specs=[pl.BlockSpec(memory_space=space) for space in out_spaces],
        scratch_shapes=[pltpu.VMEM(s, jnp.float32) if isinstance(s, tuple) else s for s in scratch],
        input_output_aliases=aliases or {},
        compiler_params=pltpu.CompilerParams(vmem_limit_bytes=24 * 2**20),
    )(*args)


def swap(value, axis, parity):
    pairs = []
    for i in range(parity, lax.axis_size(axis) - 1, 2):
        pairs += [(i, i + 1), (i + 1, i)]
    return lax.ppermute(value, axis, pairs)


def body(velocity, forcing, viscosity):
    own, g, visc, off, on = call(
        sweeps_kernel,
        [TALL, GRID, viscosity.shape, XMSG, XMSG],
        [
            GRID, forcing.shape, viscosity.shape, GRID,
            (3, ROWS + 2, 2, COLS + 8, HALF), (3, ROWS + 2, 2, WIDE + LEFT, HALF),
            pltpu.SemaphoreType.DMA((10,)),
        ],
        *(pltpu.with_memory_space_constraint(a, pltpu.HBM) for a in (velocity, forcing, viscosity)),
        spaces=[pltpu.HBM] * 3,
    )
    on = swap(on, "gx", 0)
    off = swap(off, "gx", 1)
    za, zb = call(columns_kernel, [ZMSG, ZMSG], [], own, on, visc)
    coarse_cells = CROWS * CCOLS
    own, scale = call(
        waiting_kernel,
        [TALL, (coarse_cells, HALF)],
        [(CROWS, 2, COLS, HALF), (2, coarse_cells, HALF)],
        own, on, visc, zb,
        aliases={0: 0},
    )
    zb = swap(zb, "gy", 1)
    za = swap(za, "gy", 0)
    own, ca, cb = call(off_kernel, [TALL, CMSG, CMSG], [], own, off, aliases={0: 0})
    smooth, near, gc, ca, cb = call(
        residual_kernel,
        [TALL, (3, ROWS + 2, 2, COLS, HALF), (3, CROWS, CCOLS, HALF), CMSG, CMSG],
        [(3, CROWS, 2, COLS, HALF), (2, 3 * CROWS * CCOLS, HALF)],
        own, ca, cb, zb, za, g, visc, scale,
        aliases={0: 0, 1: 3, 2: 4},
    )
    cb = swap(cb, "gy", 1)
    ca = swap(ca, "gy", 0)
    spilled = (2, 18 * 8, HALF)
    tile = (3, ROWS, 2, COLS, HALF)
    windows, sums, inverse, base = call(
        spilled_kernel,
        [(8, 2, 8, HALF), (2, 6 * 16, HALF), (16, HALF), tile],
        [spilled, spilled, (2, 32, HALF)],
        za, zb, off, visc, smooth, near, g,
    )
    rhs, edge, corner, around = call(
        corner_kernel,
        [(3, CROWS, CWIDE, HALF), (3, CWIDE, HALF), spilled, spilled],
        [(2, 6 * 16, HALF), (6 * 16, HALF)],
        gc, ca, cb, windows, sums, inverse,
    )
    beyond = swap(edge, "gx", 1)
    partner = swap(rhs, "gx", 0)
    (cor,) = call(
        coarse_kernel,
        [(3, CROWS + 1, CWIDE, HALF)],
        [(3, 2 * CROWS, CWIDE, HALF)],
        rhs, partner,
    )
    half_rows = (3, 2, COLS, HALF)
    (inner,) = call(
        inner_kernel,
        [(3, 2, ROWS, COLS, HALF)],
        [
            (3, CROWS + 1, 2, CWIDE, HALF), (3, CROWS + 1, 2, COLS, HALF), (3, CROWS, 2, COLS, HALF),
        ],
        base, corner, around, cor,
    )
    (out,) = call(
        edge_kernel,
        [velocity.shape],
        [half_rows, (3, 2, CWIDE, HALF), half_rows, pltpu.SemaphoreType.DMA((12,))],
        inner, beyond,
        out_spaces=[pltpu.HBM],
    )
    return out


def solution(mesh):
    placed = (P(None, "gx", "gy", None), P(None, "gx", "gy", None), P("gx", "gy", None))
    return jax.shard_map(
        body, mesh=mesh, in_specs=placed, out_specs=P(None, "gx", "gy", None), check_vma=False
    )
```
